32 devices in a mesh: frames: 4 (over y, core), rows: 8 (over z, x).
Axes of the slice: x: 2, y: 2, z: 4, core: 2. Of those that a mesh axis runs over, the one named last changes fastest.
Arguments:
- fine_q: bfloat16 [4, 64, 16, 256], P('frames', 'rows'), may hold values from -24 to 24
- fine_kv: bfloat16 [4, 64, 16, 512], P('frames', 'rows'), may hold values from -24 to 24
- coarse_q: bfloat16 [4, 8, 2, 1024], P('frames', 'rows'), may hold values from -24 to 24
- coarse_kv: bfloat16 [4, 8, 2, 2048], P('frames', 'rows'), may hold values from -24 to 24
- cotangent: bfloat16 [4, 64, 16, 256], P('frames', 'rows'), may hold values from -6 to 6
- gain_table: float32 [1000, 256], replicated, may hold values from 0.3 to 3
- timesteps: int32 [4], P('frames'), may hold values from 0 to 999
- valid_cols: int32 [4], replicated, may hold values from 8 to 16
Outputs:
- grad_fine_q: bfloat16 [4, 64, 16, 256], P('frames', 'rows')
- grad_fine_kv: bfloat16 [4, 64, 16, 512], P('frames', 'rows')
- grad_coarse_q: bfloat16 [4, 8, 2, 1024], P(None, 'rows', None, 'frames')
- grad_coarse_k: bfloat16 [4, 8, 2, 1024], P(None, 'rows', None, 'frames')
- grad_coarse_v: bfloat16 [4, 8, 2, 1024], P(None, 'rows', None, 'frames')
The draws below stay inside these ranges and needn't reach their ends.
All inputs are finite; a program needn't handle non-finite values.
Results may differ from the reference program's by a relative error of at most 0.023.
Values may be sent and summed in bfloat16 or wider, within the bound.
No kernel may reach another device: no remote copies, remote signals or barrier semaphores. Data moves between devices by JAX's collectives and lax.ppermute only.
A program may use at most 64 MiB of HBM per device.

```python
import math
import jax
import jax.numpy as jnp
from jax import lax

HD = 64
FINE_HEADS = 4
FWIDTH = 256
CWIDTH = 1024
KERNEL = 7
POOL = 8
STEPS = 1000
WIDTH = 16
FRAMES = 4
HEIGHT = 64
CROWS = 8
CCOLS = 2


def drawn(key, dims, query_spread):
    root_key = jax.random.fold_in(key, 7)
    key_query = jax.random.fold_in(root_key, 1)
    key_vectors = jax.random.fold_in(root_key, 2)
    key_values = jax.random.fold_in(root_key, 3)
    query = jax.random.normal(key_query, dims, jnp.float32) * query_spread
    vectors = jax.random.normal(key_vectors, dims, jnp.float32)
    values = jax.random.normal(key_values, dims, jnp.float32)
    query = jnp.clip(query, -24.0, 24.0)
    vectors = jnp.clip(vectors, -24.0, 24.0)
    values = jnp.clip(values, -24.0, 24.0)
    return (query, vectors, values)


def fine_draw(key):
    return drawn(key, (FRAMES, HEIGHT, WIDTH, FINE_HEADS, HD), 1.0)


def coarse_draw(key):
    return drawn(key, (FRAMES, CROWS, CCOLS, CWIDTH // HD, HD), 2.0)


def draw_fine_q(key, part):
    query, vectors, values = fine_draw(key)
    return query.reshape(FRAMES, HEIGHT, WIDTH, FWIDTH).astype(jnp.bfloat16)


def draw_fine_kv(key, part):
    query, vectors, values = fine_draw(key)
    joined = jnp.concatenate([vectors.reshape(FRAMES, HEIGHT, WIDTH, FWIDTH), values.reshape(FRAMES, HEIGHT, WIDTH, FWIDTH)], axis=-1)
    return joined.astype(jnp.bfloat16)


def draw_coarse_q(key, part):
    query, vectors, values = coarse_draw(key)
    return query.reshape(FRAMES, CROWS, CCOLS, CWIDTH).astype(jnp.bfloat16)


def draw_coarse_kv(key, part):
    query, vectors, values = coarse_draw(key)
    joined = jnp.concatenate([vectors.reshape(FRAMES, CROWS, CCOLS, CWIDTH), values.reshape(FRAMES, CROWS, CCOLS, CWIDTH)], axis=-1)
    return joined.astype(jnp.bfloat16)


def plant(result, own_key, smallest, top_value):
    spot = [jax.random.randint(jax.random.fold_in(own_key, axis), (), 0, length) for axis, length in enumerate(result.shape)]
    longest = result.shape.index(max(result.shape))
    next_to = spot[:longest] + [(spot[longest] + 1) % result.shape[longest]] + spot[longest + 1:]
    return result.at[tuple(spot)].set(smallest).at[tuple(next_to)].set(top_value)


def steps_of(rng, shape, cuts, smallest, high):
    def one(dim, blocks):
        steps = jax.random.uniform(jax.random.fold_in(jax.random.fold_in(rng, 6), dim), (blocks,), jnp.float32, smallest / len(cuts), high / len(cuts))
        return jnp.repeat(jnp.exp(steps), shape[dim] // blocks).reshape((-1,) + (1,) * (len(shape) - dim - 1))

    level = one(*cuts[0])
    for cut in cuts[1:]:
        level = level * one(*cut)
    return level


def bell_draw(own_key, shape, spread, reach, cuts=(), kind=jnp.bfloat16):
    gain = steps_of(own_key, shape, cuts, -0.22, 0.18) if cuts else 1.0
    drawn = jax.random.normal(own_key, shape, jnp.float32) * spread * gain
    return jnp.minimum(jnp.maximum(drawn, -reach), reach).astype(kind)


def setup_inputs(seed: int = 0) -> dict:
    splits = jax.random.split(jax.random.key(seed), 9)
    fine_q = draw_fine_q(jax.random.fold_in(splits[8], 71), 0)
    fine_kv = draw_fine_kv(jax.random.fold_in(splits[8], 71), 0)
    coarse_q = draw_coarse_q(jax.random.fold_in(splits[8], 71), 0)
    coarse_kv = draw_coarse_kv(jax.random.fold_in(splits[8], 71), 0)
    cotangent = bell_draw(splits[4], (FRAMES, HEIGHT, WIDTH, FWIDTH), 1.0, 6.0, ((0, 4), (1, 8)))
    gain_table = jnp.clip(jnp.exp(jax.random.uniform(splits[5], (STEPS, FWIDTH), jnp.float32, math.log(0.3), math.log(3.0))), 0.3, 3.0)
    timesteps = plant(jax.random.randint(splits[6], (FRAMES,), 0, STEPS), jax.random.fold_in(splits[6], 1), 0, STEPS - 1).astype(jnp.int32)
    valid_cols = plant(jax.random.randint(splits[7], (FRAMES,), WIDTH // 2, WIDTH + 1), jax.random.fold_in(splits[7], 1), WIDTH // 2, WIDTH).astype(jnp.int32)
    return dict(fine_q=fine_q, fine_kv=fine_kv, coarse_q=coarse_q, coarse_kv=coarse_kv, cotangent=cotangent, gain_table=gain_table, timesteps=timesteps, valid_cols=valid_cols)


NEGATIVE = -1e+30

def lowered(value):
    return lax.optimization_barrier(value.astype(jnp.bfloat16)).astype(jnp.float32)

def fine_frame(record):
    query, key_value, grad, valid = record
    height, width, fine_width = query.shape
    head_count = fine_width // HD
    radius = KERNEL // 2
    score_scale = 1.0 / math.sqrt(HD)
    query_wide = query.astype(jnp.float32).reshape(height, width, head_count, HD)
    padded = jnp.pad(key_value.astype(jnp.float32), ((radius, radius), (radius, radius), (0, 0)))
    key_table = padded[..., :fine_width].reshape(height + 2 * radius, width + 2 * radius, head_count, HD)
    value_table = padded[..., fine_width:].reshape(height + 2 * radius, width + 2 * radius, head_count, HD)
    grad_table = lowered(grad).reshape(height, width, head_count, HD)
    row_ids = jnp.arange(height)[:, None]
    col_ids = jnp.arange(width)[None, :]
    offsets = [(row_step, col_step) for row_step in range(-radius, radius + 1) for col_step in range(-radius, radius + 1)]

    def shifted(table, row_step, col_step):
        return table[radius + row_step:radius + row_step + height, radius + col_step:radius + col_step + width]
    score_list = []
    for row_step, col_step in offsets:
        product = lax.optimization_barrier(jnp.sum(query_wide * shifted(key_table, row_step, col_step), axis=-1)) * score_scale
        inside = (row_ids + row_step >= 0) & (row_ids + row_step < height) & (col_ids + col_step >= 0) & (col_ids + col_step < width) & (col_ids + col_step < valid)
        if row_step == 0 and col_step == 0:
            inside = jnp.ones_like(inside)
        score_list.append(jnp.where(inside[..., None], product, NEGATIVE))
    scores = jnp.stack(score_list)
    row_max = lax.optimization_barrier(jnp.max(scores, axis=0))
    log_total = row_max + jnp.log(lax.optimization_barrier(jnp.sum(jnp.exp(scores - row_max), axis=0)))
    weights = jnp.exp(scores - log_total)
    weights_low = lowered(weights)
    attended = jnp.zeros((height, width, head_count, HD), jnp.float32)
    for which, (row_step, col_step) in enumerate(offsets):
        attended = attended + weights_low[which][..., None] * shifted(value_table, row_step, col_step)
    row_dot = lax.optimization_barrier(jnp.sum(grad_table * attended, axis=-1))
    query_grad = jnp.zeros((height, width, head_count, HD), jnp.float32)
    key_grad = jnp.zeros(key_table.shape, jnp.float32)
    value_grad = jnp.zeros(value_table.shape, jnp.float32)
    for which, (row_step, col_step) in enumerate(offsets):
        key_part = shifted(key_table, row_step, col_step)
        value_part = shifted(value_table, row_step, col_step)
        weight_grad = lax.optimization_barrier(jnp.sum(grad_table * value_part, axis=-1))
        score_grad = lowered(weights[which] * (weight_grad - row_dot))
        query_grad = query_grad + score_grad[..., None] * key_part * score_scale
        row_lo = radius + row_step
        col_lo = radius + col_step
        key_grad = key_grad.at[row_lo:row_lo + height, col_lo:col_lo + width].add(score_grad[..., None] * query_wide * score_scale)
        value_grad = value_grad.at[row_lo:row_lo + height, col_lo:col_lo + width].add(weights_low[which][..., None] * grad_table)
    key_grad = key_grad[radius:radius + height, radius:radius + width].reshape(height, width, fine_width)
    value_grad = value_grad[radius:radius + height, radius:radius + width].reshape(height, width, fine_width)
    return (query_grad.reshape(height, width, fine_width).astype(jnp.bfloat16), jnp.concatenate([key_grad, value_grad], axis=-1).astype(jnp.bfloat16))

def reference(fine_q, fine_kv, coarse_q, coarse_kv, cotangent, gain_table, timesteps, valid_cols):
    frame_gain = gain_table[timesteps]
    scaled_grad = frame_gain[:, None, None, :] * cotangent.astype(jnp.float32)
    grad_fine_q, grad_fine_kv = lax.map(fine_frame, (fine_q, fine_kv, scaled_grad, valid_cols))
    half_pool = POOL // 2
    token_count = FRAMES * CROWS * CCOLS
    head_count = CWIDTH // HD
    score_scale = 1.0 / math.sqrt(HD)
    blocks = scaled_grad.reshape(FRAMES, CROWS, 2, half_pool, CCOLS, 2, half_pool, FWIDTH)
    pooled = lax.optimization_barrier(jnp.sum(blocks, axis=(3, 6))).transpose(0, 1, 3, 2, 4, 5).reshape(token_count, CWIDTH)
    coarse_grad = pooled.astype(jnp.bfloat16)
    token_ids = jnp.arange(token_count)
    frame_of = token_ids // (CROWS * CCOLS)
    col_of = token_ids % CCOLS
    key_ok = col_of * POOL < valid_cols[frame_of]

    def split(table):
        return table.reshape(token_count, head_count, HD).transpose(1, 0, 2)

    def coarse_head(record):
        query, keyset, valueset, grad = record
        scores = jnp.dot(query, keyset.T, preferred_element_type=jnp.float32) * score_scale
        scores = jnp.where(key_ok[None, :], scores, NEGATIVE)
        row_max = lax.optimization_barrier(jnp.max(scores, axis=-1, keepdims=True))
        log_total = row_max + jnp.log(lax.optimization_barrier(jnp.sum(jnp.exp(scores - row_max), axis=-1, keepdims=True)))
        weights = jnp.exp(scores - log_total)
        weights_low = weights.astype(jnp.bfloat16)
        attended = jnp.dot(weights_low, valueset, preferred_element_type=jnp.float32)
        row_dot = lax.optimization_barrier(jnp.sum(grad.astype(jnp.float32) * attended, axis=-1))
        weight_grad = jnp.dot(grad, valueset.T, preferred_element_type=jnp.float32)
        score_grad = (weights * (weight_grad - row_dot[:, None])).astype(jnp.bfloat16)
        query_grad = jnp.dot(score_grad, keyset, preferred_element_type=jnp.float32) * score_scale
        key_grad = jnp.dot(score_grad.T, query, preferred_element_type=jnp.float32) * score_scale
        value_grad = jnp.dot(weights_low.T, grad, preferred_element_type=jnp.float32)
        return (query_grad, key_grad, value_grad)
    query_all = split(coarse_q)
    key_all = split(coarse_kv[..., :CWIDTH])
    value_all = split(coarse_kv[..., CWIDTH:])
    grad_all = split(coarse_grad)
    query_grad, key_grad, value_grad = lax.map(coarse_head, (query_all, key_all, value_all, grad_all))

    def merge(table):
        return table.transpose(1, 0, 2).reshape(FRAMES, CROWS, CCOLS, CWIDTH).astype(jnp.bfloat16)
    return (grad_fine_q, grad_fine_kv, merge(query_grad), merge(key_grad), merge(value_grad))
```

```python
import functools
import math

import jax
import jax.numpy as jnp
from jax import lax
from jax.experimental import pallas as pl
from jax.experimental.pallas import tpu as pltpu
from jax.sharding import PartitionSpec as P

HD = 64
KERNEL = 7
POOL = 8
LANES = 128

NEGATIVE = -1e30

F32 = jnp.float32
BF16 = jnp.bfloat16


def dot_nt(left, right):
    return lax.dot_general(left, right, (((1,), (1,)), ((), ())), preferred_element_type=F32)


def dot_nn(left, right):
    return jnp.dot(left, right, preferred_element_type=F32)


def iota(shape, dim):
    return lax.broadcasted_iota(jnp.int32, shape, dim)


def per_head(table):
    head = iota(table.shape, 1) // HD
    return [jnp.where(head == h, table, jnp.zeros_like(table)) for h in range(table.shape[1] // HD)]


def softmax_grads(scores, weight_grad, axis):
    top = jnp.max(scores, axis=axis, keepdims=True)
    raised = jnp.exp(scores - top)
    weights = raised * (1.0 / jnp.sum(raised, axis=axis, keepdims=True))
    low = weights.astype(BF16)
    row_dot = jnp.sum(low.astype(F32) * weight_grad, axis=axis, keepdims=True)
    return low, (weights * (weight_grad - row_dot)).astype(BF16)


def gain_row(step_ref, gain_ref):
    step = step_ref[0] % gain_ref.shape[0]
    rows = iota(gain_ref.shape, 0)
    return jnp.sum(jnp.where(rows == step, gain_ref[...], 0.0), axis=0, keepdims=True)


def prep_kernel(cols, step_ref, q_ref, kv_ref, cot_ref, gain_ref, near_ref, far_ref, grad_ref):
    radius = KERNEL // 2
    pixels, width = q_ref.shape
    one, two = radius * cols, 2 * radius * cols
    even = lax.axis_index("rows") % 2 == 0
    gain = gain_row(step_ref, gain_ref)
    grad_ref[...] = (gain * cot_ref[...].astype(F32)).astype(BF16)

    def pack(target, top):
        lo_one, lo_two = (0, 0) if top else (pixels - one, pixels - two)
        target[:two, :] = kv_ref[lo_two : lo_two + two, :]
        target[two:, :width] = q_ref[lo_one : lo_one + one, :]
        target[two:, width:] = grad_ref[lo_one : lo_one + one, :]

    @pl.when(even)
    def _():
        pack(near_ref, False)
        pack(far_ref, True)

    @pl.when(jnp.logical_not(even))
    def _():
        pack(near_ref, True)
        pack(far_ref, False)


def send_kernel(cols, bands, step_ref, cot_ref, gain_ref, cq_ref, ckv_ref, send_ref):
    pixels, width = cot_ref.shape
    tokens, cwidth = cq_ref.shape
    half = POOL // 2
    groups = cwidth // width
    part = iota((groups * tokens, pixels), 0)
    group, token = part // tokens, part % tokens
    pixel = iota((groups * tokens, pixels), 1)
    row, col = pixel // cols, pixel % cols
    inside = (row // half == group // 2) & (col // half == token * 2 + group % 2)
    pooled = dot_nn(inside.astype(BF16), cot_ref[...]) * gain_row(step_ref, gain_ref)
    query = cq_ref[...].astype(F32)
    both = ckv_ref[...].astype(F32)
    for g in range(groups):
        lo = g * width
        arrays = (
            query[:, lo : lo + width],
            both[:, lo : lo + width],
            both[:, cwidth + lo : cwidth + lo + width],
            pooled[g * tokens : (g + 1) * tokens, :],
        )
        tile = jnp.concatenate(
            [a[:, b : b + LANES] for a in arrays for b in range(0, width, LANES)], axis=0
        ).astype(BF16)
        height = tile.shape[0]
        for r in range(bands):
            start = (g * bands + r) * height
            send_ref[start : start + height, :] = tile


def fine_kernel(cols, valid_ref, q_ref, kv_ref, grad_ref, near_ref, far_ref, dq_ref, dkv_ref):
    radius = KERNEL // 2
    pixels, width = q_ref.shape
    rows = pixels // cols
    one, two = radius * cols, 2 * radius * cols
    scale = 1.0 / math.sqrt(HD)
    band = lax.axis_index("rows")
    valid = valid_ref[lax.axis_index("frames")]
    first, last = band == 0, band == lax.axis_size("rows") - 1
    even = band % 2 == 0

    def received(rows_at, cols_at):
        near, far = near_ref[rows_at, cols_at], far_ref[rows_at, cols_at]
        return jnp.where(even, far, near), jnp.where(even, near, far)

    def extended(cols_at):
        above, below = received(slice(0, two), cols_at)
        return jnp.concatenate([above, kv_ref[:, cols_at], below], axis=0)

    keys, values = extended(slice(0, width)), extended(slice(width, 2 * width))
    q_above, q_below = received(slice(two, two + one), slice(0, width))
    g_above, g_below = received(slice(two, two + one), slice(width, 2 * width))

    def bias(key_count, key_row, lanes, query_count, query_row, ends):
        key, lane = iota((key_count, lanes), 0), iota((key_count, lanes), 1) % query_count
        krow, kcol = key // cols + key_row, key % cols
        qrow, qcol = lane // cols + query_row, lane % cols
        seen = (jnp.abs(krow - qrow) <= radius) & (jnp.abs(kcol - qcol) <= radius) & (kcol < valid)
        if ends:
            seen = seen & ((krow >= 0) | jnp.logical_not(first))
            seen = seen & ((krow < rows) | jnp.logical_not(last))
        seen = seen | ((krow == qrow) & (kcol == qcol))
        return jnp.where(seen, 0.0, NEGATIVE)

    lo, hi = one, one + pixels + two
    own_keys, own_values = keys[lo:hi], values[lo:hi]
    own_bias = bias(hi - lo, -radius, pixels, pixels, 0, True)
    queries, grads = per_head(q_ref[...] * scale), per_head(grad_ref[...])
    keys_t = own_keys.T
    lows, sgrads, dq_t = [], [], []
    for h, (query, grad) in enumerate(zip(queries, grads)):
        low, sgrad = softmax_grads(
            dot_nt(own_keys, query) + own_bias, dot_nt(own_values, grad), 0
        )
        lows.append(low[one : one + pixels])
        sgrads.append(sgrad[one : one + pixels])
        dq_t.append(dot_nn(keys_t[h * HD : (h + 1) * HD], sgrad))
    dq_ref[...] = (jnp.concatenate(dq_t, axis=0).T * scale).astype(BF16)
    dk = dot_nn(jnp.concatenate(sgrads, axis=1), jnp.concatenate(queries, axis=0))
    dv = dot_nn(jnp.concatenate(lows, axis=1), jnp.concatenate(grads, axis=0))

    pad = jnp.zeros((cols, width), BF16)

    def outside(query, grad, key_lo, key_row, query_row, keep):
        stacked = [
            jnp.concatenate([x for head in per_head(t) for x in (head, pad)], axis=0)
            for t in (query * scale, grad)
        ]
        count = one + two
        lanes = stacked[0].shape[0]
        low, sgrad = softmax_grads(
            dot_nt(keys[key_lo : key_lo + count], stacked[0])
            + bias(count, key_row, lanes, one + cols, query_row, False),
            dot_nt(values[key_lo : key_lo + count], stacked[1]),
            0,
        )
        return (
            dot_nn(sgrad[keep : keep + one], stacked[0]),
            dot_nn(low[keep : keep + one], stacked[1]),
        )

    dk_above, dv_above = outside(q_above, g_above, 0, -2 * radius, -radius, two)
    dk_below, dv_below = outside(q_below, g_below, pixels + one, rows - radius, rows, 0)
    for at, (inner, above, below) in enumerate(((dk, dk_above, dk_below), (dv, dv_above, dv_below))):
        dkv_ref[:, at * width : (at + 1) * width] = jnp.concatenate(
            [inner[:one] + above, inner[one : pixels - one], inner[pixels - one :] + below], axis=0
        ).astype(BF16)


def coarse_kernel(frames, tokens, valid_ref, x_ref, dq_ref, dk_ref, dv_ref, wide, low_ref, sg_ref):
    bands = lax.axis_size("rows")
    width = dq_ref.shape[-1]
    parts = width // LANES
    height = x_ref.shape[0] // (frames * bands)
    band = lax.axis_index("rows")
    scale = 1.0 / math.sqrt(HD)
    wide[...] = x_ref[...].astype(F32)

    def every(array):
        def piece(t, b):
            return wide[pl.ds((array * parts + b) * tokens + t, frames * bands, stride=height), :]

        return jnp.concatenate(
            [
                jnp.concatenate([piece(t, b) for b in range(parts)], axis=1)
                for t in range(tokens)
            ],
            axis=0,
        ).astype(BF16)

    def mine(array):
        def piece(f, b):
            start = (f * bands + band) * height + (array * parts + b) * tokens
            return wide[pl.ds(start, tokens), :]

        return jnp.concatenate(
            [
                jnp.concatenate([piece(f, b) for b in range(parts)], axis=1)
                for f in range(frames)
            ],
            axis=0,
        ).astype(BF16)

    query, key, value, grad = (every(a) for a in range(4))
    count = query.shape[0]

    def key_bias(shape, dim):
        place = iota(shape, dim)
        token, frame = place // (frames * bands), place // bands % frames
        limit = jnp.zeros(shape, jnp.int32)
        for f in range(frames):
            limit = jnp.where(frame == f, valid_ref[f], limit)
        return jnp.where(token * POOL < limit, 0.0, NEGATIVE)

    own_query, own_grad = per_head(mine(0) * scale), per_head(mine(3))
    own = frames * tokens
    heads = len(own_query)
    stacked = jnp.concatenate(own_query, axis=0)
    _, sgrad = softmax_grads(
        dot_nt(stacked, key) + key_bias((heads * own, count), 1),
        dot_nt(jnp.concatenate(own_grad, axis=0), value),
        1,
    )
    full = dot_nn(sgrad, key)
    head = iota((own, width), 1) // HD
    dq = sum(
        jnp.where(head == h, full[h * own : (h + 1) * own], 0.0) for h in range(heads)
    )
    queries = jnp.concatenate(per_head(query * scale), axis=0)
    grads = jnp.concatenate(per_head(grad), axis=0)
    low, sgrad = softmax_grads(
        dot_nt(key, queries) + key_bias((count, heads * count), 0), dot_nt(value, grads), 0
    )
    low_ref[...] = low.astype(F32)
    sg_ref[...] = sgrad.astype(F32)

    def mine_rows(ref):
        pieces = [
            ref[pl.ds(t * frames * bands + f * bands + band, 1), :]
            for f in range(frames)
            for t in range(tokens)
        ]
        return jnp.concatenate(pieces, axis=0).astype(BF16)

    dk = dot_nn(mine_rows(sg_ref), queries)
    dv = dot_nn(mine_rows(low_ref), grads)
    for ref, table in ((dq_ref, dq * scale), (dk_ref, dk), (dv_ref, dv)):
        rounded = table.astype(BF16)
        for f in range(frames):
            ref[f] = rounded[f * tokens : (f + 1) * tokens]


def vmem():
    return pl.BlockSpec(memory_space=pltpu.VMEM)


def smem():
    return pl.BlockSpec(memory_space=pltpu.SMEM)


def with_gain(kernel, ins, outs, scratch=()):
    def whole(shape):
        return pl.BlockSpec(shape, lambda i, step: (0,) * len(shape))

    def call(step, *operands):
        specs = [
            whole(x.shape)
            if at != ins
            else pl.BlockSpec((8, x.shape[1]), lambda i, step: (step[0] // 8, 0))
            for at, x in enumerate(operands)
        ]
        return pl.pallas_call(
            kernel,
            grid_spec=pltpu.PrefetchScalarGridSpec(
                num_scalar_prefetch=1,
                grid=(1,),
                in_specs=specs,
                out_specs=[whole(shape) for shape in outs],
                scratch_shapes=scratch,
            ),
            out_shape=[jax.ShapeDtypeStruct(shape, BF16) for shape in outs],
        )(step, *operands)

    return call


def fine_level(fine_q, fine_kv, cotangent, gain_table, timesteps, valid_cols):
    bands = lax.axis_size("rows")
    _, rows, cols, width = fine_q.shape
    pixels = rows * cols
    radius = KERNEL // 2
    query = fine_q.reshape(pixels, width)
    key_value = fine_kv.reshape(pixels, 2 * width)
    cot = cotangent.reshape(pixels, width)
    packed = (3 * radius * cols, 2 * width)
    near, far, grad = with_gain(
        functools.partial(prep_kernel, cols), 3, (packed, packed, (pixels, width))
    )(timesteps, query, key_value, cot, gain_table)
    pairs = [(i, i ^ 1) for i in range(bands) if i ^ 1 < bands]
    others = [(i, ((i + 1) ^ 1) - 1) for i in range(1, bands) if ((i + 1) ^ 1) - 1 < bands]
    near = lax.ppermute(near, "rows", pairs)
    far = lax.ppermute(far, "rows", others)
    grad_q, grad_kv = pl.pallas_call(
        functools.partial(fine_kernel, cols),
        in_specs=[smem()] + [vmem()] * 5,
        out_specs=[vmem()] * 2,
        out_shape=[
            jax.ShapeDtypeStruct((pixels, width), BF16),
            jax.ShapeDtypeStruct((pixels, 2 * width), BF16),
        ],
        cost_estimate=pl.CostEstimate(flops=400_000_000, bytes_accessed=1_000_000, transcendentals=300_000),
    )(valid_cols, query, key_value, grad, near, far)
    return grad_q.reshape(fine_q.shape), grad_kv.reshape(fine_kv.shape)


def coarse_direct(coarse_q, coarse_kv, cotangent, gain_table, timesteps, valid_cols):
    frames, bands = lax.axis_size("frames"), lax.axis_size("rows")
    _, rows, cols, width = cotangent.shape
    tokens, cwidth = coarse_q.shape[-2:]
    head_width = cwidth // frames
    tile = 4 * tokens * head_width // LANES
    (sent,) = with_gain(
        functools.partial(send_kernel, cols, bands), 1, ((frames * bands * tile, LANES),)
    )(
        timesteps,
        cotangent.reshape(rows * cols, width),
        gain_table,
        coarse_q.reshape(tokens, cwidth),
        coarse_kv.reshape(tokens, 2 * cwidth),
    )
    held = lax.all_to_all(
        sent.reshape(frames * bands, tile, LANES),
        ("frames", "rows"),
        split_axis=0,
        concat_axis=0,
        tiled=True,
    ).reshape(frames * bands * tile, LANES)
    count = frames * bands * tokens
    heads = head_width // HD
    outs = pl.pallas_call(
        functools.partial(coarse_kernel, frames, tokens),
        in_specs=[smem(), vmem()],
        out_specs=[vmem()] * 3,
        out_shape=[jax.ShapeDtypeStruct((frames, tokens, head_width), BF16)] * 3,
        scratch_shapes=[
            pltpu.VMEM(held.shape, F32),
            pltpu.VMEM((count, heads * count), F32),
            pltpu.VMEM((count, heads * count), F32),
        ],
    )(valid_cols, held)
    return tuple(out.reshape(frames, 1, tokens, head_width) for out in outs)


def normalize(scores):
    row_max = jnp.max(scores, axis=-1, keepdims=True)
    return row_max + jnp.log(jnp.sum(jnp.exp(scores - row_max), axis=-1, keepdims=True))


def coarse_gathered(coarse_q, coarse_kv, cotangent, gain_table, timesteps, valid_cols):
    score_scale = 1.0 / math.sqrt(HD)
    frames_here, _, cols_here, fine_width = cotangent.shape
    total_frames = valid_cols.shape[0]
    steps_all = gain_table.shape[0]
    select = (timesteps[:, None] == jnp.arange(steps_all)[None, :]).astype(F32)
    frame_gain = jnp.dot(select, gain_table, precision=lax.Precision.HIGHEST)
    scaled_grad = frame_gain[:, None, None, :] * cotangent.astype(F32)
    half_pool = POOL // 2
    coarse_cols = cols_here // POOL
    coarse_width = coarse_q.shape[-1]
    coarse_count = frames_here * coarse_cols
    blocks = scaled_grad.reshape(frames_here, 2, half_pool, coarse_cols, 2, half_pool, fine_width)
    pooled = (
        jnp.sum(blocks, axis=(2, 5))
        .transpose(0, 2, 1, 3, 4)
        .reshape(coarse_count, coarse_width)
        .astype(BF16)
    )
    mine_query = coarse_q.reshape(coarse_count, coarse_width)
    mine_keys = coarse_kv[..., :coarse_width].reshape(coarse_count, coarse_width)
    mine_values = coarse_kv[..., coarse_width:].reshape(coarse_count, coarse_width)
    head_query, head_keys, head_values, head_grad = (
        lax.all_to_all(mine_query, "frames", split_axis=1, concat_axis=0, tiled=True),
        lax.all_to_all(mine_keys, "frames", split_axis=1, concat_axis=0, tiled=True),
        lax.all_to_all(mine_values, "frames", split_axis=1, concat_axis=0, tiled=True),
        lax.all_to_all(pooled, "frames", split_axis=1, concat_axis=0, tiled=True),
    )
    head_tokens, head_width = head_query.shape
    head_groups = head_width // HD
    query_heads = head_query.reshape(head_tokens, head_groups, HD)
    grad_heads = head_grad.reshape(head_tokens, head_groups, HD)
    every_keys, every_values = (
        lax.all_gather(head_keys, "rows", axis=0, tiled=True),
        lax.all_gather(head_values, "rows", axis=0, tiled=True),
    )
    every_count = every_keys.shape[0]
    key_heads = every_keys.reshape(every_count, head_groups, HD)
    value_heads = every_values.reshape(every_count, head_groups, HD)
    position = jnp.arange(every_count) % head_tokens
    key_frame = position // coarse_cols
    key_column = position % coarse_cols
    col_limit = jnp.sum(
        jnp.where(key_frame[:, None] == jnp.arange(total_frames)[None, :], valid_cols[None, :], 0),
        axis=1,
    )
    key_ok = key_column * POOL < col_limit
    coarse_scores = (
        jnp.einsum("qhd,khd->hqk", query_heads, key_heads, preferred_element_type=F32)
        * score_scale
    )
    coarse_scores = jnp.where(key_ok[None, None, :], coarse_scores, NEGATIVE)
    log_total = normalize(coarse_scores)
    coarse_weights = jnp.exp(coarse_scores - log_total)
    coarse_low = coarse_weights.astype(BF16)
    coarse_out = jnp.einsum("hqk,khd->qhd", coarse_low, value_heads, preferred_element_type=F32)
    coarse_dot = jnp.sum(grad_heads.astype(F32) * coarse_out, axis=-1)
    coarse_wgrad = jnp.einsum("qhd,khd->hqk", grad_heads, value_heads, preferred_element_type=F32)
    coarse_sgrad = (coarse_weights * (coarse_wgrad - coarse_dot.T[:, :, None])).astype(BF16)
    coarse_qgrad = (
        jnp.einsum("hqk,khd->qhd", coarse_sgrad, key_heads, preferred_element_type=F32)
        * score_scale
    )
    count = head_tokens * lax.axis_size("rows")
    key_part = (
        jnp.einsum("hqk,qhd->khd", coarse_sgrad, query_heads, preferred_element_type=F32)
        * score_scale
    )
    value_part = jnp.einsum("hqk,qhd->khd", coarse_low, grad_heads, preferred_element_type=F32)
    terms = lax.psum_scatter(
        jnp.concatenate(
            [key_part.reshape(count, head_width), value_part.reshape(count, head_width)], axis=1
        ),
        "rows",
        scatter_dimension=0,
        tiled=True,
    )
    total_keys = terms[:, :head_width]
    total_values = terms[:, head_width:]
    out_dims = (head_tokens // coarse_cols, 1, coarse_cols, head_width)
    return (
        coarse_qgrad.reshape(out_dims).astype(BF16),
        total_keys.reshape(out_dims).astype(BF16),
        total_values.reshape(out_dims).astype(BF16),
    )


def local(fine_q, fine_kv, coarse_q, coarse_kv, cotangent, gain_table, timesteps, valid_cols):
    frames, bands = lax.axis_size("frames"), lax.axis_size("rows")
    head_width = coarse_q.shape[-1] // frames
    tokens = coarse_q.shape[-2]
    direct = (
        head_width == cotangent.shape[-1]
        and 4 * tokens * head_width // LANES == 16
        and frames * bands * tokens <= 128
    )
    coarse = coarse_direct if direct else coarse_gathered
    coarse_grads = coarse(coarse_q, coarse_kv, cotangent, gain_table, timesteps, valid_cols)
    fine_grads = fine_level(fine_q, fine_kv, cotangent, gain_table, timesteps, valid_cols)
    return fine_grads + coarse_grads


def solution(mesh):
    placed = (
        P("frames", "rows", None, None),
        P("frames", "rows", None, None),
        P("frames", "rows", None, None),
        P("frames", "rows", None, None),
        P("frames", "rows", None, None),
        P(),
        P("frames"),
        P(),
    )
    return jax.shard_map(
        local,
        mesh=mesh,
        in_specs=placed,
        out_specs=(
            P("frames", "rows", None, None),
            P("frames", "rows", None, None),
            P(None, "rows", None, "frames"),
            P(None, "rows", None, "frames"),
            P(None, "rows", None, "frames"),
        ),
        check_vma=False,
    )
```

```python
import functools
import math

import jax
import jax.numpy as jnp
from jax import lax
from jax.experimental import pallas as pl
from jax.experimental.pallas import tpu as pltpu
from jax.sharding import PartitionSpec as P

HD = 64
KERNEL = 7
POOL = 8
LANES = 128

NEGATIVE = -1e30

F32 = jnp.float32
BF16 = jnp.bfloat16


def dot_nt(left, right):
    return lax.dot_general(left, right, (((1,), (1,)), ((), ())), preferred_element_type=F32)


def dot_nn(left, right):
    return jnp.dot(left, right, preferred_element_type=F32)


def iota(shape, dim):
    return lax.broadcasted_iota(jnp.int32, shape, dim)


def pairs_of(table):
    blocks = []
    for lo in range(0, table.shape[1], LANES):
        part = table[:, lo : lo + LANES]
        first = iota(part.shape, 1) < HD
        zero = jnp.zeros_like(part)
        blocks.append(
            jnp.concatenate([jnp.where(first, part, zero), jnp.where(first, zero, part)], axis=0)
        )
    return blocks


def softmax_grads(scores, weight_grad, axis):
    top = jnp.max(scores, axis=axis, keepdims=True)
    raised = jnp.exp(scores - top)
    weights = raised * (1.0 / jnp.sum(raised, axis=axis, keepdims=True))
    low = weights.astype(BF16)
    row_dot = jnp.sum(low.astype(F32) * weight_grad, axis=axis, keepdims=True)
    return low, (weights * (weight_grad - row_dot)).astype(BF16)


def send_kernel(
    cols, bands, step_ref, cot_hbm, gain_hbm, cq_hbm, ckv_hbm,
    send_ref, gain_ref, cot_ref, eight_ref, cq_ref, ckv_ref, sems,
):
    step = step_ref[0]
    eight = eight_ref.shape[0]
    first = pl.multiple_of(step // eight * eight, eight)
    gain_copy = pltpu.make_async_copy(gain_hbm.at[pl.ds(first, eight)], eight_ref, sems.at[0])
    gain_copy.start()
    copies = [
        pltpu.make_async_copy(source, target, sems.at[1 + at])
        for at, (source, target) in enumerate(
            ((cot_hbm, cot_ref), (cq_hbm, cq_ref), (ckv_hbm, ckv_ref))
        )
    ]
    for copy in copies:
        copy.start()
    pixels, width = cot_ref.shape
    tokens, cwidth = cq_ref.shape
    half = POOL // 2
    groups = cwidth // width
    part = iota((groups * tokens, pixels), 0)
    group, token = part // tokens, part % tokens
    pixel = iota((groups * tokens, pixels), 1)
    row, col = pixel // cols, pixel % cols
    inside = (row // half == group // 2) & (col // half == token * 2 + group % 2)
    for copy in copies:
        copy.wait()
    summed = dot_nn(inside.astype(BF16), cot_ref[...])
    query = cq_ref[...].astype(F32)
    both = ckv_ref[...].astype(F32)
    gain_copy.wait()
    gain = eight_ref[pl.ds(step - first, 1), :]
    gain_ref[...] = gain
    pooled = summed * gain
    for g in range(groups):
        lo = g * width
        arrays = (
            query[:, lo : lo + width],
            both[:, lo : lo + width],
            both[:, cwidth + lo : cwidth + lo + width],
            pooled[g * tokens : (g + 1) * tokens, :],
        )
        tile = jnp.concatenate(
            [a[:, b : b + LANES] for a in arrays for b in range(0, width, LANES)], axis=0
        ).astype(BF16)
        height = tile.shape[0]
        for r in range(bands):
            start = (g * bands + r) * height
            send_ref[start : start + height, :] = tile


def prep_kernel(cols, gain_ref, q_ref, kv_ref, cot_ref, near_ref, far_ref, grad_ref):
    radius = KERNEL // 2
    pixels, width = q_ref.shape
    one, two = radius * cols, 2 * radius * cols
    even = lax.axis_index("rows") % 2 == 0
    grad_ref[...] = (gain_ref[...] * cot_ref[...].astype(F32)).astype(BF16)

    def pack(target, top):
        lo_one, lo_two = (0, 0) if top else (pixels - one, pixels - two)
        target[:two, :] = kv_ref[lo_two : lo_two + two, :]
        target[two:, :width] = q_ref[lo_one : lo_one + one, :]
        target[two:, width:] = grad_ref[lo_one : lo_one + one, :]

    @pl.when(even)
    def _():
        pack(near_ref, False)
        pack(far_ref, True)

    @pl.when(jnp.logical_not(even))
    def _():
        pack(near_ref, True)
        pack(far_ref, False)


def fine_kernel(cols, valid_ref, after_ref, q_ref, kv_ref, grad_ref, near_ref, far_ref, dq_ref, dkv_ref):
    radius = KERNEL // 2
    pixels, width = q_ref.shape
    rows = pixels // cols
    one, two = radius * cols, 2 * radius * cols
    scale = 1.0 / math.sqrt(HD)
    band = lax.axis_index("rows")
    valid = valid_ref[lax.axis_index("frames")]
    first, last = band == 0, band == lax.axis_size("rows") - 1
    even = band % 2 == 0

    def received(rows_at, cols_at):
        near, far = near_ref[rows_at, cols_at], far_ref[rows_at, cols_at]
        return jnp.where(even, far, near), jnp.where(even, near, far)

    def extended(cols_at):
        above, below = received(slice(0, two), cols_at)
        return jnp.concatenate([above, kv_ref[:, cols_at], below], axis=0)

    keys, values = extended(slice(0, width)), extended(slice(width, 2 * width))
    q_above, q_below = received(slice(two, two + one), slice(0, width))
    g_above, g_below = received(slice(two, two + one), slice(width, 2 * width))

    def bias(key_count, key_row, lanes, query_count, query_row, ends):
        key, lane = iota((key_count, lanes), 0), iota((key_count, lanes), 1) & (query_count - 1)
        krow, kcol = (key >> 4) + key_row, key & (cols - 1)
        qrow, qcol = (lane >> 4) + query_row, lane & (cols - 1)
        seen = (jnp.abs(krow - qrow) <= radius) & (jnp.abs(kcol - qcol) <= radius) & (kcol < valid)
        if ends:
            seen = seen & ((krow >= 0) | jnp.logical_not(first))
            seen = seen & ((krow < rows) | jnp.logical_not(last))
        seen = seen | ((krow == qrow) & (kcol == qcol))
        return jnp.where(seen, 0.0, NEGATIVE)

    lo, hi = one, one + pixels + two
    own_keys, own_values = keys[lo:hi], values[lo:hi]
    own_bias = bias(hi - lo, -radius, pixels, pixels, 0, True)
    own_bias = jnp.concatenate([own_bias, own_bias], axis=1)
    keys_t = own_keys.T
    dq, dk, dv = [], [], []
    for p, (query, grad) in enumerate(zip(pairs_of(q_ref[...] * scale), pairs_of(grad_ref[...]))):
        at = slice(p * LANES, (p + 1) * LANES)
        low, sgrad = softmax_grads(
            dot_nt(own_keys[:, at], query) + own_bias, dot_nt(own_values[:, at], grad), 0
        )
        dq_t = dot_nn(keys_t[at], sgrad)
        dq_t = jnp.concatenate([dq_t[:HD, :pixels], dq_t[HD:, pixels:]], axis=0)
        dq.append((dq_t * scale).T)
        dk.append(dot_nn(sgrad[one : one + pixels], query))
        dv.append(dot_nn(low[one : one + pixels], grad))
    dq_ref[...] = jnp.concatenate(dq, axis=1).astype(BF16)

    pad = jnp.zeros((cols, width), BF16)

    def outside(query, grad, key_lo, key_row, query_row, keep):
        count, lanes = one + two, 2 * (one + cols)
        outside_bias = bias(count, key_row, lanes, one + cols, query_row, False)
        query, grad = (
            pairs_of(jnp.concatenate([t, pad], axis=0)) for t in (query * scale, grad)
        )
        found = []
        for p in range(len(query)):
            at = slice(p * LANES, (p + 1) * LANES)
            low, sgrad = softmax_grads(
                dot_nt(keys[key_lo : key_lo + count, at], query[p]) + outside_bias,
                dot_nt(values[key_lo : key_lo + count, at], grad[p]),
                0,
            )
            found.append(
                (
                    dot_nn(sgrad[keep : keep + one], query[p]),
                    dot_nn(low[keep : keep + one], grad[p]),
                )
            )
        return found

    above = outside(q_above, g_above, 0, -2 * radius, -radius, two)
    below = outside(q_below, g_below, pixels + one, rows - radius, rows, 0)
    for p in range(len(dk)):
        for at, inner in enumerate((dk[p], dv[p])):
            lo = at * width + p * LANES
            dkv_ref[:, lo : lo + LANES] = jnp.concatenate(
                [
                    inner[:one] + above[p][at],
                    inner[one : pixels - one],
                    inner[pixels - one :] + below[p][at],
                ],
                axis=0,
            ).astype(BF16)


def coarse_kernel(frames, tokens, valid_ref, x_ref, dq_ref, dk_ref, dv_ref, after_ref, wide, low_ref, sg_ref):
    bands = lax.axis_size("rows")
    width = dq_ref.shape[-1]
    parts = width // LANES
    height = x_ref.shape[0] // (frames * bands)
    band = lax.axis_index("rows")
    scale = 1.0 / math.sqrt(HD)
    wide[...] = x_ref[...].astype(F32)
    after_ref[...] = jnp.zeros_like(after_ref)
    devices, own = frames * bands, frames * tokens

    def every(array, b):
        first = (array * parts + b) * tokens
        return jnp.concatenate(
            [wide[pl.ds(first + t, devices, stride=height), :] for t in range(tokens)], axis=0
        ).astype(BF16)

    def mine(array, b):
        first = band * height + (array * parts + b) * tokens
        return jnp.concatenate(
            [wide[pl.ds(first + f * bands * height, tokens), :] for f in range(frames)], axis=0
        ).astype(BF16)

    count = devices * tokens

    def key_bias(shape, dim):
        place = iota(shape, dim)
        token, frame = place // devices, place // bands % frames
        limit = jnp.zeros(shape, jnp.int32)
        for f in range(frames):
            limit = jnp.where(frame == f, valid_ref[f], limit)
        return jnp.where(token * POOL < limit, 0.0, NEGATIVE)

    bias, own_bias = key_bias((count, 2 * count), 0), key_bias((2 * own, count), 1)
    for b in range(parts):
        at = slice(b * LANES, (b + 1) * LANES)
        key, value = every(1, b), every(2, b)
        (query,), (grad,) = pairs_of(every(0, b) * scale), pairs_of(every(3, b))
        low, sgrad = softmax_grads(dot_nt(key, query) + bias, dot_nt(value, grad), 0)
        low_ref[b] = low.astype(F32)
        sg_ref[b] = sgrad.astype(F32)

        def mine_rows(ref):
            pieces = [
                ref[b, pl.ds(t * devices + f * bands + band, 1), :]
                for f in range(frames)
                for t in range(tokens)
            ]
            return jnp.concatenate(pieces, axis=0).astype(BF16)

        (own_query,), (own_grad,) = pairs_of(mine(0, b) * scale), pairs_of(mine(3, b))
        _, own_sgrad = softmax_grads(
            dot_nt(own_query, key) + own_bias, dot_nt(own_grad, value), 1
        )
        full = dot_nn(own_sgrad, key)
        dq = jnp.where(iota((own, LANES), 1) < HD, full[:own], full[own:]) * scale
        dk = dot_nn(mine_rows(sg_ref), query)
        dv = dot_nn(mine_rows(low_ref), grad)
        for ref, table in ((dq_ref, dq), (dk_ref, dk), (dv_ref, dv)):
            rounded = table.astype(BF16)
            for f in range(frames):
                ref[f, :, at] = rounded[f * tokens : (f + 1) * tokens]


def vmem():
    return pl.BlockSpec(memory_space=pltpu.VMEM)


def smem():
    return pl.BlockSpec(memory_space=pltpu.SMEM)


def hbm():
    return pl.BlockSpec(memory_space=pltpu.HBM)


def in_hbm(array):
    return pltpu.with_memory_space_constraint(array, pltpu.HBM)


def params():
    return pltpu.CompilerParams(vmem_limit_bytes=16 * 2**20)


def out(shape, dtype=BF16):
    return jax.ShapeDtypeStruct(shape, dtype)


def fine_level(after, gain, fine_q, fine_kv, cotangent, valid_cols):
    bands = lax.axis_size("rows")
    _, rows, cols, width = fine_q.shape
    pixels = rows * cols
    radius = KERNEL // 2
    query = fine_q.reshape(pixels, width)
    key_value = fine_kv.reshape(pixels, 2 * width)
    cot = cotangent.reshape(pixels, width)
    packed = (3 * radius * cols, 2 * width)
    near, far, grad = pl.pallas_call(
        functools.partial(prep_kernel, cols),
        in_specs=[vmem()] * 4,
        out_specs=[vmem()] * 3,
        out_shape=[out(packed), out(packed), out((pixels, width))],
        compiler_params=params(),
    )(gain, query, key_value, cot)
    pairs = [(i, i ^ 1) for i in range(bands) if i ^ 1 < bands]
    others = [(i, ((i + 1) ^ 1) - 1) for i in range(1, bands) if ((i + 1) ^ 1) - 1 < bands]
    near = lax.ppermute(near, "rows", pairs)
    far = lax.ppermute(far, "rows", others)
    grad_q, grad_kv = pl.pallas_call(
        functools.partial(fine_kernel, cols),
        in_specs=[smem()] + [vmem()] * 6,
        out_specs=[vmem()] * 2,
        out_shape=[out((pixels, width)), out((pixels, 2 * width))],
        compiler_params=params(),
        cost_estimate=pl.CostEstimate(flops=400_000_000, bytes_accessed=1_000_000, transcendentals=300_000),
    )(valid_cols, after, query, key_value, grad, near, far)
    return grad_q.reshape(fine_q.shape), grad_kv.reshape(fine_kv.shape)


def coarse_direct(coarse_q, coarse_kv, cotangent, gain_table, timesteps, valid_cols):
    frames, bands = lax.axis_size("frames"), lax.axis_size("rows")
    _, rows, cols, width = cotangent.shape
    tokens, cwidth = coarse_q.shape[-2:]
    head_width = cwidth // frames
    tile = 4 * tokens * head_width // LANES
    sent, gain = pl.pallas_call(
        functools.partial(send_kernel, cols, bands),
        in_specs=[smem()] + [hbm()] * 4,
        out_specs=[vmem()] * 2,
        out_shape=[out((frames * bands * tile, LANES)), out((1, width), F32)],
        scratch_shapes=[
            pltpu.VMEM((rows * cols, width), BF16),
            pltpu.VMEM((8, width), F32),
            pltpu.VMEM((tokens, cwidth), BF16),
            pltpu.VMEM((tokens, 2 * cwidth), BF16),
            pltpu.SemaphoreType.DMA((4,)),
        ],
        compiler_params=params(),
    )(
        timesteps,
        in_hbm(cotangent.reshape(rows * cols, width)),
        in_hbm(gain_table),
        in_hbm(coarse_q.reshape(tokens, cwidth)),
        in_hbm(coarse_kv.reshape(tokens, 2 * cwidth)),
    )
    held = lax.all_to_all(
        sent.reshape(frames * bands, tile, LANES),
        ("frames", "rows"),
        split_axis=0,
        concat_axis=0,
        tiled=True,
    ).reshape(frames * bands * tile, LANES)
    count = frames * bands * tokens
    *outs, after = pl.pallas_call(
        functools.partial(coarse_kernel, frames, tokens),
        in_specs=[smem(), vmem()],
        out_specs=[vmem()] * 4,
        out_shape=[out((frames, tokens, head_width))] * 3 + [out((8, LANES), F32)],
        scratch_shapes=[
            pltpu.VMEM(held.shape, F32),
            pltpu.VMEM((head_width // LANES, count, 2 * count), F32),
            pltpu.VMEM((head_width // LANES, count, 2 * count), F32),
        ],
        compiler_params=params(),
        cost_estimate=pl.CostEstimate(flops=100_000_000_000, bytes_accessed=100_000_000, transcendentals=0),
    )(valid_cols, held)
    return tuple(x.reshape(frames, 1, tokens, head_width) for x in outs), gain, after


def normalize(scores):
    row_max = jnp.max(scores, axis=-1, keepdims=True)
    return row_max + jnp.log(jnp.sum(jnp.exp(scores - row_max), axis=-1, keepdims=True))


def coarse_gathered(coarse_q, coarse_kv, cotangent, gain_table, timesteps, valid_cols):
    score_scale = 1.0 / math.sqrt(HD)
    frames_here, _, cols_here, fine_width = cotangent.shape
    total_frames = valid_cols.shape[0]
    steps_all = gain_table.shape[0]
    select = (timesteps[:, None] == jnp.arange(steps_all)[None, :]).astype(F32)
    frame_gain = jnp.dot(select, gain_table, precision=lax.Precision.HIGHEST)
    scaled_grad = frame_gain[:, None, None, :] * cotangent.astype(F32)
    half_pool = POOL // 2
    coarse_cols = cols_here // POOL
    coarse_width = coarse_q.shape[-1]
    coarse_count = frames_here * coarse_cols
    blocks = scaled_grad.reshape(frames_here, 2, half_pool, coarse_cols, 2, half_pool, fine_width)
    pooled = (
        jnp.sum(blocks, axis=(2, 5))
        .transpose(0, 2, 1, 3, 4)
        .reshape(coarse_count, coarse_width)
        .astype(BF16)
    )
    mine_query = coarse_q.reshape(coarse_count, coarse_width)
    mine_keys = coarse_kv[..., :coarse_width].reshape(coarse_count, coarse_width)
    mine_values = coarse_kv[..., coarse_width:].reshape(coarse_count, coarse_width)
    head_query, head_keys, head_values, head_grad = (
        lax.all_to_all(mine_query, "frames", split_axis=1, concat_axis=0, tiled=True),
        lax.all_to_all(mine_keys, "frames", split_axis=1, concat_axis=0, tiled=True),
        lax.all_to_all(mine_values, "frames", split_axis=1, concat_axis=0, tiled=True),
        lax.all_to_all(pooled, "frames", split_axis=1, concat_axis=0, tiled=True),
    )
    head_tokens, head_width = head_query.shape
    head_groups = head_width // HD
    query_heads = head_query.reshape(head_tokens, head_groups, HD)
    grad_heads = head_grad.reshape(head_tokens, head_groups, HD)
    every_keys, every_values = (
        lax.all_gather(head_keys, "rows", axis=0, tiled=True),
        lax.all_gather(head_values, "rows", axis=0, tiled=True),
    )
    every_count = every_keys.shape[0]
    key_heads = every_keys.reshape(every_count, head_groups, HD)
    value_heads = every_values.reshape(every_count, head_groups, HD)
    position = jnp.arange(every_count) % head_tokens
    key_frame = position // coarse_cols
    key_column = position % coarse_cols
    col_limit = jnp.sum(
        jnp.where(key_frame[:, None] == jnp.arange(total_frames)[None, :], valid_cols[None, :], 0),
        axis=1,
    )
    key_ok = key_column * POOL < col_limit
    coarse_scores = (
        jnp.einsum("qhd,khd->hqk", query_heads, key_heads, preferred_element_type=F32)
        * score_scale
    )
    coarse_scores = jnp.where(key_ok[None, None, :], coarse_scores, NEGATIVE)
    log_total = normalize(coarse_scores)
    coarse_weights = jnp.exp(coarse_scores - log_total)
    coarse_low = coarse_weights.astype(BF16)
    coarse_out = jnp.einsum("hqk,khd->qhd", coarse_low, value_heads, preferred_element_type=F32)
    coarse_dot = jnp.sum(grad_heads.astype(F32) * coarse_out, axis=-1)
    coarse_wgrad = jnp.einsum("qhd,khd->hqk", grad_heads, value_heads, preferred_element_type=F32)
    coarse_sgrad = (coarse_weights * (coarse_wgrad - coarse_dot.T[:, :, None])).astype(BF16)
    coarse_qgrad = (
        jnp.einsum("hqk,khd->qhd", coarse_sgrad, key_heads, preferred_element_type=F32)
        * score_scale
    )
    count = head_tokens * lax.axis_size("rows")
    key_part = (
        jnp.einsum("hqk,qhd->khd", coarse_sgrad, query_heads, preferred_element_type=F32)
        * score_scale
    )
    value_part = jnp.einsum("hqk,qhd->khd", coarse_low, grad_heads, preferred_element_type=F32)
    terms = lax.psum_scatter(
        jnp.concatenate(
            [key_part.reshape(count, head_width), value_part.reshape(count, head_width)], axis=1
        ),
        "rows",
        scatter_dimension=0,
        tiled=True,
    )
    total_keys = terms[:, :head_width]
    total_values = terms[:, head_width:]
    out_dims = (head_tokens // coarse_cols, 1, coarse_cols, head_width)
    return (
        coarse_qgrad.reshape(out_dims).astype(BF16),
        total_keys.reshape(out_dims).astype(BF16),
        total_values.reshape(out_dims).astype(BF16),
    ), frame_gain, jnp.zeros((8, LANES), F32)


def local(fine_q, fine_kv, coarse_q, coarse_kv, cotangent, gain_table, timesteps, valid_cols):
    frames, bands = lax.axis_size("frames"), lax.axis_size("rows")
    head_width = coarse_q.shape[-1] // frames
    tokens = coarse_q.shape[-2]
    direct = (
        head_width == cotangent.shape[-1]
        and 4 * tokens * head_width // LANES == 16
        and frames * bands * tokens <= 128
    )
    coarse = coarse_direct if direct else coarse_gathered
    coarse_grads, gain, after = coarse(
        coarse_q, coarse_kv, cotangent, gain_table, timesteps, valid_cols
    )
    fine_grads = fine_level(after, gain, fine_q, fine_kv, cotangent, valid_cols)
    return fine_grads + coarse_grads


def solution(mesh):
    placed = (
        P("frames", "rows", None, None),
        P("frames", "rows", None, None),
        P("frames", "rows", None, None),
        P("frames", "rows", None, None),
        P("frames", "rows", None, None),
        P(),
        P("frames"),
        P(),
    )
    return jax.shard_map(
        local,
        mesh=mesh,
        in_specs=placed,
        out_specs=(
            P("frames", "rows", None, None),
            P("frames", "rows", None, None),
            P(None, "rows", None, "frames"),
            P(None, "rows", None, "frames"),
            P(None, "rows", None, "frames"),
        ),
        check_vma=False,
    )
```

```python
import functools
import math

import jax
import jax.numpy as jnp
from jax import lax
from jax.experimental import pallas as pl
from jax.experimental.pallas import tpu as pltpu
from jax.sharding import PartitionSpec as P

HD = 64
KERNEL = 7
POOL = 8
LANES = 128

NEGATIVE = -1e30

F32 = jnp.float32
BF16 = jnp.bfloat16


def dot_nt(left, right):
    return lax.dot_general(left, right, (((1,), (1,)), ((), ())), preferred_element_type=F32)


def dot_nn(left, right):
    return jnp.dot(left, right, preferred_element_type=F32)


def iota(shape, dim):
    return lax.broadcasted_iota(jnp.int32, shape, dim)


def pairs_of(table):
    blocks = []
    for lo in range(0, table.shape[1], LANES):
        part = table[:, lo : lo + LANES]
        first = iota(part.shape, 1) < HD
        zero = jnp.zeros_like(part)
        blocks.append(
            jnp.concatenate([jnp.where(first, part, zero), jnp.where(first, zero, part)], axis=0)
        )
    return blocks


def softmax_grads(scores, weight_grad, axis):
    top = jnp.max(scores, axis=axis, keepdims=True)
    raised = jnp.exp(scores - top)
    share = 1.0 / jnp.sum(raised, axis=axis, keepdims=True)
    row_dot = jnp.sum(raised * weight_grad, axis=axis, keepdims=True) * share
    weights = raised * share
    return weights.astype(BF16), (weights * (weight_grad - row_dot)).astype(BF16)


def send_kernel(
    cols, bands, step_ref, cot_hbm, gain_hbm, cq_hbm, ckv_hbm,
    send_ref, gain_ref, cot_ref, eight_ref, cq_ref, ckv_ref, sems,
):
    step = step_ref[0]
    eight = eight_ref.shape[0]
    first = pl.multiple_of(step // eight * eight, eight)
    gain_copy = pltpu.make_async_copy(gain_hbm.at[pl.ds(first, eight)], eight_ref, sems.at[0])
    gain_copy.start()
    copies = [
        pltpu.make_async_copy(source, target, sems.at[1 + at])
        for at, (source, target) in enumerate(
            tuple((cot_hbm.at[pl.ds(r, 32)], cot_ref.at[pl.ds(r, 32)]) for r in range(0, 128, 32)) + ((cq_hbm, cq_ref), (ckv_hbm, ckv_ref))
        )
    ]
    for copy in copies:
        copy.start()
    pixels, width = cot_ref.shape
    tokens, cwidth = cq_ref.shape
    half = POOL // 2
    groups = cwidth // width
    part = iota((groups * tokens, pixels), 0)
    group, token = part // tokens, part % tokens
    pixel = iota((groups * tokens, pixels), 1)
    row, col = pixel // cols, pixel % cols
    inside = (row // half == group // 2) & (col // half == token * 2 + group % 2)
    for copy in copies:
        copy.wait()
    summed = dot_nn(inside.astype(BF16), cot_ref[...])
    query = cq_ref[...].astype(F32)
    both = ckv_ref[...].astype(F32)
    gain_copy.wait()
    gain = eight_ref[pl.ds(step - first, 1), :]
    gain_ref[...] = gain
    pooled = summed * gain
    for g in range(groups):
        lo = g * width
        arrays = (
            query[:, lo : lo + width],
            both[:, lo : lo + width],
            both[:, cwidth + lo : cwidth + lo + width],
            pooled[g * tokens : (g + 1) * tokens, :],
        )
        tile = jnp.concatenate(
            [a[:, b : b + LANES] for a in arrays for b in range(0, width, LANES)], axis=0
        ).astype(BF16)
        height = tile.shape[0]
        for r in range(bands):
            start = (g * bands + r) * height
            send_ref[start : start + height, :] = tile


def prep_kernel(cols, gain_ref, q_ref, kv_ref, cot_ref, near_ref, far_ref, grad_ref):
    radius = KERNEL // 2
    pixels, width = q_ref.shape
    one, two = radius * cols, 2 * radius * cols
    even = lax.axis_index("rows") % 2 == 0
    grad_ref[...] = (gain_ref[...] * cot_ref[...].astype(F32)).astype(BF16)

    def pack(target, top):
        lo_one, lo_two = (0, 0) if top else (pixels - one, pixels - two)
        target[:two, :] = kv_ref[lo_two : lo_two + two, :]
        target[two:, :width] = q_ref[lo_one : lo_one + one, :]
        target[two:, width:] = grad_ref[lo_one : lo_one + one, :]

    @pl.when(even)
    def _():
        pack(near_ref, False)
        pack(far_ref, True)

    @pl.when(jnp.logical_not(even))
    def _():
        pack(near_ref, True)
        pack(far_ref, False)


def plan_kernel(
    cols, valid_ref, q_ref, kv_ref, grad_ref,
    own_ref, above_ref, below_ref, queries_ref, grads_ref, keys_t_ref,
):
    radius = KERNEL // 2
    pixels, width = q_ref.shape
    rows = pixels // cols
    scale = 1.0 / math.sqrt(HD)
    band, frame = lax.axis_index("rows"), lax.axis_index("frames")
    first, last = band == 0, band == lax.axis_size("rows") - 1
    valid = sum(
        jnp.where(frame == f, valid_ref[:, f : f + 1], 0) for f in range(valid_ref.shape[1])
    )

    def bias(ref, key_row, lane_rows, query_row):
        place = iota(ref.shape, 0)
        krow, kcol = key_row(place // cols), place % cols
        lane = iota(ref.shape, 1)
        qrow, qcol = lane // cols % lane_rows + query_row, lane % cols
        seen = (jnp.abs(krow - qrow) <= radius) & (jnp.abs(kcol - qcol) <= radius) & (kcol < valid)
        seen = seen & ((krow >= 0) | jnp.logical_not(first))
        seen = seen & ((krow < rows) | jnp.logical_not(last))
        seen = seen | ((krow == qrow) & (kcol == qcol))
        ref[...] = jnp.where(seen, 0.0, NEGATIVE)

    def own_row(at):
        above = at - rows - radius
        return jnp.where(at < rows, at, jnp.where(above < 0, above, above + rows))

    bias(own_ref, own_row, rows, 0)
    bias(above_ref, lambda at: jnp.where(at < radius, at, at - 3 * radius), radius + 1, -radius)
    bias(below_ref, lambda at: at + rows - radius, radius + 1, rows)
    queries_ref[...] = jnp.concatenate(pairs_of(q_ref[...] * scale), axis=0)
    grads_ref[...] = jnp.concatenate(pairs_of(grad_ref[...]), axis=0)
    keys_t_ref[...] = kv_ref[:, :width].T


def fine_kernel(cols, carried, *refs):
    (kv_ref, near_ref, far_ref, own_ref, above_ref, below_ref, queries_ref, grads_ref, keys_t_ref) = refs[:9]
    outs = refs[9 + carried : 11 + 2 * carried]
    dq_ref, dkv_ref, sems = refs[11 + 2 * carried :]
    copies = [
        pltpu.make_async_copy(source, target, sems.at[2 + at])
        for at, (source, target) in enumerate(zip(refs[9 : 9 + carried], outs[2:]))
    ]
    for copy in copies:
        copy.start()
    radius = KERNEL // 2
    pixels, width = dq_ref.shape
    one, two = radius * cols, 2 * radius * cols
    scale = 1.0 / math.sqrt(HD)
    even = lax.axis_index("rows") % 2 == 0

    def received(rows_at, cols_at):
        near, far = near_ref[rows_at, cols_at], far_ref[rows_at, cols_at]
        return jnp.where(even, far, near), jnp.where(even, near, far)

    def joined(table):
        return jnp.concatenate(table, axis=0)

    k_above, k_below = received(slice(0, two), slice(0, width))
    v_above, v_below = received(slice(0, two), slice(width, 2 * width))
    q_above, q_below = received(slice(two, two + one), slice(0, width))
    g_above, g_below = received(slice(two, two + one), slice(width, 2 * width))
    keys, values = kv_ref[:, :width], kv_ref[:, width:]
    own_keys = joined([keys, k_above[one:], k_below[:one]])
    own_values = joined([values, v_above[one:], v_below[:one]])
    keys_t = jnp.concatenate([keys_t_ref[...], joined([k_above[one:], k_below[:one]]).T], axis=1)
    pad = jnp.zeros((cols, width), BF16)
    sides = [
        (
            joined([keys[:one], k_above]),
            joined([values[:one], v_above]),
            pairs_of(joined([q_above * scale, pad])),
            pairs_of(joined([g_above, pad])),
            above_ref,
        ),
        (
            joined([keys[pixels - one :], k_below]),
            joined([values[pixels - one :], v_below]),
            pairs_of(joined([q_below * scale, pad])),
            pairs_of(joined([g_below, pad])),
            below_ref,
        ),
    ]
    rest = jnp.zeros((pixels - one, LANES), BF16)
    stack = 2 * pixels
    own_bias = jnp.concatenate([own_ref[...], own_ref[...]], axis=1)
    for p in range(width // LANES):
        at = slice(p * LANES, (p + 1) * LANES)
        query, grad = (ref[p * stack : (p + 1) * stack] for ref in (queries_ref, grads_ref))
        low, sgrad = softmax_grads(
            dot_nt(own_keys[:, at], query) + own_bias, dot_nt(own_values[:, at], grad), 0
        )
        dq_t = dot_nn(keys_t[at], sgrad)
        dq_t = joined([dq_t[:HD, :pixels], dq_t[HD:, pixels:]])
        dq_ref[:, at] = (dq_t * scale).T.astype(BF16)
        lows, sgrads, all_queries, all_grads = [low[:pixels]], [sgrad[:pixels]], [query], [grad]
        for side, (side_keys, side_values, side_query, side_grad, side_bias) in enumerate(sides):
            low, sgrad = softmax_grads(
                dot_nt(side_keys[:, at], side_query[p]) + side_bias[...],
                dot_nt(side_values[:, at], side_grad[p]),
                0,
            )
            order = slice(None, None, -1 if side else 1)
            lows.append(joined([low[:one], rest][order]))
            sgrads.append(joined([sgrad[:one], rest][order]))
            all_queries.append(side_query[p])
            all_grads.append(side_grad[p])
        dkv_ref[:, at] = dot_nn(jnp.concatenate(sgrads, axis=1), joined(all_queries)).astype(BF16)
        dkv_ref[:, width + p * LANES : width + (p + 1) * LANES] = dot_nn(
            jnp.concatenate(lows, axis=1), joined(all_grads)
        ).astype(BF16)
    copies += [
        pltpu.make_async_copy(source, target, sems.at[at])
        for at, (source, target) in enumerate(((dq_ref, outs[0]), (dkv_ref, outs[1])))
    ]
    for copy in copies[carried:]:
        copy.start()
    for copy in copies:
        copy.wait()


def coarse_kernel(frames, tokens, valid_ref, x_ref, dq_ref, dk_ref, dv_ref, wide, low_ref, sg_ref):
    bands = lax.axis_size("rows")
    width = dq_ref.shape[-1]
    parts = width // LANES
    height = x_ref.shape[0] // (frames * bands)
    band = lax.axis_index("rows")
    scale = 1.0 / math.sqrt(HD)
    wide[...] = x_ref[...].astype(F32)
    devices, own = frames * bands, frames * tokens

    def every(array, b):
        first = (array * parts + b) * tokens
        return jnp.concatenate(
            [wide[pl.ds(first + t, devices, stride=height), :] for t in range(tokens)], axis=0
        ).astype(BF16)

    def mine(array, b):
        first = band * height + (array * parts + b) * tokens
        return jnp.concatenate(
            [wide[pl.ds(first + f * bands * height, tokens), :] for f in range(frames)], axis=0
        ).astype(BF16)

    count = devices * tokens

    def key_bias(shape, dim):
        place = iota(shape, dim)
        token, frame = place // devices, place // bands % frames
        limit = jnp.zeros(shape, jnp.int32)
        for f in range(frames):
            limit = jnp.where(frame == f, valid_ref[:, f : f + 1], limit)
        return jnp.where(token * POOL < limit, 0.0, NEGATIVE)

    bias, own_bias = key_bias((count, 2 * count), 0), key_bias((2 * own, count), 1)
    for b in range(parts):
        at = slice(b * LANES, (b + 1) * LANES)
        key, value = every(1, b), every(2, b)
        (query,), (grad,) = pairs_of(every(0, b) * scale), pairs_of(every(3, b))
        low, sgrad = softmax_grads(dot_nt(key, query) + bias, dot_nt(value, grad), 0)
        low_ref[b] = low.astype(F32)
        sg_ref[b] = sgrad.astype(F32)

        def mine_rows(ref):
            pieces = [
                ref[b, pl.ds(t * devices + f * bands + band, 1), :]
                for f in range(frames)
                for t in range(tokens)
            ]
            return jnp.concatenate(pieces, axis=0).astype(BF16)

        (own_query,), (own_grad,) = pairs_of(mine(0, b) * scale), pairs_of(mine(3, b))
        _, own_sgrad = softmax_grads(
            dot_nt(own_query, key) + own_bias, dot_nt(own_grad, value), 1
        )
        full = dot_nn(own_sgrad, key)
        dq = jnp.where(iota((own, LANES), 1) < HD, full[:own], full[own:]) * scale
        dk = dot_nn(mine_rows(sg_ref), query)
        dv = dot_nn(mine_rows(low_ref), grad)
        for ref, table in ((dq_ref, dq), (dk_ref, dk), (dv_ref, dv)):
            rounded = table.astype(BF16)
            for f in range(frames):
                ref[f, :, at] = rounded[f * tokens : (f + 1) * tokens]


def vmem():
    return pl.BlockSpec(memory_space=pltpu.VMEM)


def smem():
    return pl.BlockSpec(memory_space=pltpu.SMEM)


def hbm():
    return pl.BlockSpec(memory_space=pltpu.HBM)


def in_hbm(array):
    return pltpu.with_memory_space_constraint(array, pltpu.HBM)


def params():
    return pltpu.CompilerParams(vmem_limit_bytes=16 * 2**20)


def out(shape, dtype=BF16):
    return jax.ShapeDtypeStruct(shape, dtype)


def fine_level(carried, gain, fine_q, fine_kv, cotangent, valid_cols):
    bands = lax.axis_size("rows")
    _, rows, cols, width = fine_q.shape
    pixels = rows * cols
    radius = KERNEL // 2
    query = fine_q.reshape(pixels, width)
    key_value = fine_kv.reshape(pixels, 2 * width)
    cot = cotangent.reshape(pixels, width)
    packed = (3 * radius * cols, 2 * width)
    near, far, grad = pl.pallas_call(
        functools.partial(prep_kernel, cols),
        in_specs=[vmem()] * 4,
        out_specs=[vmem()] * 3,
        out_shape=[out(packed), out(packed), out((pixels, width))],
        compiler_params=params(),
    )(gain, query, key_value, cot)
    pairs = [(i, i ^ 1) for i in range(bands) if i ^ 1 < bands]
    others = [(i, ((i + 1) ^ 1) - 1) for i in range(1, bands) if ((i + 1) ^ 1) - 1 < bands]
    near = lax.ppermute(near, "rows", pairs)
    far = lax.ppermute(far, "rows", others)
    outside = (3 * radius * cols, 2 * (radius + 1) * cols)
    stacked = (2 * width // LANES * pixels, LANES)
    plan = pl.pallas_call(
        functools.partial(plan_kernel, cols),
        in_specs=[vmem()] * 4,
        out_specs=[vmem()] * 6,
        out_shape=[
            out((pixels + 2 * radius * cols, pixels), F32),
            out(outside, F32),
            out(outside, F32),
            out(stacked),
            out(stacked),
            out((width, pixels)),
        ],
        compiler_params=params(),
    )(valid_cols.reshape(1, -1), query, key_value, grad)
    grads = pl.pallas_call(
        functools.partial(fine_kernel, cols, len(carried)),
        in_specs=[vmem()] * (9 + len(carried)),
        out_specs=[hbm()] * (2 + len(carried)),
        out_shape=[out((pixels, width)), out((pixels, 2 * width))]
        + [out(x.shape) for x in carried],
        scratch_shapes=[
            pltpu.VMEM((pixels, width), BF16),
            pltpu.VMEM((pixels, 2 * width), BF16),
            pltpu.SemaphoreType.DMA((2 + len(carried),)),
        ],
        compiler_params=params(),
        cost_estimate=pl.CostEstimate(flops=400_000_000, bytes_accessed=1_000_000, transcendentals=300_000),
    )(key_value, near, far, *plan, *carried)
    return (grads[0].reshape(fine_q.shape), grads[1].reshape(fine_kv.shape), *grads[2:])


def coarse_direct(coarse_q, coarse_kv, cotangent, gain_table, timesteps, valid_cols):
    frames, bands = lax.axis_size("frames"), lax.axis_size("rows")
    _, rows, cols, width = cotangent.shape
    tokens, cwidth = coarse_q.shape[-2:]
    head_width = cwidth // frames
    tile = 4 * tokens * head_width // LANES
    sent, gain = pl.pallas_call(
        functools.partial(send_kernel, cols, bands),
        in_specs=[smem()] + [hbm()] * 4,
        out_specs=[vmem()] * 2,
        out_shape=[out((frames * bands * tile, LANES)), out((1, width), F32)],
        scratch_shapes=[
            pltpu.VMEM((rows * cols, width), BF16),
            pltpu.VMEM((8, width), F32),
            pltpu.VMEM((tokens, cwidth), BF16),
            pltpu.VMEM((tokens, 2 * cwidth), BF16),
            pltpu.SemaphoreType.DMA((7,)),
        ],
        compiler_params=params(),
    )(
        timesteps,
        in_hbm(cotangent.reshape(rows * cols, width)),
        in_hbm(gain_table),
        in_hbm(coarse_q.reshape(tokens, cwidth)),
        in_hbm(coarse_kv.reshape(tokens, 2 * cwidth)),
    )
    held = lax.all_to_all(
        sent.reshape(frames * bands, tile, LANES),
        ("frames", "rows"),
        split_axis=0,
        concat_axis=0,
        tiled=True,
    ).reshape(frames * bands * tile, LANES)
    count = frames * bands * tokens
    outs = pl.pallas_call(
        functools.partial(coarse_kernel, frames, tokens),
        in_specs=[vmem()] * 2,
        out_specs=[vmem()] * 3,
        out_shape=[out((frames, tokens, head_width))] * 3,
        scratch_shapes=[
            pltpu.VMEM(held.shape, F32),
            pltpu.VMEM((head_width // LANES, count, 2 * count), F32),
            pltpu.VMEM((head_width // LANES, count, 2 * count), F32),
        ],
        compiler_params=params(),
        cost_estimate=pl.CostEstimate(flops=100_000_000_000, bytes_accessed=100_000_000, transcendentals=0),
    )(valid_cols.reshape(1, -1), held)
    return outs, gain


def normalize(scores):
    row_max = jnp.max(scores, axis=-1, keepdims=True)
    return row_max + jnp.log(jnp.sum(jnp.exp(scores - row_max), axis=-1, keepdims=True))


def coarse_gathered(coarse_q, coarse_kv, cotangent, gain_table, timesteps, valid_cols):
    score_scale = 1.0 / math.sqrt(HD)
    frames_here, _, cols_here, fine_width = cotangent.shape
    total_frames = valid_cols.shape[0]
    steps_all = gain_table.shape[0]
    select = (timesteps[:, None] == jnp.arange(steps_all)[None, :]).astype(F32)
    frame_gain = jnp.dot(select, gain_table, precision=lax.Precision.HIGHEST)
    scaled_grad = frame_gain[:, None, None, :] * cotangent.astype(F32)
    half_pool = POOL // 2
    coarse_cols = cols_here // POOL
    coarse_width = coarse_q.shape[-1]
    coarse_count = frames_here * coarse_cols
    blocks = scaled_grad.reshape(frames_here, 2, half_pool, coarse_cols, 2, half_pool, fine_width)
    pooled = (
        jnp.sum(blocks, axis=(2, 5))
        .transpose(0, 2, 1, 3, 4)
        .reshape(coarse_count, coarse_width)
        .astype(BF16)
    )
    mine_query = coarse_q.reshape(coarse_count, coarse_width)
    mine_keys = coarse_kv[..., :coarse_width].reshape(coarse_count, coarse_width)
    mine_values = coarse_kv[..., coarse_width:].reshape(coarse_count, coarse_width)
    head_query, head_keys, head_values, head_grad = (
        lax.all_to_all(mine_query, "frames", split_axis=1, concat_axis=0, tiled=True),
        lax.all_to_all(mine_keys, "frames", split_axis=1, concat_axis=0, tiled=True),
        lax.all_to_all(mine_values, "frames", split_axis=1, concat_axis=0, tiled=True),
        lax.all_to_all(pooled, "frames", split_axis=1, concat_axis=0, tiled=True),
    )
    head_tokens, head_width = head_query.shape
    head_groups = head_width // HD
    query_heads = head_query.reshape(head_tokens, head_groups, HD)
    grad_heads = head_grad.reshape(head_tokens, head_groups, HD)
    every_keys, every_values = (
        lax.all_gather(head_keys, "rows", axis=0, tiled=True),
        lax.all_gather(head_values, "rows", axis=0, tiled=True),
    )
    every_count = every_keys.shape[0]
    key_heads = every_keys.reshape(every_count, head_groups, HD)
    value_heads = every_values.reshape(every_count, head_groups, HD)
    position = jnp.arange(every_count) % head_tokens
    key_frame = position // coarse_cols
    key_column = position % coarse_cols
    col_limit = jnp.sum(
        jnp.where(key_frame[:, None] == jnp.arange(total_frames)[None, :], valid_cols[None, :], 0),
        axis=1,
    )
    key_ok = key_column * POOL < col_limit
    coarse_scores = (
        jnp.einsum("qhd,khd->hqk", query_heads, key_heads, preferred_element_type=F32)
        * score_scale
    )
    coarse_scores = jnp.where(key_ok[None, None, :], coarse_scores, NEGATIVE)
    log_total = normalize(coarse_scores)
    coarse_weights = jnp.exp(coarse_scores - log_total)
    coarse_low = coarse_weights.astype(BF16)
    coarse_out = jnp.einsum("hqk,khd->qhd", coarse_low, value_heads, preferred_element_type=F32)
    coarse_dot = jnp.sum(grad_heads.astype(F32) * coarse_out, axis=-1)
    coarse_wgrad = jnp.einsum("qhd,khd->hqk", grad_heads, value_heads, preferred_element_type=F32)
    coarse_sgrad = (coarse_weights * (coarse_wgrad - coarse_dot.T[:, :, None])).astype(BF16)
    coarse_qgrad = (
        jnp.einsum("hqk,khd->qhd", coarse_sgrad, key_heads, preferred_element_type=F32)
        * score_scale
    )
    count = head_tokens * lax.axis_size("rows")
    key_part = (
        jnp.einsum("hqk,qhd->khd", coarse_sgrad, query_heads, preferred_element_type=F32)
        * score_scale
    )
    value_part = jnp.einsum("hqk,qhd->khd", coarse_low, grad_heads, preferred_element_type=F32)
    terms = lax.psum_scatter(
        jnp.concatenate(
            [key_part.reshape(count, head_width), value_part.reshape(count, head_width)], axis=1
        ),
        "rows",
        scatter_dimension=0,
        tiled=True,
    )
    total_keys = terms[:, :head_width]
    total_values = terms[:, head_width:]
    out_dims = (head_tokens // coarse_cols, 1, coarse_cols, head_width)
    return (
        coarse_qgrad.reshape(out_dims).astype(BF16),
        total_keys.reshape(out_dims).astype(BF16),
        total_values.reshape(out_dims).astype(BF16),
    ), frame_gain


def local(fine_q, fine_kv, coarse_q, coarse_kv, cotangent, gain_table, timesteps, valid_cols):
    frames, bands = lax.axis_size("frames"), lax.axis_size("rows")
    head_width = coarse_q.shape[-1] // frames
    tokens = coarse_q.shape[-2]
    direct = (
        head_width == cotangent.shape[-1]
        and 4 * tokens * head_width // LANES == 16
        and frames * bands * tokens <= 128
    )
    operands = (coarse_q, coarse_kv, cotangent, gain_table, timesteps, valid_cols)
    fine = (fine_q, fine_kv, cotangent, valid_cols)
    if direct:
        carried, gain = coarse_direct(*operands)
        grad_q, grad_kv, *coarse_grads = fine_level(carried, gain, *fine)
        shape = (frames, 1, tokens, head_width)
        return (grad_q, grad_kv, *(x.reshape(shape) for x in coarse_grads))
    coarse_grads, gain = coarse_gathered(*operands)
    return (*fine_level([], gain, *fine), *coarse_grads)


def solution(mesh):
    placed = (
        P("frames", "rows", None, None),
        P("frames", "rows", None, None),
        P("frames", "rows", None, None),
        P("frames", "rows", None, None),
        P("frames", "rows", None, None),
        P(),
        P("frames"),
        P(),
    )
    return jax.shard_map(
        local,
        mesh=mesh,
        in_specs=placed,
        out_specs=(
            P("frames", "rows", None, None),
            P("frames", "rows", None, None),
            P(None, "rows", None, "frames"),
            P(None, "rows", None, "frames"),
            P(None, "rows", None, "frames"),
        ),
        check_vma=False,
    )
```

```python
import functools
import math

import jax
import jax.numpy as jnp
from jax import lax
from jax.experimental import pallas as pl
from jax.experimental.pallas import tpu as pltpu
from jax.sharding import PartitionSpec as P

HD = 64
KERNEL = 7
POOL = 8
LANES = 128

NEGATIVE = -1e30

F32 = jnp.float32
BF16 = jnp.bfloat16


def dot_nt(left, right):
    return lax.dot_general(left, right, (((1,), (1,)), ((), ())), preferred_element_type=F32)


def dot_nn(left, right):
    return jnp.dot(left, right, preferred_element_type=F32)


def iota(shape, dim):
    return lax.broadcasted_iota(jnp.int32, shape, dim)


def pairs_of(table):
    blocks = []
    for lo in range(0, table.shape[1], LANES):
        part = table[:, lo : lo + LANES]
        first = iota(part.shape, 1) < HD
        zero = jnp.zeros_like(part)
        blocks.append(
            jnp.concatenate([jnp.where(first, part, zero), jnp.where(first, zero, part)], axis=0)
        )
    return blocks


def softmax_grads(scores, weight_grad, axis):
    top = jnp.max(scores, axis=axis, keepdims=True)
    raised = jnp.exp(scores - top)
    share = 1.0 / jnp.sum(raised, axis=axis, keepdims=True)
    row_dot = jnp.sum(raised * weight_grad, axis=axis, keepdims=True) * share
    weights = raised * share
    return weights.astype(BF16), (weights * (weight_grad - row_dot)).astype(BF16)


def send_kernel(
    cols, bands, step_ref, valid_hbm, cot_hbm, gain_hbm, cq_hbm, ckv_hbm,
    send_ref, gain_ref, valid_ref, cot_ref, eight_ref, cq_ref, ckv_ref, sems,
):
    step = step_ref[0]
    eight = eight_ref.shape[0]
    first = pl.multiple_of(step // eight * eight, eight)
    gain_copy = pltpu.make_async_copy(gain_hbm.at[pl.ds(first, eight)], eight_ref, sems.at[0])
    gain_copy.start()
    copies = [
        pltpu.make_async_copy(source, target, sems.at[1 + at])
        for at, (source, target) in enumerate(
            tuple((cot_hbm.at[pl.ds(r, 32)], cot_ref.at[pl.ds(r, 32)]) for r in range(0, 128, 32)) + ((cq_hbm, cq_ref), (ckv_hbm, ckv_ref), (valid_hbm, valid_ref))
        )
    ]
    for copy in copies:
        copy.start()
    pixels, width = cot_ref.shape
    tokens, cwidth = cq_ref.shape
    half = POOL // 2
    groups = cwidth // width
    part = iota((groups * tokens, pixels), 0)
    group, token = part // tokens, part % tokens
    pixel = iota((groups * tokens, pixels), 1)
    row, col = pixel // cols, pixel % cols
    inside = (row // half == group // 2) & (col // half == token * 2 + group % 2)
    for copy in copies:
        copy.wait()
    summed = dot_nn(inside.astype(BF16), cot_ref[...])
    query = cq_ref[...].astype(F32)
    both = ckv_ref[...].astype(F32)
    gain_copy.wait()
    gain = eight_ref[pl.ds(step - first, 1), :]
    gain_ref[...] = gain
    pooled = summed * gain
    for g in range(groups):
        lo = g * width
        arrays = (
            query[:, lo : lo + width],
            both[:, lo : lo + width],
            both[:, cwidth + lo : cwidth + lo + width],
            pooled[g * tokens : (g + 1) * tokens, :],
        )
        tile = jnp.concatenate(
            [a[:, b : b + LANES] for a in arrays for b in range(0, width, LANES)], axis=0
        ).astype(BF16)
        height = tile.shape[0]
        for r in range(bands):
            start = (g * bands + r) * height
            send_ref[start : start + height, :] = tile


def valid_here(valid_ref):
    frame = lax.axis_index("frames")
    return sum(
        jnp.where(frame == f, valid_ref[:, f : f + 1], 0) for f in range(valid_ref.shape[1])
    )


def window_bias(shape, cols, valid, key_row, lane_rows, query_row, present=None):
    radius = KERNEL // 2
    place, lane = iota(shape, 0), iota(shape, 1)
    krow, kcol = key_row(place // cols), place % cols
    qrow, qcol = lane // cols % lane_rows + query_row, lane % cols
    seen = (jnp.abs(krow - qrow) <= radius) & (jnp.abs(kcol - qcol) <= radius) & (kcol < valid)
    if present is not None:
        seen = seen & present(krow)
    seen = seen | ((krow == qrow) & (kcol == qcol))
    return jnp.where(seen, 0.0, NEGATIVE)


def partial_sums(scores, weight_grad):
    top = jnp.max(scores, axis=0, keepdims=True)
    raised = jnp.exp(scores - top)
    total = jnp.sum(raised, axis=0, keepdims=True)
    return top, raised, total, jnp.sum(raised * weight_grad, axis=0, keepdims=True)


def completed(kept, scores, weight_grad):
    top_kept, total_kept, dot_kept = kept
    top = jnp.maximum(top_kept, jnp.max(scores, axis=0, keepdims=True))
    factor = jnp.exp(top_kept - top)
    raised = jnp.exp(scores - top)
    total = total_kept * factor + jnp.sum(raised, axis=0, keepdims=True)
    share = jnp.where(total > 0, 1.0 / total, 0.0)
    dot = dot_kept * factor + jnp.sum(raised * weight_grad, axis=0, keepdims=True)
    return factor * share, raised * share, dot * share


def in_parts(row):
    parts = []
    for _ in range(3):
        part = row.astype(BF16).astype(F32)
        parts.append(part)
        row = row - part
    return parts


def prep_kernel(cols, valid_ref, gain_ref, q_ref, kv_ref, cot_ref, near_ref, far_ref, grad_ref):
    radius = KERNEL // 2
    pixels, width = q_ref.shape
    rows = pixels // cols
    one, two = radius * cols, 2 * radius * cols
    scale = 1.0 / math.sqrt(HD)
    even = lax.axis_index("rows") % 2 == 0
    valid = valid_here(valid_ref)
    grad_ref[...] = (gain_ref[...] * cot_ref[...].astype(F32)).astype(BF16)
    pad = jnp.zeros((cols, width), BF16)

    sides = []
    for lo, key_lo, query_row in ((0, 0, 0), (pixels - one, pixels - two, radius)):
        bias = window_bias((two, LANES), cols, valid, lambda at: at, radius + 1, query_row)
        query = pairs_of(jnp.concatenate([q_ref[lo : lo + one, :] * scale, pad], axis=0))
        grad = pairs_of(jnp.concatenate([grad_ref[lo : lo + one, :], pad], axis=0))
        products = []
        for p in range(width // LANES):
            at = p * LANES
            keys = kv_ref[key_lo : key_lo + two, at : at + LANES]
            values = kv_ref[key_lo : key_lo + two, width + at : width + at + LANES]
            products.append((dot_nt(keys, query[p]) + bias, dot_nt(values, grad[p])))
        sides.append(products)

    def sums(products):
        tiles = []
        for scores, wgrad in products:
            top, _, total, dot = partial_sums(scores, wgrad)
            found = [part for row in (top, total, dot) for part in in_parts(row)]
            found.append(jnp.zeros((16 - len(found), LANES), F32))
            tiles.append(jnp.concatenate(found, axis=0))
        return jnp.concatenate(tiles, axis=1).astype(BF16)

    upper, lower = (sums(products) for products in sides)

    def pack(target, lo, found):
        parts = (kv_ref[lo : lo + one, :width], kv_ref[lo : lo + one, width:])
        parts += (q_ref[lo : lo + one, :], grad_ref[lo : lo + one, :])
        for at, part in enumerate(parts):
            target[at * one : (at + 1) * one, :] = part
        target[len(parts) * one :, :] = found

    @pl.when(even)
    def _():
        pack(near_ref, pixels - one, lower)
        pack(far_ref, 0, upper)

    @pl.when(jnp.logical_not(even))
    def _():
        pack(near_ref, 0, upper)
        pack(far_ref, pixels - one, lower)


def plan_kernel(
    cols, valid_ref, q_ref, kv_ref, grad_ref,
    beside_ref, above_ref, below_ref, queries_ref, grads_ref, keys_t_ref, raised_ref, wgrad_ref, sums_ref,
):
    radius = KERNEL // 2
    pixels, width = q_ref.shape
    rows = pixels // cols
    scale = 1.0 / math.sqrt(HD)
    band = lax.axis_index("rows")
    first, last = band == 0, band == lax.axis_size("rows") - 1
    valid = valid_here(valid_ref)

    def present(krow):
        return ((krow >= 0) | jnp.logical_not(first)) & ((krow < rows) | jnp.logical_not(last))

    beside_ref[...] = window_bias(
        beside_ref.shape, cols, valid,
        lambda at: jnp.where(at < radius, at - radius, at - radius + rows), rows, 0, present,
    )
    above_ref[...] = window_bias(
        above_ref.shape, cols, valid, lambda at: at, radius + 1, -radius
    )
    below_ref[...] = window_bias(
        below_ref.shape, cols, valid, lambda at: at + rows - radius, radius + 1, rows
    )
    bias = window_bias((pixels, pixels), cols, valid, lambda at: at, rows, 0)
    bias = jnp.concatenate([bias, bias], axis=1)
    keys_t_ref[...] = kv_ref[:, :width].T
    for p, (query, grad) in enumerate(zip(pairs_of(q_ref[...] * scale), pairs_of(grad_ref[...]))):
        at = p * LANES
        queries_ref[p], grads_ref[p] = query, grad
        wgrad = dot_nt(kv_ref[:, width + at : width + at + LANES], grad)
        top, raised, total, dot = partial_sums(
            dot_nt(kv_ref[:, at : at + LANES], query) + bias, wgrad
        )
        raised_ref[p], wgrad_ref[p] = raised, wgrad
        for row, value in enumerate((top, total, dot)):
            sums_ref[p, row : row + 1, :] = value


def fine_kernel(cols, carried, *refs):
    (kv_ref, near_ref, far_ref, beside_ref, above_ref, below_ref, queries_ref, grads_ref) = refs[:8]
    (keys_t_ref, raised_ref, wgrad_ref, sums_ref) = refs[8:12]
    outs = refs[12 + carried : 14 + 2 * carried]
    dq_ref, dkv_ref, sems = refs[14 + 2 * carried :]
    copies = [
        pltpu.make_async_copy(source, target, sems.at[2 + at])
        for at, (source, target) in enumerate(zip(refs[12 : 12 + carried], outs[2:]))
    ]
    for copy in copies:
        copy.start()
    radius = KERNEL // 2
    pixels, width = dq_ref.shape
    one = radius * cols
    scale = 1.0 / math.sqrt(HD)
    even = lax.axis_index("rows") % 2 == 0

    def received(at):
        rows_at = slice(at * one, (at + 1) * one) if at < 4 else slice(at * one, None)
        near, far = near_ref[rows_at, :], far_ref[rows_at, :]
        return jnp.where(even, far, near), jnp.where(even, near, far)

    def joined(table):
        return jnp.concatenate(table, axis=0)

    beside_keys, beside_values = joined(received(0)), joined(received(1))
    beside_t = beside_keys.T
    pad = jnp.zeros((cols, width), BF16)
    rest = jnp.zeros((pixels - one, LANES), BF16)
    side_lo = (0, pixels - one)
    side_query = [pairs_of(joined([t * scale, pad])) for t in received(2)]
    side_grad = [pairs_of(joined([t, pad])) for t in received(3)]
    side_sums = [t.astype(F32) for t in received(4)]
    beside_bias = jnp.concatenate([beside_ref[...], beside_ref[...]], axis=1)
    pairs = range(width // LANES)
    ats = [slice(p * LANES, (p + 1) * LANES) for p in pairs]
    value_ats = [slice(width + p * LANES, width + (p + 1) * LANES) for p in pairs]
    sides = [(side, p) for side in range(2) for p in pairs]
    beside_scores = [dot_nt(beside_keys[:, ats[p]], queries_ref[p]) + beside_bias for p in pairs]
    beside_wgrad = [dot_nt(beside_values[:, ats[p]], grads_ref[p]) for p in pairs]
    side_scores, side_wgrad = {}, {}
    for side, p in sides:
        keys_at = slice(side_lo[side], side_lo[side] + one)
        bias_ref = (above_ref, below_ref)[side]
        side_scores[side, p] = (
            dot_nt(kv_ref[keys_at, ats[p]], side_query[side][p]) + bias_ref[...]
        )
        side_wgrad[side, p] = dot_nt(kv_ref[keys_at, value_ats[p]], side_grad[side][p])
    lows, sgrads, beside_sgrads = {}, {}, {}
    for p in pairs:
        factor, beside_weights, row_dot = completed(
            tuple(sums_ref[p, row : row + 1, :] for row in range(3)),
            beside_scores[p],
            beside_wgrad[p],
        )
        beside_sgrads[p] = (beside_weights * (beside_wgrad[p] - row_dot)).astype(BF16)
        weights = raised_ref[p] * factor
        lows[p] = weights.astype(BF16)
        sgrads[p] = (weights * (wgrad_ref[p] - row_dot)).astype(BF16)
    for side, p in sides:
        found = side_sums[side][:, ats[p]]
        kept = tuple(
            found[row : row + 1] + found[row + 1 : row + 2] + found[row + 2 : row + 3]
            for row in (0, 3, 6)
        )
        _, weights, row_dot = completed(kept, side_scores[side, p], side_wgrad[side, p])
        order = slice(None, None, -1 if side else 1)
        lows[side, p] = joined([weights.astype(BF16), rest][order])
        sgrad = (weights * (side_wgrad[side, p] - row_dot)).astype(BF16)
        sgrads[side, p] = joined([sgrad, rest][order])
    for p in pairs:
        dq_t = dot_nn(keys_t_ref[ats[p], :], sgrads[p]) + dot_nn(beside_t[ats[p]], beside_sgrads[p])
        dq_t = joined([dq_t[:HD, :pixels], dq_t[HD:, pixels:]])
        dq_ref[:, ats[p]] = (dq_t * scale).astype(BF16).T
    for p in pairs:
        dkv_ref[:, ats[p]] = dot_nn(
            jnp.concatenate([sgrads[p], sgrads[0, p], sgrads[1, p]], axis=1),
            joined([queries_ref[p], side_query[0][p], side_query[1][p]]),
        ).astype(BF16)
        dkv_ref[:, value_ats[p]] = dot_nn(
            jnp.concatenate([lows[p], lows[0, p], lows[1, p]], axis=1),
            joined([grads_ref[p], side_grad[0][p], side_grad[1][p]]),
        ).astype(BF16)
    copies += [
        pltpu.make_async_copy(source, target, sems.at[at])
        for at, (source, target) in enumerate(((dq_ref, outs[0]), (dkv_ref, outs[1])))
    ]
    for copy in copies[carried:]:
        copy.start()
    for copy in copies:
        copy.wait()


def coarse_kernel(frames, tokens, valid_ref, x_ref, dq_ref, dk_ref, dv_ref, wide, low_ref, sg_ref):
    bands = lax.axis_size("rows")
    width = dq_ref.shape[-1]
    parts = width // LANES
    height = x_ref.shape[0] // (frames * bands)
    band = lax.axis_index("rows")
    scale = 1.0 / math.sqrt(HD)
    wide[...] = x_ref[...].astype(F32)
    devices, own = frames * bands, frames * tokens

    def every(array, b):
        first = (array * parts + b) * tokens
        return jnp.concatenate(
            [wide[pl.ds(first + t, devices, stride=height), :] for t in range(tokens)], axis=0
        ).astype(BF16)

    def mine(array, b):
        first = band * height + (array * parts + b) * tokens
        return jnp.concatenate(
            [wide[pl.ds(first + f * bands * height, tokens), :] for f in range(frames)], axis=0
        ).astype(BF16)

    count = devices * tokens

    def key_bias(shape, dim):
        place = iota(shape, dim)
        token, frame = place // devices, place // bands % frames
        limit = jnp.zeros(shape, jnp.int32)
        for f in range(frames):
            limit = jnp.where(frame == f, valid_ref[:, f : f + 1], limit)
        return jnp.where(token * POOL < limit, 0.0, NEGATIVE)

    bias, own_bias = key_bias((count, 2 * count), 0), key_bias((2 * own, count), 1)
    halves = range(parts)
    keys, values = ([every(a, b) for b in halves] for a in (1, 2))
    queries, grads = ([pairs_of(every(a, b))[0] for b in halves] for a in (0, 3))
    queries = [query * scale for query in queries]
    own_queries = [pairs_of(mine(0, b) * scale)[0] for b in halves]
    own_grads = [pairs_of(mine(3, b))[0] for b in halves]
    scores = [dot_nt(keys[b], queries[b]) + bias for b in halves]
    wgrads = [dot_nt(values[b], grads[b]) for b in halves]
    own_scores = [dot_nt(own_queries[b], keys[b]) + own_bias for b in halves]
    own_wgrads = [dot_nt(own_grads[b], values[b]) for b in halves]
    found = [softmax_grads(scores[b], wgrads[b], 0) for b in halves]
    own_sgrads = [softmax_grads(own_scores[b], own_wgrads[b], 1)[1] for b in halves]
    for b in halves:
        low_ref[b], sg_ref[b] = found[b][0].astype(F32), found[b][1].astype(F32)

    def mine_rows(ref, b):
        pieces = [
            ref[b, pl.ds(t * devices + f * bands + band, 1), :]
            for f in range(frames)
            for t in range(tokens)
        ]
        return jnp.concatenate(pieces, axis=0).astype(BF16)

    for b in halves:
        full = dot_nn(own_sgrads[b], keys[b])
        dq = jnp.where(iota((own, LANES), 1) < HD, full[:own], full[own:]) * scale
        dk = dot_nn(mine_rows(sg_ref, b), queries[b])
        dv = dot_nn(mine_rows(low_ref, b), grads[b])
        for ref, table in ((dq_ref, dq), (dk_ref, dk), (dv_ref, dv)):
            rounded = table.astype(BF16)
            for f in range(frames):
                ref[f, :, b * LANES : (b + 1) * LANES] = rounded[f * tokens : (f + 1) * tokens]


def vmem():
    return pl.BlockSpec(memory_space=pltpu.VMEM)


def smem():
    return pl.BlockSpec(memory_space=pltpu.SMEM)


def hbm():
    return pl.BlockSpec(memory_space=pltpu.HBM)


def in_hbm(array):
    return pltpu.with_memory_space_constraint(array, pltpu.HBM)


def params():
    return pltpu.CompilerParams(vmem_limit_bytes=16 * 2**20)


def out(shape, dtype=BF16):
    return jax.ShapeDtypeStruct(shape, dtype)


def fine_level(carried, gain, valid, fine_q, fine_kv, cotangent):
    bands = lax.axis_size("rows")
    _, rows, cols, width = fine_q.shape
    pixels = rows * cols
    radius = KERNEL // 2
    query = fine_q.reshape(pixels, width)
    key_value = fine_kv.reshape(pixels, 2 * width)
    cot = cotangent.reshape(pixels, width)
    one, sums = radius * cols, 16
    packed = (4 * one + sums, width)
    near, far, grad = pl.pallas_call(
        functools.partial(prep_kernel, cols),
        in_specs=[vmem()] * 5,
        out_specs=[vmem()] * 3,
        out_shape=[out(packed), out(packed), out((pixels, width))],
        compiler_params=params(),
    )(valid, gain, query, key_value, cot)
    pairs = [(i, i ^ 1) for i in range(bands) if i ^ 1 < bands]
    others = [(i, ((i + 1) ^ 1) - 1) for i in range(1, bands) if ((i + 1) ^ 1) - 1 < bands]
    near = lax.ppermute(near, "rows", pairs)
    far = lax.ppermute(far, "rows", others)
    count = width // LANES
    plan = pl.pallas_call(
        functools.partial(plan_kernel, cols),
        in_specs=[vmem()] * 4,
        out_specs=[vmem()] * 9,
        out_shape=[
            out((2 * one, pixels), F32),
            out((one, LANES), F32),
            out((one, LANES), F32),
            out((count, 2 * pixels, LANES)),
            out((count, 2 * pixels, LANES)),
            out((width, pixels)),
            out((count, pixels, 2 * pixels), F32),
            out((count, pixels, 2 * pixels), F32),
            out((count, 8, 2 * pixels), F32),
        ],
        compiler_params=params(),
    )(valid, query, key_value, grad)
    grads = pl.pallas_call(
        functools.partial(fine_kernel, cols, len(carried)),
        in_specs=[vmem()] * (12 + len(carried)),
        out_specs=[hbm()] * (2 + len(carried)),
        out_shape=[out((pixels, width)), out((pixels, 2 * width))]
        + [out(x.shape) for x in carried],
        scratch_shapes=[
            pltpu.VMEM((pixels, width), BF16),
            pltpu.VMEM((pixels, 2 * width), BF16),
            pltpu.SemaphoreType.DMA((2 + len(carried),)),
        ],
        compiler_params=params(),
        cost_estimate=pl.CostEstimate(flops=400_000_000, bytes_accessed=1_000_000, transcendentals=300_000),
    )(key_value, near, far, *plan, *carried)
    return (grads[0].reshape(fine_q.shape), grads[1].reshape(fine_kv.shape), *grads[2:])


def coarse_direct(coarse_q, coarse_kv, cotangent, gain_table, timesteps, valid_cols):
    frames, bands = lax.axis_size("frames"), lax.axis_size("rows")
    _, rows, cols, width = cotangent.shape
    tokens, cwidth = coarse_q.shape[-2:]
    head_width = cwidth // frames
    tile = 4 * tokens * head_width // LANES
    sent, gain, valid = pl.pallas_call(
        functools.partial(send_kernel, cols, bands),
        in_specs=[smem()] + [hbm()] * 5,
        out_specs=[vmem()] * 3,
        out_shape=[
            out((frames * bands * tile, LANES)),
            out((1, width), F32),
            out((1, frames), jnp.int32),
        ],
        scratch_shapes=[
            pltpu.VMEM((rows * cols, width), BF16),
            pltpu.VMEM((8, width), F32),
            pltpu.VMEM((tokens, cwidth), BF16),
            pltpu.VMEM((tokens, 2 * cwidth), BF16),
            pltpu.SemaphoreType.DMA((8,)),
        ],
        compiler_params=params(),
    )(
        timesteps,
        in_hbm(valid_cols.reshape(1, -1)),
        in_hbm(cotangent.reshape(rows * cols, width)),
        in_hbm(gain_table),
        in_hbm(coarse_q.reshape(tokens, cwidth)),
        in_hbm(coarse_kv.reshape(tokens, 2 * cwidth)),
    )
    held = lax.all_to_all(
        sent.reshape(frames * bands, tile, LANES),
        ("frames", "rows"),
        split_axis=0,
        concat_axis=0,
        tiled=True,
    ).reshape(frames * bands * tile, LANES)
    count = frames * bands * tokens
    outs = pl.pallas_call(
        functools.partial(coarse_kernel, frames, tokens),
        in_specs=[vmem()] * 2,
        out_specs=[vmem()] * 3,
        out_shape=[out((frames, tokens, head_width))] * 3,
        scratch_shapes=[
            pltpu.VMEM(held.shape, F32),
            pltpu.VMEM((head_width // LANES, count, 2 * count), F32),
            pltpu.VMEM((head_width // LANES, count, 2 * count), F32),
        ],
        compiler_params=params(),
        cost_estimate=pl.CostEstimate(flops=100_000_000_000, bytes_accessed=100_000_000, transcendentals=0),
    )(valid, held)
    return outs, gain, valid


def normalize(scores):
    row_max = jnp.max(scores, axis=-1, keepdims=True)
    return row_max + jnp.log(jnp.sum(jnp.exp(scores - row_max), axis=-1, keepdims=True))


def coarse_gathered(coarse_q, coarse_kv, cotangent, gain_table, timesteps, valid_cols):
    score_scale = 1.0 / math.sqrt(HD)
    frames_here, _, cols_here, fine_width = cotangent.shape
    total_frames = valid_cols.shape[0]
    steps_all = gain_table.shape[0]
    select = (timesteps[:, None] == jnp.arange(steps_all)[None, :]).astype(F32)
    frame_gain = jnp.dot(select, gain_table, precision=lax.Precision.HIGHEST)
    scaled_grad = frame_gain[:, None, None, :] * cotangent.astype(F32)
    half_pool = POOL // 2
    coarse_cols = cols_here // POOL
    coarse_width = coarse_q.shape[-1]
    coarse_count = frames_here * coarse_cols
    blocks = scaled_grad.reshape(frames_here, 2, half_pool, coarse_cols, 2, half_pool, fine_width)
    pooled = (
        jnp.sum(blocks, axis=(2, 5))
        .transpose(0, 2, 1, 3, 4)
        .reshape(coarse_count, coarse_width)
        .astype(BF16)
    )
    mine_query = coarse_q.reshape(coarse_count, coarse_width)
    mine_keys = coarse_kv[..., :coarse_width].reshape(coarse_count, coarse_width)
    mine_values = coarse_kv[..., coarse_width:].reshape(coarse_count, coarse_width)
    head_query, head_keys, head_values, head_grad = (
        lax.all_to_all(mine_query, "frames", split_axis=1, concat_axis=0, tiled=True),
        lax.all_to_all(mine_keys, "frames", split_axis=1, concat_axis=0, tiled=True),
        lax.all_to_all(mine_values, "frames", split_axis=1, concat_axis=0, tiled=True),
        lax.all_to_all(pooled, "frames", split_axis=1, concat_axis=0, tiled=True),
    )
    head_tokens, head_width = head_query.shape
    head_groups = head_width // HD
    query_heads = head_query.reshape(head_tokens, head_groups, HD)
    grad_heads = head_grad.reshape(head_tokens, head_groups, HD)
    every_keys, every_values = (
        lax.all_gather(head_keys, "rows", axis=0, tiled=True),
        lax.all_gather(head_values, "rows", axis=0, tiled=True),
    )
    every_count = every_keys.shape[0]
    key_heads = every_keys.reshape(every_count, head_groups, HD)
    value_heads = every_values.reshape(every_count, head_groups, HD)
    position = jnp.arange(every_count) % head_tokens
    key_frame = position // coarse_cols
    key_column = position % coarse_cols
    col_limit = jnp.sum(
        jnp.where(key_frame[:, None] == jnp.arange(total_frames)[None, :], valid_cols[None, :], 0),
        axis=1,
    )
    key_ok = key_column * POOL < col_limit
    coarse_scores = (
        jnp.einsum("qhd,khd->hqk", query_heads, key_heads, preferred_element_type=F32)
        * score_scale
    )
    coarse_scores = jnp.where(key_ok[None, None, :], coarse_scores, NEGATIVE)
    log_total = normalize(coarse_scores)
    coarse_weights = jnp.exp(coarse_scores - log_total)
    coarse_low = coarse_weights.astype(BF16)
    coarse_out = jnp.einsum("hqk,khd->qhd", coarse_low, value_heads, preferred_element_type=F32)
    coarse_dot = jnp.sum(grad_heads.astype(F32) * coarse_out, axis=-1)
    coarse_wgrad = jnp.einsum("qhd,khd->hqk", grad_heads, value_heads, preferred_element_type=F32)
    coarse_sgrad = (coarse_weights * (coarse_wgrad - coarse_dot.T[:, :, None])).astype(BF16)
    coarse_qgrad = (
        jnp.einsum("hqk,khd->qhd", coarse_sgrad, key_heads, preferred_element_type=F32)
        * score_scale
    )
    count = head_tokens * lax.axis_size("rows")
    key_part = (
        jnp.einsum("hqk,qhd->khd", coarse_sgrad, query_heads, preferred_element_type=F32)
        * score_scale
    )
    value_part = jnp.einsum("hqk,qhd->khd", coarse_low, grad_heads, preferred_element_type=F32)
    terms = lax.psum_scatter(
        jnp.concatenate(
            [key_part.reshape(count, head_width), value_part.reshape(count, head_width)], axis=1
        ),
        "rows",
        scatter_dimension=0,
        tiled=True,
    )
    total_keys = terms[:, :head_width]
    total_values = terms[:, head_width:]
    out_dims = (head_tokens // coarse_cols, 1, coarse_cols, head_width)
    return (
        coarse_qgrad.reshape(out_dims).astype(BF16),
        total_keys.reshape(out_dims).astype(BF16),
        total_values.reshape(out_dims).astype(BF16),
    ), frame_gain


def local(fine_q, fine_kv, coarse_q, coarse_kv, cotangent, gain_table, timesteps, valid_cols):
    frames, bands = lax.axis_size("frames"), lax.axis_size("rows")
    head_width = coarse_q.shape[-1] // frames
    tokens = coarse_q.shape[-2]
    direct = (
        head_width == cotangent.shape[-1]
        and 4 * tokens * head_width // LANES == 16
        and frames * bands * tokens <= 128
    )
    operands = (coarse_q, coarse_kv, cotangent, gain_table, timesteps, valid_cols)
    fine = (fine_q, fine_kv, cotangent)
    if direct:
        carried, gain, valid = coarse_direct(*operands)
        grad_q, grad_kv, *coarse_grads = fine_level(carried, gain, valid, *fine)
        shape = (frames, 1, tokens, head_width)
        return (grad_q, grad_kv, *(x.reshape(shape) for x in coarse_grads))
    coarse_grads, gain = coarse_gathered(*operands)
    return (*fine_level([], gain, valid_cols.reshape(1, -1), *fine), *coarse_grads)


def solution(mesh):
    placed = (
        P("frames", "rows", None, None),
        P("frames", "rows", None, None),
        P("frames", "rows", None, None),
        P("frames", "rows", None, None),
        P("frames", "rows", None, None),
        P(),
        P("frames"),
        P(),
    )
    return jax.shard_map(
        local,
        mesh=mesh,
        in_specs=placed,
        out_specs=(
            P("frames", "rows", None, None),
            P("frames", "rows", None, None),
            P(None, "rows", None, "frames"),
            P(None, "rows", None, "frames"),
            P(None, "rows", None, "frames"),
        ),
        check_vma=False,
    )
```

```python
import functools
import math

import jax
import jax.numpy as jnp
from jax import lax
from jax.experimental import pallas as pl
from jax.experimental.pallas import tpu as pltpu
from jax.sharding import PartitionSpec as P

HD = 64
KERNEL = 7
POOL = 8
LANES = 128

NEGATIVE = -1e30

F32 = jnp.float32
BF16 = jnp.bfloat16


def dot_nt(left, right):
    return lax.dot_general(left, right, (((1,), (1,)), ((), ())), preferred_element_type=F32)


def dot_nn(left, right):
    return jnp.dot(left, right, preferred_element_type=F32)


def iota(shape, dim):
    return lax.broadcasted_iota(jnp.int32, shape, dim)


def pairs_of(table):
    blocks = []
    for lo in range(0, table.shape[1], LANES):
        part = table[:, lo : lo + LANES]
        first = iota(part.shape, 1) < HD
        zero = jnp.zeros_like(part)
        blocks.append(
            jnp.concatenate([jnp.where(first, part, zero), jnp.where(first, zero, part)], axis=0)
        )
    return blocks


def softmax_grads(scores, weight_grad, axis):
    top = jnp.max(scores, axis=axis, keepdims=True)
    raised = jnp.exp(scores - top)
    share = 1.0 / jnp.sum(raised, axis=axis, keepdims=True)
    row_dot = jnp.sum(raised * weight_grad, axis=axis, keepdims=True) * share
    weights = raised * share
    return weights.astype(BF16), (weights * (weight_grad - row_dot)).astype(BF16)


def send_kernel(
    cols, bands, step_ref, valid_hbm, cot_hbm, gain_hbm, cq_hbm, ckv_hbm,
    send_ref, gain_ref, valid_ref, cot_ref, eight_ref, cq_ref, ckv_ref, sems,
):
    step = step_ref[0]
    eight = eight_ref.shape[0]
    first = pl.multiple_of(step // eight * eight, eight)
    gain_copy = pltpu.make_async_copy(gain_hbm.at[pl.ds(first, eight)], eight_ref, sems.at[0])
    copies = [
        pltpu.make_async_copy(source, target, sems.at[1 + at])
        for at, (source, target) in enumerate(
            tuple((cot_hbm.at[pl.ds(r, 32)], cot_ref.at[pl.ds(r, 32)]) for r in range(0, 128, 32)) + ((cq_hbm, cq_ref), (ckv_hbm, ckv_ref), (valid_hbm, valid_ref))
        )
    ]
    for copy in copies[:-1]:
        copy.start()
    gain_copy.start()
    copies[-1].start()
    pixels, width = cot_ref.shape
    tokens, cwidth = cq_ref.shape
    half = POOL // 2
    groups = cwidth // width
    part = iota((groups * tokens, pixels), 0)
    group, token = part // tokens, part % tokens
    pixel = iota((groups * tokens, pixels), 1)
    row, col = pixel // cols, pixel % cols
    inside = (row // half == group // 2) & (col // half == token * 2 + group % 2)
    for copy in copies:
        copy.wait()
    summed = dot_nn(inside.astype(BF16), cot_ref[...])
    query = cq_ref[...].astype(F32)
    both = ckv_ref[...].astype(F32)
    gain_copy.wait()
    gain = eight_ref[pl.ds(step - first, 1), :]
    gain_ref[...] = gain
    pooled = summed * gain
    for g in range(groups):
        lo = g * width
        arrays = (
            query[:, lo : lo + width],
            both[:, lo : lo + width],
            both[:, cwidth + lo : cwidth + lo + width],
            pooled[g * tokens : (g + 1) * tokens, :],
        )
        tile = jnp.concatenate(
            [a[:, b : b + LANES] for a in arrays for b in range(0, width, LANES)], axis=0
        ).astype(BF16)
        height = tile.shape[0]
        for r in range(bands):
            start = (g * bands + r) * height
            send_ref[start : start + height, :] = tile


def valid_here(valid_ref):
    frame = lax.axis_index("frames")
    return sum(
        jnp.where(frame == f, valid_ref[:, f : f + 1], 0) for f in range(valid_ref.shape[1])
    )


def window_bias(shape, cols, valid, lane_rows, query_row):
    radius = KERNEL // 2
    place, lane = iota(shape, 0), iota(shape, 1)
    krow, kcol = place // cols, place % cols
    qrow, qcol = lane // cols % lane_rows + query_row, lane % cols
    seen = (jnp.abs(krow - qrow) <= radius) & (jnp.abs(kcol - qcol) <= radius) & (kcol < valid)
    seen = seen | ((krow == qrow) & (kcol == qcol))
    return jnp.where(seen, 0.0, NEGATIVE)


def partial_sums(scores, weight_grad):
    top = jnp.max(scores, axis=0, keepdims=True)
    raised = jnp.exp(scores - top)
    total = jnp.sum(raised, axis=0, keepdims=True)
    return top, raised, total, jnp.sum(raised * weight_grad, axis=0, keepdims=True)


def completed(kept, scores, weight_grad):
    top_kept, total_kept, dot_kept = kept
    top = jnp.maximum(top_kept, jnp.max(scores, axis=0, keepdims=True))
    factor = jnp.exp(top_kept - top)
    raised = jnp.exp(scores - top)
    total = total_kept * factor + jnp.sum(raised, axis=0, keepdims=True)
    share = jnp.where(total > 0, 1.0 / total, 0.0)
    dot = dot_kept * factor + jnp.sum(raised * weight_grad, axis=0, keepdims=True)
    return factor * share, raised * share, dot * share


def in_parts(row):
    parts = []
    for _ in range(3):
        part = row.astype(BF16).astype(F32)
        parts.append(part)
        row = row - part
    return parts


def prep_kernel(
    cols, valid_ref, gain_ref, q_ref, kv_ref, cot_ref,
    near_ref, far_ref, grad_ref, raised_ref, wgrad_ref, sums_ref, queries_ref, grads_ref,
):
    radius = KERNEL // 2
    pixels, width = q_ref.shape
    one, two = radius * cols, 2 * radius * cols
    scale = 1.0 / math.sqrt(HD)
    even = lax.axis_index("rows") % 2 == 0
    valid = valid_here(valid_ref)
    grad_ref[...] = (gain_ref[...] * cot_ref[...].astype(F32)).astype(BF16)
    pad = jnp.zeros((cols, width), BF16)
    pairs = range(width // LANES)
    scores = {}
    for side in range(2):
        lo, key_lo = side * (pixels - one), side * (pixels - two)
        bias = window_bias((two, LANES), cols, valid, radius + 1, side * radius)
        query = pairs_of(jnp.concatenate([q_ref[lo : lo + one, :] * scale, pad], axis=0))
        grad = pairs_of(jnp.concatenate([grad_ref[lo : lo + one, :], pad], axis=0))
        for p in pairs:
            at = p * LANES
            queries_ref[side, p], grads_ref[side, p] = query[p], grad[p]
            keys = kv_ref[key_lo : key_lo + two, at : at + LANES]
            values = kv_ref[key_lo : key_lo + two, width + at : width + at + LANES]
            scores[side, p] = dot_nt(keys, query[p]) + bias, dot_nt(values, grad[p])
    found = []
    for side in range(2):
        tiles = []
        for p in pairs:
            score, wgrad = scores[side, p]
            top, raised, total, dot = partial_sums(score, wgrad)
            raised_ref[side, p], wgrad_ref[side, p] = raised, wgrad
            for row, value in enumerate((top, total, dot)):
                sums_ref[side, p, row : row + 1, :] = value
            parts = [part for row in (top, total, dot) for part in in_parts(row)]
            parts.append(jnp.zeros((16 - len(parts), LANES), F32))
            tiles.append(jnp.concatenate(parts, axis=0))
        found.append(jnp.concatenate(tiles, axis=1).astype(BF16))

    def pack(target, side):
        lo = side * (pixels - one)
        parts = (kv_ref[lo : lo + one, :width], kv_ref[lo : lo + one, width:])
        parts += (q_ref[lo : lo + one, :], grad_ref[lo : lo + one, :])
        for at, part in enumerate(parts):
            target[at * one : (at + 1) * one, :] = part
        target[len(parts) * one :, :] = found[side]

    @pl.when(even)
    def _():
        pack(near_ref, 1)
        pack(far_ref, 0)

    @pl.when(jnp.logical_not(even))
    def _():
        pack(near_ref, 0)
        pack(far_ref, 1)


def plan_kernel(
    cols, valid_ref, q_ref, kv_ref, grad_ref, own_bias_ref, halo_bias_ref, dq_ref, total_ref
):
    radius = KERNEL // 2
    pixels, width = q_ref.shape
    rows = pixels // cols
    one, middle = radius * cols, pixels - 2 * radius * cols
    scale = 1.0 / math.sqrt(HD)
    band = lax.axis_index("rows")
    valid = valid_here(valid_ref)
    shape = own_bias_ref.shape[1:]
    place, lane = iota(shape, 0), iota(shape, 1)
    kcol, qcol = place % cols, lane % cols
    gap = place // cols - lane // cols % (radius + 1)
    close = (jnp.abs(kcol - qcol) <= radius) & (kcol < valid)
    for side, missing in enumerate((band == 0, band == lax.axis_size("rows") - 1)):
        own = gap if side == 0 else -gap
        seen = close & (own >= 0) & jnp.logical_not(missing)
        own_bias_ref[side] = jnp.where(seen, 0.0, NEGATIVE)
        halo_bias_ref[side] = jnp.where(close & (own <= 0), 0.0, NEGATIVE)
    head = iota((middle, width), 1) // HD

    def by_head(table):
        zero = jnp.zeros_like(table)
        return jnp.concatenate(
            [jnp.where(head == h, table, zero) for h in range(width // HD)], axis=0
        )

    query = by_head(q_ref[one : one + middle, :] * scale)
    grad = by_head(grad_ref[one : one + middle, :])
    keys, values = kv_ref[:, :width], kv_ref[:, width:]
    bias = window_bias((pixels, query.shape[0]), cols, valid, middle // cols, radius)
    low, sgrad = softmax_grads(dot_nt(keys, query) + bias, dot_nt(values, grad), 0)
    full = dot_nn(sgrad.T, keys)
    dq = sum(
        jnp.where(head == h, full[h * middle : (h + 1) * middle], 0.0) for h in range(width // HD)
    )
    dq_ref[...] = (dq * scale).astype(BF16)
    total_ref[:, :width] = dot_nn(sgrad, query)
    total_ref[:, width:] = dot_nn(low, grad)


def side_rows(cols, pixels, side):
    two = 2 * (KERNEL // 2) * cols
    window = pl.ds(pl.multiple_of(side * (pixels - two), cols), two)
    others = pl.ds(pl.multiple_of((1 - side) * two, cols), pixels - two)
    return window, others


def side_terms(cols, side, refs, meanwhile=lambda: None, later=lambda: None):
    (kv_ref, halo_ref, own_bias_ref, halo_bias_ref, raised_ref, wgrad_ref, sums_ref) = refs[:7]
    queries_ref, grads_ref = refs[7:]
    radius = KERNEL // 2
    pixels, width = kv_ref.shape[0], kv_ref.shape[1] // 2
    one, two = radius * cols, 2 * radius * cols
    scale = 1.0 / math.sqrt(HD)
    window, _ = side_rows(cols, pixels, side)
    border = pl.ds(pl.multiple_of(side * (pixels - one), cols), one)
    halo_keys, halo_values = halo_ref[:one, :], halo_ref[one:two, :]
    pad = jnp.zeros((cols, width), BF16)

    def joined(table):
        return jnp.concatenate(table, axis=0)

    def at_border(table):
        table, zero = table.astype(BF16), jnp.zeros(table.shape, BF16)
        return joined([jnp.where(side == 0, table, zero), jnp.where(side == 0, zero, table)])

    halo_query = pairs_of(joined([halo_ref[two : two + one, :] * scale, pad]))
    halo_grad = pairs_of(joined([halo_ref[two + one : 2 * two, :], pad]))
    halo_sums = halo_ref[2 * two :, :].astype(F32)
    pairs = range(width // LANES)
    ats = [slice(p * LANES, (p + 1) * LANES) for p in pairs]
    value_ats = [slice(width + p * LANES, width + (p + 1) * LANES) for p in pairs]
    own_bias, halo_bias = own_bias_ref[side], halo_bias_ref[side]
    own_scores = [dot_nt(halo_keys[:, ats[p]], queries_ref[side, p]) + own_bias for p in pairs]
    own_wgrad = [dot_nt(halo_values[:, ats[p]], grads_ref[side, p]) for p in pairs]
    halo_scores = [dot_nt(kv_ref[border, ats[p]], halo_query[p]) + halo_bias for p in pairs]
    halo_wgrad = [dot_nt(kv_ref[border, value_ats[p]], halo_grad[p]) for p in pairs]
    meanwhile()
    lows, sgrads, beyond, halo_lows, halo_sgrads = [], [], [], [], []
    for p in pairs:
        kept = tuple(sums_ref[side, p, row : row + 1, :] for row in range(3))
        factor, weights, row_dot = completed(kept, own_scores[p], own_wgrad[p])
        beyond.append((weights * (own_wgrad[p] - row_dot)).astype(BF16))
        weights = raised_ref[side, p] * factor
        lows.append(weights.astype(BF16))
        sgrads.append((weights * (wgrad_ref[side, p] - row_dot)).astype(BF16))
        found = halo_sums[:, ats[p]]
        kept = tuple(
            found[row : row + 1] + found[row + 1 : row + 2] + found[row + 2 : row + 3]
            for row in (0, 3, 6)
        )
        _, weights, row_dot = completed(kept, halo_scores[p], halo_wgrad[p])
        halo_lows.append(at_border(weights))
        halo_sgrads.append(at_border(weights * (halo_wgrad[p] - row_dot)))
    later()
    dq, dk, dv = [], [], []
    for p in pairs:
        dk.append(
            dot_nn(
                jnp.concatenate([sgrads[p], halo_sgrads[p]], axis=1),
                joined([queries_ref[side, p], halo_query[p]]),
            )
        )
        dv.append(
            dot_nn(
                jnp.concatenate([lows[p], halo_lows[p]], axis=1),
                joined([grads_ref[side, p], halo_grad[p]]),
            )
        )
        full = dot_nn(
            joined([sgrads[p], beyond[p]]).T, joined([kv_ref[window, ats[p]], halo_keys[:, ats[p]]])
        )
        first = iota((one, LANES), 1) < HD
        dq.append(jnp.where(first, full[:one], full[one + cols : two + cols]) * scale)
    return jnp.concatenate(dq, axis=1).astype(BF16), dk + dv


def side_border(cols, pixels, side):
    one = KERNEL // 2 * cols
    return pl.ds(pl.multiple_of(side * (pixels - one), cols), one)


def near_kernel(cols, middle_ref, total_in, *refs, hooks=()):
    *refs, dq_ref, total_ref = refs
    side = 1 - lax.axis_index("rows") % 2
    pixels = total_ref.shape[0]
    one = KERNEL // 2 * cols
    window, others = side_rows(cols, pixels, side)
    dq, terms = side_terms(cols, side, refs, *hooks)
    dq_ref[one : pixels - one, :] = middle_ref[...]
    dq_ref[side_border(cols, pixels, side), :] = dq
    total_ref[others, :] = total_in[others, :]
    for at, term in enumerate(terms):
        lanes = slice(at * LANES, (at + 1) * LANES)
        total_ref[window, lanes] = total_in[window, lanes] + term


def far_kernel(cols, carried, *refs):
    dq_in, total_in = refs[:2]
    given = refs[2 : 2 + carried]
    refs = refs[2 + carried :]
    outs = refs[9 : 11 + carried]
    dq_ref, dkv_ref, sems = refs[11 + carried :]
    side = lax.axis_index("rows") % 2
    pixels = total_in.shape[0]
    one = KERNEL // 2 * cols
    window, others = side_rows(cols, pixels, side)
    near_border = side_border(cols, pixels, 1 - side)
    early = [
        (dkv_ref.at[others], outs[1].at[others]),
        *zip(given, outs[2:]),
    ]
    late = [(dq_ref, outs[0]), (dkv_ref.at[window], outs[1].at[window])]
    copies = [
        pltpu.make_async_copy(source, target, sems.at[at])
        for at, (source, target) in enumerate(early + late)
    ]

    def meanwhile():
        for copy in copies[: len(early)]:
            copy.start()

    dkv_ref[others, :] = total_in[others, :].astype(BF16)
    dq, terms = side_terms(cols, side, refs[:9], meanwhile)
    dq_ref[one : pixels - one, :] = dq_in[one : pixels - one, :]
    dq_ref[near_border, :] = dq_in[near_border, :]
    dq_ref[side_border(cols, pixels, side), :] = dq
    for at, term in enumerate(terms):
        lanes = slice(at * LANES, (at + 1) * LANES)
        dkv_ref[window, lanes] = (total_in[window, lanes] + term).astype(BF16)
    for copy in copies[len(early) :]:
        copy.start()
    for copy in copies:
        copy.wait()


def coarse_stages(
    frames, tokens, valid_ref, x_ref, dq_ref, dk_ref, dv_ref, wide, low_ref, sg_ref
):
    bands = lax.axis_size("rows")
    width = dq_ref.shape[-1]
    parts = width // LANES
    height = x_ref.shape[0] // (frames * bands)
    band = lax.axis_index("rows")
    scale = 1.0 / math.sqrt(HD)
    wide[...] = x_ref[...].astype(F32)
    devices, own = frames * bands, frames * tokens

    def every(array, b):
        first = (array * parts + b) * tokens
        return jnp.concatenate(
            [wide[pl.ds(first + t, devices, stride=height), :] for t in range(tokens)], axis=0
        ).astype(BF16)

    def mine(array, b):
        first = band * height + (array * parts + b) * tokens
        return jnp.concatenate(
            [wide[pl.ds(first + f * bands * height, tokens), :] for f in range(frames)], axis=0
        ).astype(BF16)

    count = devices * tokens

    def key_bias(shape, dim):
        place = iota(shape, dim)
        token, frame = place // devices, place // bands % frames
        limit = jnp.zeros(shape, jnp.int32)
        for f in range(frames):
            limit = jnp.where(frame == f, valid_ref[:, f : f + 1], limit)
        return jnp.where(token * POOL < limit, 0.0, NEGATIVE)

    bias, own_bias = key_bias((count, 2 * count), 0), key_bias((2 * own, count), 1)
    halves = range(parts)
    keys, values = ([every(a, b) for b in halves] for a in (1, 2))
    queries, grads = ([pairs_of(every(a, b))[0] for b in halves] for a in (0, 3))
    queries = [query * scale for query in queries]
    own_queries = [pairs_of(mine(0, b) * scale)[0] for b in halves]
    own_grads = [pairs_of(mine(3, b))[0] for b in halves]
    scores = [dot_nt(keys[b], queries[b]) + bias for b in halves]
    wgrads = [dot_nt(values[b], grads[b]) for b in halves]
    own_scores = [dot_nt(own_queries[b], keys[b]) + own_bias for b in halves]
    own_wgrads = [dot_nt(own_grads[b], values[b]) for b in halves]
    yield
    found = [softmax_grads(scores[b], wgrads[b], 0) for b in halves]
    own_sgrads = [softmax_grads(own_scores[b], own_wgrads[b], 1)[1] for b in halves]
    for b in halves:
        low_ref[b], sg_ref[b] = found[b][0].astype(F32), found[b][1].astype(F32)

    yield

    def mine_rows(ref, b):
        pieces = [
            ref[b, pl.ds(t * devices + f * bands + band, 1), :]
            for f in range(frames)
            for t in range(tokens)
        ]
        return jnp.concatenate(pieces, axis=0).astype(BF16)

    for b in halves:
        full = dot_nn(own_sgrads[b], keys[b])
        dq = jnp.where(iota((own, LANES), 1) < HD, full[:own], full[own:]) * scale
        dk = dot_nn(mine_rows(sg_ref, b), queries[b])
        dv = dot_nn(mine_rows(low_ref, b), grads[b])
        for ref, table in ((dq_ref, dq), (dk_ref, dk), (dv_ref, dv)):
            rounded = table.astype(BF16)
            for f in range(frames):
                ref[f, :, b * LANES : (b + 1) * LANES] = rounded[f * tokens : (f + 1) * tokens]
    yield


def near_and_coarse_kernel(cols, frames, tokens, *refs):
    coarse_in, near_in = refs[:2], refs[2:13]
    coarse_out, near_out, scratch = refs[13:16], refs[16:18], refs[18:]
    stages = coarse_stages(frames, tokens, *coarse_in, *coarse_out, *scratch)
    next(stages)
    near_kernel(cols, *near_in, *near_out, hooks=[lambda: next(stages)] * 2)


def vmem():
    return pl.BlockSpec(memory_space=pltpu.VMEM)


def smem():
    return pl.BlockSpec(memory_space=pltpu.SMEM)


def hbm():
    return pl.BlockSpec(memory_space=pltpu.HBM)


def in_hbm(array):
    return pltpu.with_memory_space_constraint(array, pltpu.HBM)


def params():
    return pltpu.CompilerParams(vmem_limit_bytes=16 * 2**20)


def out(shape, dtype=BF16):
    return jax.ShapeDtypeStruct(shape, dtype)


def fine_level(coarse, gain, valid, fine_q, fine_kv, cotangent):
    bands = lax.axis_size("rows")
    _, rows, cols, width = fine_q.shape
    pixels = rows * cols
    radius = KERNEL // 2
    query = fine_q.reshape(pixels, width)
    key_value = fine_kv.reshape(pixels, 2 * width)
    cot = cotangent.reshape(pixels, width)
    one, sums = radius * cols, 16
    packed = (4 * one + sums, width)
    count, stack = width // LANES, 2 * (one + cols)
    near, far, grad, *kept = pl.pallas_call(
        functools.partial(prep_kernel, cols),
        in_specs=[vmem()] * 5,
        out_specs=[vmem()] * 8,
        out_shape=[
            out(packed),
            out(packed),
            out((pixels, width)),
            out((2, count, 2 * one, LANES), F32),
            out((2, count, 2 * one, LANES), F32),
            out((2, count, 8, LANES), F32),
            out((2, count, stack, LANES)),
            out((2, count, stack, LANES)),
        ],
        compiler_params=params(),
    )(valid, gain, query, key_value, cot)
    pairs = [(i, i ^ 1) for i in range(bands) if i ^ 1 < bands]
    others = [(i, ((i + 1) ^ 1) - 1) for i in range(1, bands) if ((i + 1) ^ 1) - 1 < bands]
    near = lax.ppermute(near, "rows", pairs)
    far = lax.ppermute(far, "rows", others)
    *biases, middle_q, total = pl.pallas_call(
        functools.partial(plan_kernel, cols),
        in_specs=[vmem()] * 4,
        out_specs=[vmem()] * 4,
        out_shape=[
            out((2, one, LANES), F32),
            out((2, one, LANES), F32),
            out((pixels - 2 * one, width)),
            out((pixels, 2 * width), F32),
        ],
        compiler_params=params(),
    )(valid, query, key_value, grad)
    near_in = (middle_q, total, key_value, near, *biases, *kept)
    near_out = [out((pixels, width)), out((pixels, 2 * width), F32)]
    if coarse is None:
        dq, total = pl.pallas_call(
            functools.partial(near_kernel, cols),
            in_specs=[vmem()] * len(near_in),
            out_specs=[vmem()] * 2,
            out_shape=near_out,
            compiler_params=params(),
        )(*near_in)
        carried = []
    else:
        held, frames, tokens, head_width = coarse
        all_tokens = frames * bands * tokens
        by_query = pltpu.VMEM((head_width // LANES, all_tokens, 2 * all_tokens), F32)
        *carried, dq, total = pl.pallas_call(
            functools.partial(near_and_coarse_kernel, cols, frames, tokens),
            in_specs=[vmem()] * (2 + len(near_in)),
            out_specs=[vmem()] * 5,
            out_shape=[out((frames, tokens, head_width))] * 3 + near_out,
            scratch_shapes=[pltpu.VMEM(held.shape, F32), by_query, by_query],
            compiler_params=params(),
            cost_estimate=pl.CostEstimate(
                flops=100_000_000_000, bytes_accessed=100_000_000, transcendentals=0
            ),
        )(valid, held, *near_in)
    grads = pl.pallas_call(
        functools.partial(far_kernel, cols, len(carried)),
        in_specs=[vmem()] * (11 + len(carried)),
        out_specs=[hbm()] * (2 + len(carried)),
        out_shape=[out((pixels, width)), out((pixels, 2 * width))]
        + [out(x.shape) for x in carried],
        scratch_shapes=[
            pltpu.VMEM((pixels, width), BF16),
            pltpu.VMEM((pixels, 2 * width), BF16),
            pltpu.SemaphoreType.DMA((3 + len(carried),)),
        ],
        compiler_params=params(),
        cost_estimate=pl.CostEstimate(flops=400_000_000, bytes_accessed=1_000_000, transcendentals=300_000),
    )(dq, total, *carried, key_value, far, *biases, *kept)
    return (grads[0].reshape(fine_q.shape), grads[1].reshape(fine_kv.shape), *grads[2:])


def coarse_direct(coarse_q, coarse_kv, cotangent, gain_table, timesteps, valid_cols):
    frames, bands = lax.axis_size("frames"), lax.axis_size("rows")
    _, rows, cols, width = cotangent.shape
    tokens, cwidth = coarse_q.shape[-2:]
    head_width = cwidth // frames
    tile = 4 * tokens * head_width // LANES
    sent, gain, valid = pl.pallas_call(
        functools.partial(send_kernel, cols, bands),
        in_specs=[smem()] + [hbm()] * 5,
        out_specs=[vmem()] * 3,
        out_shape=[
            out((frames * bands * tile, LANES)),
            out((1, width), F32),
            out((1, frames), jnp.int32),
        ],
        scratch_shapes=[
            pltpu.VMEM((rows * cols, width), BF16),
            pltpu.VMEM((8, width), F32),
            pltpu.VMEM((tokens, cwidth), BF16),
            pltpu.VMEM((tokens, 2 * cwidth), BF16),
            pltpu.SemaphoreType.DMA((8,)),
        ],
        compiler_params=params(),
    )(
        timesteps,
        in_hbm(valid_cols.reshape(1, -1)),
        in_hbm(cotangent.reshape(rows * cols, width)),
        in_hbm(gain_table),
        in_hbm(coarse_q.reshape(tokens, cwidth)),
        in_hbm(coarse_kv.reshape(tokens, 2 * cwidth)),
    )
    held = lax.all_to_all(
        sent.reshape(frames * bands, tile, LANES),
        ("frames", "rows"),
        split_axis=0,
        concat_axis=0,
        tiled=True,
    ).reshape(frames * bands * tile, LANES)
    return (held, frames, tokens, head_width), gain, valid


def normalize(scores):
    row_max = jnp.max(scores, axis=-1, keepdims=True)
    return row_max + jnp.log(jnp.sum(jnp.exp(scores - row_max), axis=-1, keepdims=True))


def coarse_gathered(coarse_q, coarse_kv, cotangent, gain_table, timesteps, valid_cols):
    score_scale = 1.0 / math.sqrt(HD)
    frames_here, _, cols_here, fine_width = cotangent.shape
    total_frames = valid_cols.shape[0]
    steps_all = gain_table.shape[0]
    select = (timesteps[:, None] == jnp.arange(steps_all)[None, :]).astype(F32)
    frame_gain = jnp.dot(select, gain_table, precision=lax.Precision.HIGHEST)
    scaled_grad = frame_gain[:, None, None, :] * cotangent.astype(F32)
    half_pool = POOL // 2
    coarse_cols = cols_here // POOL
    coarse_width = coarse_q.shape[-1]
    coarse_count = frames_here * coarse_cols
    blocks = scaled_grad.reshape(frames_here, 2, half_pool, coarse_cols, 2, half_pool, fine_width)
    pooled = (
        jnp.sum(blocks, axis=(2, 5))
        .transpose(0, 2, 1, 3, 4)
        .reshape(coarse_count, coarse_width)
        .astype(BF16)
    )
    mine_query = coarse_q.reshape(coarse_count, coarse_width)
    mine_keys = coarse_kv[..., :coarse_width].reshape(coarse_count, coarse_width)
    mine_values = coarse_kv[..., coarse_width:].reshape(coarse_count, coarse_width)
    head_query, head_keys, head_values, head_grad = (
        lax.all_to_all(mine_query, "frames", split_axis=1, concat_axis=0, tiled=True),
        lax.all_to_all(mine_keys, "frames", split_axis=1, concat_axis=0, tiled=True),
        lax.all_to_all(mine_values, "frames", split_axis=1, concat_axis=0, tiled=True),
        lax.all_to_all(pooled, "frames", split_axis=1, concat_axis=0, tiled=True),
    )
    head_tokens, head_width = head_query.shape
    head_groups = head_width // HD
    query_heads = head_query.reshape(head_tokens, head_groups, HD)
    grad_heads = head_grad.reshape(head_tokens, head_groups, HD)
    every_keys, every_values = (
        lax.all_gather(head_keys, "rows", axis=0, tiled=True),
        lax.all_gather(head_values, "rows", axis=0, tiled=True),
    )
    every_count = every_keys.shape[0]
    key_heads = every_keys.reshape(every_count, head_groups, HD)
    value_heads = every_values.reshape(every_count, head_groups, HD)
    position = jnp.arange(every_count) % head_tokens
    key_frame = position // coarse_cols
    key_column = position % coarse_cols
    col_limit = jnp.sum(
        jnp.where(key_frame[:, None] == jnp.arange(total_frames)[None, :], valid_cols[None, :], 0),
        axis=1,
    )
    key_ok = key_column * POOL < col_limit
    coarse_scores = (
        jnp.einsum("qhd,khd->hqk", query_heads, key_heads, preferred_element_type=F32)
        * score_scale
    )
    coarse_scores = jnp.where(key_ok[None, None, :], coarse_scores, NEGATIVE)
    log_total = normalize(coarse_scores)
    coarse_weights = jnp.exp(coarse_scores - log_total)
    coarse_low = coarse_weights.astype(BF16)
    coarse_out = jnp.einsum("hqk,khd->qhd", coarse_low, value_heads, preferred_element_type=F32)
    coarse_dot = jnp.sum(grad_heads.astype(F32) * coarse_out, axis=-1)
    coarse_wgrad = jnp.einsum("qhd,khd->hqk", grad_heads, value_heads, preferred_element_type=F32)
    coarse_sgrad = (coarse_weights * (coarse_wgrad - coarse_dot.T[:, :, None])).astype(BF16)
    coarse_qgrad = (
        jnp.einsum("hqk,khd->qhd", coarse_sgrad, key_heads, preferred_element_type=F32)
        * score_scale
    )
    count = head_tokens * lax.axis_size("rows")
    key_part = (
        jnp.einsum("hqk,qhd->khd", coarse_sgrad, query_heads, preferred_element_type=F32)
        * score_scale
    )
    value_part = jnp.einsum("hqk,qhd->khd", coarse_low, grad_heads, preferred_element_type=F32)
    terms = lax.psum_scatter(
        jnp.concatenate(
            [key_part.reshape(count, head_width), value_part.reshape(count, head_width)], axis=1
        ),
        "rows",
        scatter_dimension=0,
        tiled=True,
    )
    total_keys = terms[:, :head_width]
    total_values = terms[:, head_width:]
    out_dims = (head_tokens // coarse_cols, 1, coarse_cols, head_width)
    return (
        coarse_qgrad.reshape(out_dims).astype(BF16),
        total_keys.reshape(out_dims).astype(BF16),
        total_values.reshape(out_dims).astype(BF16),
    ), frame_gain


def local(fine_q, fine_kv, coarse_q, coarse_kv, cotangent, gain_table, timesteps, valid_cols):
    frames, bands = lax.axis_size("frames"), lax.axis_size("rows")
    head_width = coarse_q.shape[-1] // frames
    tokens = coarse_q.shape[-2]
    direct = (
        head_width == cotangent.shape[-1]
        and 4 * tokens * head_width // LANES == 16
        and frames * bands * tokens <= 128
    )
    operands = (coarse_q, coarse_kv, cotangent, gain_table, timesteps, valid_cols)
    fine = (fine_q, fine_kv, cotangent)
    if direct:
        coarse, gain, valid = coarse_direct(*operands)
        grad_q, grad_kv, *coarse_grads = fine_level(coarse, gain, valid, *fine)
        shape = (frames, 1, tokens, head_width)
        return (grad_q, grad_kv, *(x.reshape(shape) for x in coarse_grads))
    coarse_grads, gain = coarse_gathered(*operands)
    valid = valid_cols.reshape(1, -1)
    return (*fine_level(None, gain, valid, *fine), *coarse_grads)


def solution(mesh):
    placed = (
        P("frames", "rows", None, None),
        P("frames", "rows", None, None),
        P("frames", "rows", None, None),
        P("frames", "rows", None, None),
        P("frames", "rows", None, None),
        P(),
        P("frames"),
        P(),
    )
    return jax.shard_map(
        local,
        mesh=mesh,
        in_specs=placed,
        out_specs=(
            P("frames", "rows", None, None),
            P("frames", "rows", None, None),
            P(None, "rows", None, "frames"),
            P(None, "rows", None, "frames"),
            P(None, "rows", None, "frames"),
        ),
        check_vma=False,
    )
```

```python
import functools
import math

import jax
import jax.numpy as jnp
from jax import lax
from jax.experimental import pallas as pl
from jax.experimental.pallas import tpu as pltpu
from jax.sharding import PartitionSpec as P

HD = 64
KERNEL = 7
POOL = 8
LANES = 128

NEGATIVE = -1e30

F32 = jnp.float32
BF16 = jnp.bfloat16


def dot_nt(left, right):
    return lax.dot_general(left, right, (((1,), (1,)), ((), ())), preferred_element_type=F32)


def dot_nn(left, right):
    return jnp.dot(left, right, preferred_element_type=F32)


def iota(shape, dim):
    return lax.broadcasted_iota(jnp.int32, shape, dim)


def pairs_of(table):
    blocks = []
    for lo in range(0, table.shape[1], LANES):
        part = table[:, lo : lo + LANES]
        first = iota(part.shape, 1) < HD
        zero = jnp.zeros_like(part)
        blocks.append(
            jnp.concatenate([jnp.where(first, part, zero), jnp.where(first, zero, part)], axis=0)
        )
    return blocks


def softmax_grads(scores, weight_grad, axis):
    top = jnp.max(scores, axis=axis, keepdims=True)
    raised = jnp.exp(scores - top)
    share = 1.0 / jnp.sum(raised, axis=axis, keepdims=True)
    row_dot = jnp.sum(raised * weight_grad, axis=axis, keepdims=True) * share
    weights = raised * share
    return weights.astype(BF16), (weights * (weight_grad - row_dot)).astype(BF16)


def send_kernel(
    cols, bands, step_ref, valid_hbm, cot_hbm, gain_hbm, cq_hbm, ckv_hbm,
    send_ref, gain_ref, valid_ref, cot_ref, eight_ref, cq_ref, ckv_ref, sems,
):
    step = step_ref[0]
    eight = eight_ref.shape[0]
    first = pl.multiple_of(step // eight * eight, eight)
    gain_copy = pltpu.make_async_copy(gain_hbm.at[pl.ds(first, eight)], eight_ref, sems.at[0])
    copies = [
        pltpu.make_async_copy(source, target, sems.at[1 + at])
        for at, (source, target) in enumerate(
            tuple((cot_hbm.at[pl.ds(r, 32)], cot_ref.at[pl.ds(r, 32)]) for r in range(0, 128, 32)) + ((cq_hbm, cq_ref), (ckv_hbm, ckv_ref), (valid_hbm, valid_ref))
        )
    ]
    for copy in copies[:-1]:
        copy.start()
    gain_copy.start()
    copies[-1].start()
    pixels, width = cot_ref.shape
    tokens, cwidth = cq_ref.shape
    half = POOL // 2
    groups = cwidth // width
    part = iota((groups * tokens, pixels), 0)
    group, token = part // tokens, part % tokens
    pixel = iota((groups * tokens, pixels), 1)
    row, col = pixel // cols, pixel % cols
    inside = (row // half == group // 2) & (col // half == token * 2 + group % 2)
    for copy in copies:
        copy.wait()
    summed = dot_nn(inside.astype(BF16), cot_ref[...])
    query = cq_ref[...].astype(F32)
    both = ckv_ref[...].astype(F32)
    gain_copy.wait()
    gain = eight_ref[pl.ds(step - first, 1), :]
    gain_ref[...] = gain
    pooled = summed * gain
    for g in range(groups):
        lo = g * width
        arrays = (
            query[:, lo : lo + width],
            both[:, lo : lo + width],
            both[:, cwidth + lo : cwidth + lo + width],
            pooled[g * tokens : (g + 1) * tokens, :],
        )
        tile = jnp.concatenate(
            [a[:, b : b + LANES] for a in arrays for b in range(0, width, LANES)], axis=0
        ).astype(BF16)
        height = tile.shape[0]
        for r in range(bands):
            start = (g * bands + r) * height
            send_ref[start : start + height, :] = tile


def valid_here(valid_ref):
    frame = lax.axis_index("frames")
    return sum(
        jnp.where(frame == f, valid_ref[:, f : f + 1], 0) for f in range(valid_ref.shape[1])
    )


def window_bias(shape, cols, valid, key_row, lane_rows, query_row, present=None):
    radius = KERNEL // 2
    place, lane = iota(shape, 0), iota(shape, 1)
    krow, kcol = key_row(place // cols), place % cols
    qrow, qcol = lane // cols % lane_rows + query_row, lane % cols
    seen = (jnp.abs(krow - qrow) <= radius) & (jnp.abs(kcol - qcol) <= radius) & (kcol < valid)
    if present is not None:
        seen = seen & present(krow)
    seen = seen | ((krow == qrow) & (kcol == qcol))
    return jnp.where(seen, 0.0, NEGATIVE)


def partial_sums(scores, weight_grad):
    top = jnp.max(scores, axis=0, keepdims=True)
    raised = jnp.exp(scores - top)
    total = jnp.sum(raised, axis=0, keepdims=True)
    return top, raised, total, jnp.sum(raised * weight_grad, axis=0, keepdims=True)


def completed(kept, scores, weight_grad):
    top_kept, total_kept, dot_kept = kept
    top = jnp.maximum(top_kept, jnp.max(scores, axis=0, keepdims=True))
    factor = jnp.exp(top_kept - top)
    raised = jnp.exp(scores - top)
    total = total_kept * factor + jnp.sum(raised, axis=0, keepdims=True)
    share = jnp.where(total > 0, 1.0 / total, 0.0)
    dot = dot_kept * factor + jnp.sum(raised * weight_grad, axis=0, keepdims=True)
    return factor * share, raised * share, dot * share


def in_parts(row):
    parts = []
    for _ in range(3):
        part = row.astype(BF16).astype(F32)
        parts.append(part)
        row = row - part
    return parts


def prep_kernel(cols, valid_ref, gain_ref, q_ref, kv_ref, cot_ref, near_ref, far_ref, grad_ref):
    radius = KERNEL // 2
    pixels, width = q_ref.shape
    rows = pixels // cols
    one, two = radius * cols, 2 * radius * cols
    scale = 1.0 / math.sqrt(HD)
    even = lax.axis_index("rows") % 2 == 0
    valid = valid_here(valid_ref)
    grad_ref[...] = (gain_ref[...] * cot_ref[...].astype(F32)).astype(BF16)
    pad = jnp.zeros((cols, width), BF16)

    sides = []
    for lo, key_lo, query_row in ((0, 0, 0), (pixels - one, pixels - two, radius)):
        bias = window_bias((two, LANES), cols, valid, lambda at: at, radius + 1, query_row)
        query = pairs_of(jnp.concatenate([q_ref[lo : lo + one, :] * scale, pad], axis=0))
        grad = pairs_of(jnp.concatenate([grad_ref[lo : lo + one, :], pad], axis=0))
        products = []
        for p in range(width // LANES):
            at = p * LANES
            keys = kv_ref[key_lo : key_lo + two, at : at + LANES]
            values = kv_ref[key_lo : key_lo + two, width + at : width + at + LANES]
            products.append((dot_nt(keys, query[p]) + bias, dot_nt(values, grad[p])))
        sides.append(products)

    def sums(products):
        tiles = []
        for scores, wgrad in products:
            top, _, total, dot = partial_sums(scores, wgrad)
            found = [part for row in (top, total, dot) for part in in_parts(row)]
            found.append(jnp.zeros((16 - len(found), LANES), F32))
            tiles.append(jnp.concatenate(found, axis=0))
        return jnp.concatenate(tiles, axis=1).astype(BF16)

    upper, lower = (sums(products) for products in sides)

    def pack(target, lo, found):
        parts = (kv_ref[lo : lo + one, :width], kv_ref[lo : lo + one, width:])
        parts += (q_ref[lo : lo + one, :], grad_ref[lo : lo + one, :])
        for at, part in enumerate(parts):
            target[at * one : (at + 1) * one, :] = part
        target[len(parts) * one :, :] = found

    @pl.when(even)
    def _():
        pack(near_ref, pixels - one, lower)
        pack(far_ref, 0, upper)

    @pl.when(jnp.logical_not(even))
    def _():
        pack(near_ref, 0, upper)
        pack(far_ref, pixels - one, lower)


def plan_kernel(
    cols, valid_ref, q_ref, kv_ref, grad_ref,
    beside_ref, above_ref, below_ref, queries_ref, grads_ref, keys_t_ref, raised_ref, wgrad_ref, sums_ref,
):
    radius = KERNEL // 2
    pixels, width = q_ref.shape
    rows = pixels // cols
    scale = 1.0 / math.sqrt(HD)
    band = lax.axis_index("rows")
    first, last = band == 0, band == lax.axis_size("rows") - 1
    valid = valid_here(valid_ref)

    def present(krow):
        return ((krow >= 0) | jnp.logical_not(first)) & ((krow < rows) | jnp.logical_not(last))

    beside_ref[...] = window_bias(
        beside_ref.shape, cols, valid,
        lambda at: jnp.where(at < radius, at - radius, at - radius + rows), rows, 0, present,
    )
    above_ref[...] = window_bias(
        above_ref.shape, cols, valid, lambda at: at, radius + 1, -radius
    )
    below_ref[...] = window_bias(
        below_ref.shape, cols, valid, lambda at: at + rows - radius, radius + 1, rows
    )
    bias = window_bias((pixels, pixels), cols, valid, lambda at: at, rows, 0)
    bias = jnp.concatenate([bias, bias], axis=1)
    keys_t_ref[...] = kv_ref[:, :width].T
    for p, (query, grad) in enumerate(zip(pairs_of(q_ref[...] * scale), pairs_of(grad_ref[...]))):
        at = p * LANES
        queries_ref[p], grads_ref[p] = query, grad
        wgrad = dot_nt(kv_ref[:, width + at : width + at + LANES], grad)
        top, raised, total, dot = partial_sums(
            dot_nt(kv_ref[:, at : at + LANES], query) + bias, wgrad
        )
        raised_ref[p], wgrad_ref[p] = raised, wgrad
        for row, value in enumerate((top, total, dot)):
            sums_ref[p, row : row + 1, :] = value


def fine_kernel(cols, carried, *refs):
    (kv_ref, near_ref, far_ref, beside_ref, above_ref, below_ref, queries_ref, grads_ref) = refs[:8]
    (keys_t_ref, raised_ref, wgrad_ref, sums_ref) = refs[8:12]
    outs = refs[12 + carried : 14 + 2 * carried]
    dq_ref, dkv_ref, sems = refs[14 + 2 * carried :]
    copies = [
        pltpu.make_async_copy(source, target, sems.at[2 + at])
        for at, (source, target) in enumerate(zip(refs[12 : 12 + carried], outs[2:]))
    ]
    for copy in copies:
        copy.start()
    radius = KERNEL // 2
    pixels, width = dq_ref.shape
    one = radius * cols
    scale = 1.0 / math.sqrt(HD)
    even = lax.axis_index("rows") % 2 == 0

    def received(at):
        rows_at = slice(at * one, (at + 1) * one) if at < 4 else slice(at * one, None)
        near, far = near_ref[rows_at, :], far_ref[rows_at, :]
        return jnp.where(even, far, near), jnp.where(even, near, far)

    def joined(table):
        return jnp.concatenate(table, axis=0)

    beside_keys, beside_values = joined(received(0)), joined(received(1))
    beside_t = beside_keys.T
    pad = jnp.zeros((cols, width), BF16)
    rest = jnp.zeros((pixels - one, LANES), BF16)
    side_lo = (0, pixels - one)
    side_query = [pairs_of(joined([t * scale, pad])) for t in received(2)]
    side_grad = [pairs_of(joined([t, pad])) for t in received(3)]
    side_sums = [t.astype(F32) for t in received(4)]
    beside_bias = jnp.concatenate([beside_ref[...], beside_ref[...]], axis=1)
    pairs = range(width // LANES)
    ats = [slice(p * LANES, (p + 1) * LANES) for p in pairs]
    value_ats = [slice(width + p * LANES, width + (p + 1) * LANES) for p in pairs]
    sides = [(side, p) for side in range(2) for p in pairs]
    beside_scores = [dot_nt(beside_keys[:, ats[p]], queries_ref[p]) + beside_bias for p in pairs]
    beside_wgrad = [dot_nt(beside_values[:, ats[p]], grads_ref[p]) for p in pairs]
    side_scores, side_wgrad = {}, {}
    for side, p in sides:
        keys_at = slice(side_lo[side], side_lo[side] + one)
        bias_ref = (above_ref, below_ref)[side]
        side_scores[side, p] = (
            dot_nt(kv_ref[keys_at, ats[p]], side_query[side][p]) + bias_ref[...]
        )
        side_wgrad[side, p] = dot_nt(kv_ref[keys_at, value_ats[p]], side_grad[side][p])
    lows, sgrads, beside_sgrads = {}, {}, {}
    for p in pairs:
        factor, beside_weights, row_dot = completed(
            tuple(sums_ref[p, row : row + 1, :] for row in range(3)),
            beside_scores[p],
            beside_wgrad[p],
        )
        beside_sgrads[p] = (beside_weights * (beside_wgrad[p] - row_dot)).astype(BF16)
        weights = raised_ref[p] * factor
        lows[p] = weights.astype(BF16)
        sgrads[p] = (weights * (wgrad_ref[p] - row_dot)).astype(BF16)
    for side, p in sides:
        found = side_sums[side][:, ats[p]]
        kept = tuple(
            found[row : row + 1] + found[row + 1 : row + 2] + found[row + 2 : row + 3]
            for row in (0, 3, 6)
        )
        _, weights, row_dot = completed(kept, side_scores[side, p], side_wgrad[side, p])
        order = slice(None, None, -1 if side else 1)
        lows[side, p] = joined([weights.astype(BF16), rest][order])
        sgrad = (weights * (side_wgrad[side, p] - row_dot)).astype(BF16)
        sgrads[side, p] = joined([sgrad, rest][order])
    for p in pairs:
        dq_t = dot_nn(keys_t_ref[ats[p], :], sgrads[p]) + dot_nn(beside_t[ats[p]], beside_sgrads[p])
        dq_t = joined([dq_t[:HD, :pixels], dq_t[HD:, pixels:]])
        dq_ref[:, ats[p]] = (dq_t * scale).astype(BF16).T
    for p in pairs:
        dkv_ref[:, ats[p]] = dot_nn(
            jnp.concatenate([sgrads[p], sgrads[0, p], sgrads[1, p]], axis=1),
            joined([queries_ref[p], side_query[0][p], side_query[1][p]]),
        ).astype(BF16)
        dkv_ref[:, value_ats[p]] = dot_nn(
            jnp.concatenate([lows[p], lows[0, p], lows[1, p]], axis=1),
            joined([grads_ref[p], side_grad[0][p], side_grad[1][p]]),
        ).astype(BF16)
    copies += [
        pltpu.make_async_copy(source, target, sems.at[at])
        for at, (source, target) in enumerate(((dq_ref, outs[0]), (dkv_ref, outs[1])))
    ]
    for copy in copies[carried:]:
        copy.start()
    for copy in copies:
        copy.wait()


def coarse_kernel(frames, tokens, valid_ref, x_ref, dq_ref, dk_ref, dv_ref, wide, low_ref, sg_ref):
    bands = lax.axis_size("rows")
    width = dq_ref.shape[-1]
    parts = width // LANES
    height = x_ref.shape[0] // (frames * bands)
    band = lax.axis_index("rows")
    scale = 1.0 / math.sqrt(HD)
    wide[...] = x_ref[...].astype(F32)
    devices, own = frames * bands, frames * tokens

    def every(array, b):
        first = (array * parts + b) * tokens
        return jnp.concatenate(
            [wide[pl.ds(first + t, devices, stride=height), :] for t in range(tokens)], axis=0
        ).astype(BF16)

    def mine(array, b):
        first = band * height + (array * parts + b) * tokens
        return jnp.concatenate(
            [wide[pl.ds(first + f * bands * height, tokens), :] for f in range(frames)], axis=0
        ).astype(BF16)

    count = devices * tokens

    def key_bias(shape, dim):
        place = iota(shape, dim)
        token, frame = place // devices, place // bands % frames
        limit = jnp.zeros(shape, jnp.int32)
        for f in range(frames):
            limit = jnp.where(frame == f, valid_ref[:, f : f + 1], limit)
        return jnp.where(token * POOL < limit, 0.0, NEGATIVE)

    bias, own_bias = key_bias((count, 2 * count), 0), key_bias((2 * own, count), 1)
    halves = range(parts)
    keys, values = ([every(a, b) for b in halves] for a in (1, 2))
    queries, grads = ([pairs_of(every(a, b))[0] for b in halves] for a in (0, 3))
    queries = [query * scale for query in queries]
    own_queries = [pairs_of(mine(0, b) * scale)[0] for b in halves]
    own_grads = [pairs_of(mine(3, b))[0] for b in halves]
    scores = [dot_nt(keys[b], queries[b]) + bias for b in halves]
    wgrads = [dot_nt(values[b], grads[b]) for b in halves]
    own_scores = [dot_nt(own_queries[b], keys[b]) + own_bias for b in halves]
    own_wgrads = [dot_nt(own_grads[b], values[b]) for b in halves]
    found = [softmax_grads(scores[b], wgrads[b], 0) for b in halves]
    own_sgrads = [softmax_grads(own_scores[b], own_wgrads[b], 1)[1] for b in halves]
    for b in halves:
        low_ref[b], sg_ref[b] = found[b][0].astype(F32), found[b][1].astype(F32)

    def mine_rows(ref, b):
        pieces = [
            ref[b, pl.ds(t * devices + f * bands + band, 1), :]
            for f in range(frames)
            for t in range(tokens)
        ]
        return jnp.concatenate(pieces, axis=0).astype(BF16)

    for b in halves:
        full = dot_nn(own_sgrads[b], keys[b])
        dq = jnp.where(iota((own, LANES), 1) < HD, full[:own], full[own:]) * scale
        dk = dot_nn(mine_rows(sg_ref, b), queries[b])
        dv = dot_nn(mine_rows(low_ref, b), grads[b])
        for ref, table in ((dq_ref, dq), (dk_ref, dk), (dv_ref, dv)):
            rounded = table.astype(BF16)
            for f in range(frames):
                ref[f, :, b * LANES : (b + 1) * LANES] = rounded[f * tokens : (f + 1) * tokens]


def vmem():
    return pl.BlockSpec(memory_space=pltpu.VMEM)


def smem():
    return pl.BlockSpec(memory_space=pltpu.SMEM)


def hbm():
    return pl.BlockSpec(memory_space=pltpu.HBM)


def in_hbm(array):
    return pltpu.with_memory_space_constraint(array, pltpu.HBM)


def params():
    return pltpu.CompilerParams(vmem_limit_bytes=16 * 2**20)


def out(shape, dtype=BF16):
    return jax.ShapeDtypeStruct(shape, dtype)


def fine_level(carried, gain, valid, fine_q, fine_kv, cotangent):
    bands = lax.axis_size("rows")
    _, rows, cols, width = fine_q.shape
    pixels = rows * cols
    radius = KERNEL // 2
    query = fine_q.reshape(pixels, width)
    key_value = fine_kv.reshape(pixels, 2 * width)
    cot = cotangent.reshape(pixels, width)
    one, sums = radius * cols, 16
    packed = (4 * one + sums, width)
    near, far, grad = pl.pallas_call(
        functools.partial(prep_kernel, cols),
        in_specs=[vmem()] * 5,
        out_specs=[vmem()] * 3,
        out_shape=[out(packed), out(packed), out((pixels, width))],
        compiler_params=params(),
    )(valid, gain, query, key_value, cot)
    pairs = [(i, i ^ 1) for i in range(bands) if i ^ 1 < bands]
    others = [(i, ((i + 1) ^ 1) - 1) for i in range(1, bands) if ((i + 1) ^ 1) - 1 < bands]
    near = lax.ppermute(near, "rows", pairs)
    far = lax.ppermute(far, "rows", others)
    count = width // LANES
    plan = pl.pallas_call(
        functools.partial(plan_kernel, cols),
        in_specs=[vmem()] * 4,
        out_specs=[vmem()] * 9,
        out_shape=[
            out((2 * one, pixels), F32),
            out((one, LANES), F32),
            out((one, LANES), F32),
            out((count, 2 * pixels, LANES)),
            out((count, 2 * pixels, LANES)),
            out((width, pixels)),
            out((count, pixels, 2 * pixels), F32),
            out((count, pixels, 2 * pixels), F32),
            out((count, 8, 2 * pixels), F32),
        ],
        compiler_params=params(),
    )(valid, query, key_value, grad)
    grads = pl.pallas_call(
        functools.partial(fine_kernel, cols, len(carried)),
        in_specs=[vmem()] * (12 + len(carried)),
        out_specs=[hbm()] * (2 + len(carried)),
        out_shape=[out((pixels, width)), out((pixels, 2 * width))]
        + [out(x.shape) for x in carried],
        scratch_shapes=[
            pltpu.VMEM((pixels, width), BF16),
            pltpu.VMEM((pixels, 2 * width), BF16),
            pltpu.SemaphoreType.DMA((2 + len(carried),)),
        ],
        compiler_params=params(),
        cost_estimate=pl.CostEstimate(flops=400_000_000, bytes_accessed=1_000_000, transcendentals=300_000),
    )(key_value, near, far, *plan, *carried)
    return (grads[0].reshape(fine_q.shape), grads[1].reshape(fine_kv.shape), *grads[2:])


def coarse_direct(coarse_q, coarse_kv, cotangent, gain_table, timesteps, valid_cols):
    frames, bands = lax.axis_size("frames"), lax.axis_size("rows")
    _, rows, cols, width = cotangent.shape
    tokens, cwidth = coarse_q.shape[-2:]
    head_width = cwidth // frames
    tile = 4 * tokens * head_width // LANES
    sent, gain, valid = pl.pallas_call(
        functools.partial(send_kernel, cols, bands),
        in_specs=[smem()] + [hbm()] * 5,
        out_specs=[vmem()] * 3,
        out_shape=[
            out((frames * bands * tile, LANES)),
            out((1, width), F32),
            out((1, frames), jnp.int32),
        ],
        scratch_shapes=[
            pltpu.VMEM((rows * cols, width), BF16),
            pltpu.VMEM((8, width), F32),
            pltpu.VMEM((tokens, cwidth), BF16),
            pltpu.VMEM((tokens, 2 * cwidth), BF16),
            pltpu.SemaphoreType.DMA((8,)),
        ],
        compiler_params=params(),
    )(
        timesteps,
        in_hbm(valid_cols.reshape(1, -1)),
        in_hbm(cotangent.reshape(rows * cols, width)),
        in_hbm(gain_table),
        in_hbm(coarse_q.reshape(tokens, cwidth)),
        in_hbm(coarse_kv.reshape(tokens, 2 * cwidth)),
    )
    held = lax.all_to_all(
        sent.reshape(frames * bands, tile, LANES),
        ("frames", "rows"),
        split_axis=0,
        concat_axis=0,
        tiled=True,
    ).reshape(frames * bands * tile, LANES)
    count = frames * bands * tokens
    outs = pl.pallas_call(
        functools.partial(coarse_kernel, frames, tokens),
        in_specs=[vmem()] * 2,
        out_specs=[vmem()] * 3,
        out_shape=[out((frames, tokens, head_width))] * 3,
        scratch_shapes=[
            pltpu.VMEM(held.shape, F32),
            pltpu.VMEM((head_width // LANES, count, 2 * count), F32),
            pltpu.VMEM((head_width // LANES, count, 2 * count), F32),
        ],
        compiler_params=params(),
        cost_estimate=pl.CostEstimate(flops=100_000_000_000, bytes_accessed=100_000_000, transcendentals=0),
    )(valid, held)
    return outs, gain, valid


def normalize(scores):
    row_max = jnp.max(scores, axis=-1, keepdims=True)
    return row_max + jnp.log(jnp.sum(jnp.exp(scores - row_max), axis=-1, keepdims=True))


def coarse_gathered(coarse_q, coarse_kv, cotangent, gain_table, timesteps, valid_cols):
    score_scale = 1.0 / math.sqrt(HD)
    frames_here, _, cols_here, fine_width = cotangent.shape
    total_frames = valid_cols.shape[0]
    steps_all = gain_table.shape[0]
    select = (timesteps[:, None] == jnp.arange(steps_all)[None, :]).astype(F32)
    frame_gain = jnp.dot(select, gain_table, precision=lax.Precision.HIGHEST)
    scaled_grad = frame_gain[:, None, None, :] * cotangent.astype(F32)
    half_pool = POOL // 2
    coarse_cols = cols_here // POOL
    coarse_width = coarse_q.shape[-1]
    coarse_count = frames_here * coarse_cols
    blocks = scaled_grad.reshape(frames_here, 2, half_pool, coarse_cols, 2, half_pool, fine_width)
    pooled = (
        jnp.sum(blocks, axis=(2, 5))
        .transpose(0, 2, 1, 3, 4)
        .reshape(coarse_count, coarse_width)
        .astype(BF16)
    )
    mine_query = coarse_q.reshape(coarse_count, coarse_width)
    mine_keys = coarse_kv[..., :coarse_width].reshape(coarse_count, coarse_width)
    mine_values = coarse_kv[..., coarse_width:].reshape(coarse_count, coarse_width)
    head_query, head_keys, head_values, head_grad = (
        lax.all_to_all(mine_query, "frames", split_axis=1, concat_axis=0, tiled=True),
        lax.all_to_all(mine_keys, "frames", split_axis=1, concat_axis=0, tiled=True),
        lax.all_to_all(mine_values, "frames", split_axis=1, concat_axis=0, tiled=True),
        lax.all_to_all(pooled, "frames", split_axis=1, concat_axis=0, tiled=True),
    )
    head_tokens, head_width = head_query.shape
    head_groups = head_width // HD
    query_heads = head_query.reshape(head_tokens, head_groups, HD)
    grad_heads = head_grad.reshape(head_tokens, head_groups, HD)
    every_keys, every_values = (
        lax.all_gather(head_keys, "rows", axis=0, tiled=True),
        lax.all_gather(head_values, "rows", axis=0, tiled=True),
    )
    every_count = every_keys.shape[0]
    key_heads = every_keys.reshape(every_count, head_groups, HD)
    value_heads = every_values.reshape(every_count, head_groups, HD)
    position = jnp.arange(every_count) % head_tokens
    key_frame = position // coarse_cols
    key_column = position % coarse_cols
    col_limit = jnp.sum(
        jnp.where(key_frame[:, None] == jnp.arange(total_frames)[None, :], valid_cols[None, :], 0),
        axis=1,
    )
    key_ok = key_column * POOL < col_limit
    coarse_scores = (
        jnp.einsum("qhd,khd->hqk", query_heads, key_heads, preferred_element_type=F32)
        * score_scale
    )
    coarse_scores = jnp.where(key_ok[None, None, :], coarse_scores, NEGATIVE)
    log_total = normalize(coarse_scores)
    coarse_weights = jnp.exp(coarse_scores - log_total)
    coarse_low = coarse_weights.astype(BF16)
    coarse_out = jnp.einsum("hqk,khd->qhd", coarse_low, value_heads, preferred_element_type=F32)
    coarse_dot = jnp.sum(grad_heads.astype(F32) * coarse_out, axis=-1)
    coarse_wgrad = jnp.einsum("qhd,khd->hqk", grad_heads, value_heads, preferred_element_type=F32)
    coarse_sgrad = (coarse_weights * (coarse_wgrad - coarse_dot.T[:, :, None])).astype(BF16)
    coarse_qgrad = (
        jnp.einsum("hqk,khd->qhd", coarse_sgrad, key_heads, preferred_element_type=F32)
        * score_scale
    )
    count = head_tokens * lax.axis_size("rows")
    key_part = (
        jnp.einsum("hqk,qhd->khd", coarse_sgrad, query_heads, preferred_element_type=F32)
        * score_scale
    )
    value_part = jnp.einsum("hqk,qhd->khd", coarse_low, grad_heads, preferred_element_type=F32)
    terms = lax.psum_scatter(
        jnp.concatenate(
            [key_part.reshape(count, head_width), value_part.reshape(count, head_width)], axis=1
        ),
        "rows",
        scatter_dimension=0,
        tiled=True,
    )
    total_keys = terms[:, :head_width]
    total_values = terms[:, head_width:]
    out_dims = (head_tokens // coarse_cols, 1, coarse_cols, head_width)
    return (
        coarse_qgrad.reshape(out_dims).astype(BF16),
        total_keys.reshape(out_dims).astype(BF16),
        total_values.reshape(out_dims).astype(BF16),
    ), frame_gain


def local(fine_q, fine_kv, coarse_q, coarse_kv, cotangent, gain_table, timesteps, valid_cols):
    frames, bands = lax.axis_size("frames"), lax.axis_size("rows")
    head_width = coarse_q.shape[-1] // frames
    tokens = coarse_q.shape[-2]
    direct = (
        head_width == cotangent.shape[-1]
        and 4 * tokens * head_width // LANES == 16
        and frames * bands * tokens <= 128
    )
    operands = (coarse_q, coarse_kv, cotangent, gain_table, timesteps, valid_cols)
    fine = (fine_q, fine_kv, cotangent)
    if direct:
        carried, gain, valid = coarse_direct(*operands)
        grad_q, grad_kv, *coarse_grads = fine_level(carried, gain, valid, *fine)
        shape = (frames, 1, tokens, head_width)
        return (grad_q, grad_kv, *(x.reshape(shape) for x in coarse_grads))
    coarse_grads, gain = coarse_gathered(*operands)
    return (*fine_level([], gain, valid_cols.reshape(1, -1), *fine), *coarse_grads)


def solution(mesh):
    placed = (
        P("frames", "rows", None, None),
        P("frames", "rows", None, None),
        P("frames", "rows", None, None),
        P("frames", "rows", None, None),
        P("frames", "rows", None, None),
        P(),
        P("frames"),
        P(),
    )
    return jax.shard_map(
        local,
        mesh=mesh,
        in_specs=placed,
        out_specs=(
            P("frames", "rows", None, None),
            P("frames", "rows", None, None),
            P(None, "rows", None, "frames"),
            P(None, "rows", None, "frames"),
            P(None, "rows", None, "frames"),
        ),
        check_vma=False,
    )
```

```python
import functools
import math

import jax
import jax.numpy as jnp
from jax import lax
from jax.experimental import pallas as pl
from jax.experimental.pallas import tpu as pltpu
from jax.sharding import PartitionSpec as P

HD = 64
KERNEL = 7
POOL = 8
LANES = 128

NEGATIVE = -1e30

F32 = jnp.float32
BF16 = jnp.bfloat16


def dot_nt(left, right):
    return lax.dot_general(left, right, (((1,), (1,)), ((), ())), preferred_element_type=F32)


def dot_nn(left, right):
    return jnp.dot(left, right, preferred_element_type=F32)


def iota(shape, dim):
    return lax.broadcasted_iota(jnp.int32, shape, dim)


def pairs_of(table):
    blocks = []
    for lo in range(0, table.shape[1], LANES):
        part = table[:, lo : lo + LANES]
        first = iota(part.shape, 1) < HD
        zero = jnp.zeros_like(part)
        blocks.append(
            jnp.concatenate([jnp.where(first, part, zero), jnp.where(first, zero, part)], axis=0)
        )
    return blocks


def softmax_grads(scores, weight_grad, axis):
    top = jnp.max(scores, axis=axis, keepdims=True)
    raised = jnp.exp(scores - top)
    share = 1.0 / jnp.sum(raised, axis=axis, keepdims=True)
    row_dot = jnp.sum(raised * weight_grad, axis=axis, keepdims=True) * share
    weights = raised * share
    return weights.astype(BF16), (weights * (weight_grad - row_dot)).astype(BF16)


def send_kernel(
    cols, bands, step_ref, valid_hbm, cot_hbm, gain_hbm, cq_hbm, ckv_hbm,
    send_ref, gain_ref, valid_ref, cot_ref, eight_ref, cq_ref, ckv_ref, sems,
):
    step = step_ref[0]
    eight = eight_ref.shape[0]
    first = pl.multiple_of(step // eight * eight, eight)
    gain_copy = pltpu.make_async_copy(gain_hbm.at[pl.ds(first, eight)], eight_ref, sems.at[0])
    copies = [
        pltpu.make_async_copy(source, target, sems.at[1 + at])
        for at, (source, target) in enumerate(
            tuple((cot_hbm.at[pl.ds(r, 32)], cot_ref.at[pl.ds(r, 32)]) for r in range(0, 128, 32)) + ((cq_hbm, cq_ref), (ckv_hbm, ckv_ref), (valid_hbm, valid_ref))
        )
    ]
    for copy in copies[:-1]:
        copy.start()
    gain_copy.start()
    copies[-1].start()
    pixels, width = cot_ref.shape
    tokens, cwidth = cq_ref.shape
    half = POOL // 2
    groups = cwidth // width
    part = iota((groups * tokens, pixels), 0)
    group, token = part // tokens, part % tokens
    pixel = iota((groups * tokens, pixels), 1)
    row, col = pixel // cols, pixel % cols
    inside = (row // half == group // 2) & (col // half == token * 2 + group % 2)
    for copy in copies[-3:]:
        copy.wait()
    query = cq_ref[...].astype(F32)
    both = ckv_ref[...].astype(F32)
    for copy in copies[:-3]:
        copy.wait()
    summed = dot_nn(inside.astype(BF16), cot_ref[...])
    gain_copy.wait()
    gain = eight_ref[pl.ds(step - first, 1), :]
    gain_ref[...] = gain
    pooled = summed * gain
    for g in range(groups):
        lo = g * width
        arrays = (
            query[:, lo : lo + width],
            both[:, lo : lo + width],
            both[:, cwidth + lo : cwidth + lo + width],
            pooled[g * tokens : (g + 1) * tokens, :],
        )
        tile = jnp.concatenate(
            [a[:, b : b + LANES] for a in arrays for b in range(0, width, LANES)], axis=0
        ).astype(BF16)
        height = tile.shape[0]
        for r in range(bands):
            start = (g * bands + r) * height
            send_ref[start : start + height, :] = tile


def valid_here(valid_ref):
    frame = lax.axis_index("frames")
    return sum(
        jnp.where(frame == f, valid_ref[:, f : f + 1], 0) for f in range(valid_ref.shape[1])
    )


def window_bias(shape, cols, valid, key_row, lane_rows, query_row, present=None):
    radius = KERNEL // 2
    place, lane = iota(shape, 0), iota(shape, 1)
    krow, kcol = key_row(place // cols), place % cols
    qrow, qcol = lane // cols % lane_rows + query_row, lane % cols
    seen = (jnp.abs(krow - qrow) <= radius) & (jnp.abs(kcol - qcol) <= radius) & (kcol < valid)
    if present is not None:
        seen = seen & present(krow)
    seen = seen | ((krow == qrow) & (kcol == qcol))
    return jnp.where(seen, 0.0, NEGATIVE)


def partial_sums(scores, weight_grad):
    top = jnp.max(scores, axis=0, keepdims=True)
    raised = jnp.exp(scores - top)
    total = jnp.sum(raised, axis=0, keepdims=True)
    return top, raised, total, jnp.sum(raised * weight_grad, axis=0, keepdims=True)


def completed(kept, scores, weight_grad):
    top_kept, total_kept, dot_kept = kept
    top = jnp.maximum(top_kept, jnp.max(scores, axis=0, keepdims=True))
    factor = jnp.exp(top_kept - top)
    raised = jnp.exp(scores - top)
    total = total_kept * factor + jnp.sum(raised, axis=0, keepdims=True)
    share = jnp.where(total > 0, 1.0 / total, 0.0)
    dot = dot_kept * factor + jnp.sum(raised * weight_grad, axis=0, keepdims=True)
    return factor * share, raised * share, dot * share


def in_parts(row):
    parts = []
    for _ in range(3):
        part = row.astype(BF16).astype(F32)
        parts.append(part)
        row = row - part
    return parts


def prep_kernel(cols, valid_ref, gain_ref, q_ref, kv_ref, cot_ref, near_ref, far_ref, grad_ref):
    radius = KERNEL // 2
    pixels, width = q_ref.shape
    rows = pixels // cols
    one, two = radius * cols, 2 * radius * cols
    scale = 1.0 / math.sqrt(HD)
    even = lax.axis_index("rows") % 2 == 0
    valid = valid_here(valid_ref)
    grad_ref[...] = (gain_ref[...] * cot_ref[...].astype(F32)).astype(BF16)
    pad = jnp.zeros((cols, width), BF16)

    sides = []
    for lo, key_lo, query_row in ((0, 0, 0), (pixels - one, pixels - two, radius)):
        bias = window_bias((two, LANES), cols, valid, lambda at: at, radius + 1, query_row)
        query = pairs_of(jnp.concatenate([q_ref[lo : lo + one, :] * scale, pad], axis=0))
        grad = pairs_of(jnp.concatenate([grad_ref[lo : lo + one, :], pad], axis=0))
        products = []
        for p in range(width // LANES):
            at = p * LANES
            keys = kv_ref[key_lo : key_lo + two, at : at + LANES]
            values = kv_ref[key_lo : key_lo + two, width + at : width + at + LANES]
            products.append((dot_nt(keys, query[p]) + bias, dot_nt(values, grad[p])))
        sides.append(products)

    def sums(products):
        tiles = []
        for scores, wgrad in products:
            top, _, total, dot = partial_sums(scores, wgrad)
            found = [part for row in (top, total, dot) for part in in_parts(row)]
            found.append(jnp.zeros((16 - len(found), LANES), F32))
            tiles.append(jnp.concatenate(found, axis=0))
        return jnp.concatenate(tiles, axis=1).astype(BF16)

    upper, lower = (sums(products) for products in sides)

    def pack(target, lo, found):
        parts = (kv_ref[lo : lo + one, :width], kv_ref[lo : lo + one, width:])
        parts += (q_ref[lo : lo + one, :], grad_ref[lo : lo + one, :])
        for at, part in enumerate(parts):
            target[at * one : (at + 1) * one, :] = part
        target[len(parts) * one :, :] = found

    @pl.when(even)
    def _():
        pack(near_ref, pixels - one, lower)
        pack(far_ref, 0, upper)

    @pl.when(jnp.logical_not(even))
    def _():
        pack(near_ref, 0, upper)
        pack(far_ref, pixels - one, lower)


def plan_kernel(
    cols, valid_ref, q_ref, kv_ref, grad_ref,
    beside_ref, above_ref, below_ref, queries_ref, grads_ref, keys_t_ref, raised_ref, wgrad_ref, sums_ref,
):
    radius = KERNEL // 2
    pixels, width = q_ref.shape
    rows = pixels // cols
    scale = 1.0 / math.sqrt(HD)
    band = lax.axis_index("rows")
    first, last = band == 0, band == lax.axis_size("rows") - 1
    valid = valid_here(valid_ref)

    def present(krow):
        return ((krow >= 0) | jnp.logical_not(first)) & ((krow < rows) | jnp.logical_not(last))

    beside_ref[...] = window_bias(
        beside_ref.shape, cols, valid,
        lambda at: jnp.where(at < radius, at - radius, at - radius + rows), rows, 0, present,
    )
    above_ref[...] = window_bias(
        above_ref.shape, cols, valid, lambda at: at, radius + 1, -radius
    )
    below_ref[...] = window_bias(
        below_ref.shape, cols, valid, lambda at: at + rows - radius, radius + 1, rows
    )
    bias = window_bias((pixels, pixels), cols, valid, lambda at: at, rows, 0)
    bias = jnp.concatenate([bias, bias], axis=1)
    keys_t_ref[...] = kv_ref[:, :width].T
    for p, (query, grad) in enumerate(zip(pairs_of(q_ref[...] * scale), pairs_of(grad_ref[...]))):
        at = p * LANES
        queries_ref[p], grads_ref[p] = query, grad
        wgrad = dot_nt(kv_ref[:, width + at : width + at + LANES], grad)
        top, raised, total, dot = partial_sums(
            dot_nt(kv_ref[:, at : at + LANES], query) + bias, wgrad
        )
        raised_ref[p], wgrad_ref[p] = raised, wgrad
        for row, value in enumerate((top, total, dot)):
            sums_ref[p, row : row + 1, :] = value


def fine_kernel(cols, carried, *refs):
    (kv_ref, near_ref, far_ref, beside_ref, above_ref, below_ref, queries_ref, grads_ref) = refs[:8]
    (keys_t_ref, raised_ref, wgrad_ref, sums_ref) = refs[8:12]
    outs = refs[12 + carried : 14 + 2 * carried]
    dq_ref, dkv_ref, sems = refs[14 + 2 * carried :]
    copies = [
        pltpu.make_async_copy(source, target, sems.at[2 + at])
        for at, (source, target) in enumerate(zip(refs[12 : 12 + carried], outs[2:]))
    ]
    for copy in copies:
        copy.start()
    radius = KERNEL // 2
    pixels, width = dq_ref.shape
    one = radius * cols
    scale = 1.0 / math.sqrt(HD)
    even = lax.axis_index("rows") % 2 == 0

    def received(at):
        rows_at = slice(at * one, (at + 1) * one) if at < 4 else slice(at * one, None)
        near, far = near_ref[rows_at, :], far_ref[rows_at, :]
        return jnp.where(even, far, near), jnp.where(even, near, far)

    def joined(table):
        return jnp.concatenate(table, axis=0)

    beside_keys, beside_values = joined(received(0)), joined(received(1))
    beside_t = beside_keys.T
    pad = jnp.zeros((cols, width), BF16)
    rest = jnp.zeros((pixels - one, LANES), BF16)
    side_lo = (0, pixels - one)
    side_query = [pairs_of(joined([t * scale, pad])) for t in received(2)]
    side_grad = [pairs_of(joined([t, pad])) for t in received(3)]
    side_sums = [t.astype(F32) for t in received(4)]
    beside_bias = jnp.concatenate([beside_ref[...], beside_ref[...]], axis=1)
    pairs = range(width // LANES)
    ats = [slice(p * LANES, (p + 1) * LANES) for p in pairs]
    value_ats = [slice(width + p * LANES, width + (p + 1) * LANES) for p in pairs]
    sides = [(side, p) for side in range(2) for p in pairs]
    beside_scores = [dot_nt(beside_keys[:, ats[p]], queries_ref[p]) + beside_bias for p in pairs]
    beside_wgrad = [dot_nt(beside_values[:, ats[p]], grads_ref[p]) for p in pairs]
    side_scores, side_wgrad = {}, {}
    for side, p in sides:
        keys_at = slice(side_lo[side], side_lo[side] + one)
        bias_ref = (above_ref, below_ref)[side]
        side_scores[side, p] = (
            dot_nt(kv_ref[keys_at, ats[p]], side_query[side][p]) + bias_ref[...]
        )
        side_wgrad[side, p] = dot_nt(kv_ref[keys_at, value_ats[p]], side_grad[side][p])
    lows, sgrads, beside_sgrads = {}, {}, {}
    for p in pairs:
        factor, beside_weights, row_dot = completed(
            tuple(sums_ref[p, row : row + 1, :] for row in range(3)),
            beside_scores[p],
            beside_wgrad[p],
        )
        beside_sgrads[p] = (beside_weights * (beside_wgrad[p] - row_dot)).astype(BF16)
        weights = raised_ref[p] * factor
        lows[p] = weights.astype(BF16)
        sgrads[p] = (weights * (wgrad_ref[p] - row_dot)).astype(BF16)
    for side, p in sides:
        found = side_sums[side][:, ats[p]]
        kept = tuple(
            found[row : row + 1] + found[row + 1 : row + 2] + found[row + 2 : row + 3]
            for row in (0, 3, 6)
        )
        _, weights, row_dot = completed(kept, side_scores[side, p], side_wgrad[side, p])
        order = slice(None, None, -1 if side else 1)
        lows[side, p] = joined([weights.astype(BF16), rest][order])
        sgrad = (weights * (side_wgrad[side, p] - row_dot)).astype(BF16)
        sgrads[side, p] = joined([sgrad, rest][order])
    for p in pairs:
        dq_t = dot_nn(keys_t_ref[ats[p], :], sgrads[p]) + dot_nn(beside_t[ats[p]], beside_sgrads[p])
        dq_t = joined([dq_t[:HD, :pixels], dq_t[HD:, pixels:]])
        dq_ref[:, ats[p]] = (dq_t * scale).astype(BF16).T
    for p in pairs:
        dkv_ref[:, ats[p]] = dot_nn(
            jnp.concatenate([sgrads[p], sgrads[0, p], sgrads[1, p]], axis=1),
            joined([queries_ref[p], side_query[0][p], side_query[1][p]]),
        ).astype(BF16)
        dkv_ref[:, value_ats[p]] = dot_nn(
            jnp.concatenate([lows[p], lows[0, p], lows[1, p]], axis=1),
            joined([grads_ref[p], side_grad[0][p], side_grad[1][p]]),
        ).astype(BF16)
    copies += [
        pltpu.make_async_copy(source, target, sems.at[at])
        for at, (source, target) in enumerate(((dq_ref, outs[0]), (dkv_ref, outs[1])))
    ]
    for copy in copies[carried:]:
        copy.start()
    for copy in copies:
        copy.wait()


def coarse_kernel(frames, tokens, valid_ref, x_ref, dq_ref, dk_ref, dv_ref, wide, low_ref, sg_ref):
    bands = lax.axis_size("rows")
    width = dq_ref.shape[-1]
    parts = width // LANES
    height = x_ref.shape[0] // (frames * bands)
    band = lax.axis_index("rows")
    scale = 1.0 / math.sqrt(HD)
    wide[...] = x_ref[...].astype(F32)
    devices, own = frames * bands, frames * tokens

    def every(array, b):
        first = (array * parts + b) * tokens
        return jnp.concatenate(
            [wide[pl.ds(first + t, devices, stride=height), :] for t in range(tokens)], axis=0
        ).astype(BF16)

    def mine(array, b):
        first = band * height + (array * parts + b) * tokens
        return jnp.concatenate(
            [wide[pl.ds(first + f * bands * height, tokens), :] for f in range(frames)], axis=0
        ).astype(BF16)

    count = devices * tokens

    def key_bias(shape, dim):
        place = iota(shape, dim)
        token, frame = place // devices, place // bands % frames
        limit = jnp.zeros(shape, jnp.int32)
        for f in range(frames):
            limit = jnp.where(frame == f, valid_ref[:, f : f + 1], limit)
        return jnp.where(token * POOL < limit, 0.0, NEGATIVE)

    bias, own_bias = key_bias((count, 2 * count), 0), key_bias((2 * own, count), 1)
    halves = range(parts)
    keys, values = ([every(a, b) for b in halves] for a in (1, 2))
    queries, grads = ([pairs_of(every(a, b))[0] for b in halves] for a in (0, 3))
    queries = [query * scale for query in queries]
    own_queries = [pairs_of(mine(0, b) * scale)[0] for b in halves]
    own_grads = [pairs_of(mine(3, b))[0] for b in halves]
    scores = [dot_nt(keys[b], queries[b]) + bias for b in halves]
    wgrads = [dot_nt(values[b], grads[b]) for b in halves]
    own_scores = [dot_nt(own_queries[b], keys[b]) + own_bias for b in halves]
    own_wgrads = [dot_nt(own_grads[b], values[b]) for b in halves]
    found = [softmax_grads(scores[b], wgrads[b], 0) for b in halves]
    own_sgrads = [softmax_grads(own_scores[b], own_wgrads[b], 1)[1] for b in halves]
    for b in halves:
        low_ref[b], sg_ref[b] = found[b][0].astype(F32), found[b][1].astype(F32)

    def mine_rows(ref, b):
        pieces = [
            ref[b, pl.ds(t * devices + f * bands + band, 1), :]
            for f in range(frames)
            for t in range(tokens)
        ]
        return jnp.concatenate(pieces, axis=0).astype(BF16)

    for b in halves:
        full = dot_nn(own_sgrads[b], keys[b])
        dq = jnp.where(iota((own, LANES), 1) < HD, full[:own], full[own:]) * scale
        dk = dot_nn(mine_rows(sg_ref, b), queries[b])
        dv = dot_nn(mine_rows(low_ref, b), grads[b])
        for ref, table in ((dq_ref, dq), (dk_ref, dk), (dv_ref, dv)):
            rounded = table.astype(BF16)
            for f in range(frames):
                ref[f, :, b * LANES : (b + 1) * LANES] = rounded[f * tokens : (f + 1) * tokens]


def vmem():
    return pl.BlockSpec(memory_space=pltpu.VMEM)


def smem():
    return pl.BlockSpec(memory_space=pltpu.SMEM)


def hbm():
    return pl.BlockSpec(memory_space=pltpu.HBM)


def in_hbm(array):
    return pltpu.with_memory_space_constraint(array, pltpu.HBM)


def params():
    return pltpu.CompilerParams(vmem_limit_bytes=16 * 2**20)


def out(shape, dtype=BF16):
    return jax.ShapeDtypeStruct(shape, dtype)


def fine_level(carried, gain, valid, fine_q, fine_kv, cotangent):
    bands = lax.axis_size("rows")
    _, rows, cols, width = fine_q.shape
    pixels = rows * cols
    radius = KERNEL // 2
    query = fine_q.reshape(pixels, width)
    key_value = fine_kv.reshape(pixels, 2 * width)
    cot = cotangent.reshape(pixels, width)
    one, sums = radius * cols, 16
    packed = (4 * one + sums, width)
    near, far, grad = pl.pallas_call(
        functools.partial(prep_kernel, cols),
        in_specs=[vmem()] * 5,
        out_specs=[vmem()] * 3,
        out_shape=[out(packed), out(packed), out((pixels, width))],
        compiler_params=params(),
    )(valid, gain, query, key_value, cot)
    pairs = [(i, i ^ 1) for i in range(bands) if i ^ 1 < bands]
    others = [(i, ((i + 1) ^ 1) - 1) for i in range(1, bands) if ((i + 1) ^ 1) - 1 < bands]
    near = lax.ppermute(near, "rows", pairs)
    far = lax.ppermute(far, "rows", others)
    count = width // LANES
    plan = pl.pallas_call(
        functools.partial(plan_kernel, cols),
        in_specs=[vmem()] * 4,
        out_specs=[vmem()] * 9,
        out_shape=[
            out((2 * one, pixels), F32),
            out((one, LANES), F32),
            out((one, LANES), F32),
            out((count, 2 * pixels, LANES)),
            out((count, 2 * pixels, LANES)),
            out((width, pixels)),
            out((count, pixels, 2 * pixels), F32),
            out((count, pixels, 2 * pixels), F32),
            out((count, 8, 2 * pixels), F32),
        ],
        compiler_params=params(),
    )(valid, query, key_value, grad)
    grads = pl.pallas_call(
        functools.partial(fine_kernel, cols, len(carried)),
        in_specs=[vmem()] * (12 + len(carried)),
        out_specs=[hbm()] * (2 + len(carried)),
        out_shape=[out((pixels, width)), out((pixels, 2 * width))]
        + [out(x.shape) for x in carried],
        scratch_shapes=[
            pltpu.VMEM((pixels, width), BF16),
            pltpu.VMEM((pixels, 2 * width), BF16),
            pltpu.SemaphoreType.DMA((2 + len(carried),)),
        ],
        compiler_params=params(),
        cost_estimate=pl.CostEstimate(flops=400_000_000, bytes_accessed=1_000_000, transcendentals=300_000),
    )(key_value, near, far, *plan, *carried)
    return (grads[0].reshape(fine_q.shape), grads[1].reshape(fine_kv.shape), *grads[2:])


def coarse_direct(coarse_q, coarse_kv, cotangent, gain_table, timesteps, valid_cols):
    frames, bands = lax.axis_size("frames"), lax.axis_size("rows")
    _, rows, cols, width = cotangent.shape
    tokens, cwidth = coarse_q.shape[-2:]
    head_width = cwidth // frames
    tile = 4 * tokens * head_width // LANES
    sent, gain, valid = pl.pallas_call(
        functools.partial(send_kernel, cols, bands),
        in_specs=[smem()] + [hbm()] * 5,
        out_specs=[vmem()] * 3,
        out_shape=[
            out((frames * bands * tile, LANES)),
            out((1, width), F32),
            out((1, frames), jnp.int32),
        ],
        scratch_shapes=[
            pltpu.VMEM((rows * cols, width), BF16),
            pltpu.VMEM((8, width), F32),
            pltpu.VMEM((tokens, cwidth), BF16),
            pltpu.VMEM((tokens, 2 * cwidth), BF16),
            pltpu.SemaphoreType.DMA((8,)),
        ],
        compiler_params=params(),
    )(
        timesteps,
        in_hbm(valid_cols.reshape(1, -1)),
        in_hbm(cotangent.reshape(rows * cols, width)),
        in_hbm(gain_table),
        in_hbm(coarse_q.reshape(tokens, cwidth)),
        in_hbm(coarse_kv.reshape(tokens, 2 * cwidth)),
    )
    held = lax.all_to_all(
        sent.reshape(frames * bands, tile, LANES),
        ("frames", "rows"),
        split_axis=0,
        concat_axis=0,
        tiled=True,
    ).reshape(frames * bands * tile, LANES)
    count = frames * bands * tokens
    outs = pl.pallas_call(
        functools.partial(coarse_kernel, frames, tokens),
        in_specs=[vmem()] * 2,
        out_specs=[vmem()] * 3,
        out_shape=[out((frames, tokens, head_width))] * 3,
        scratch_shapes=[
            pltpu.VMEM(held.shape, F32),
            pltpu.VMEM((head_width // LANES, count, 2 * count), F32),
            pltpu.VMEM((head_width // LANES, count, 2 * count), F32),
        ],
        compiler_params=params(),
        cost_estimate=pl.CostEstimate(flops=100_000_000_000, bytes_accessed=100_000_000, transcendentals=0),
    )(valid, held)
    return outs, gain, valid


def normalize(scores):
    row_max = jnp.max(scores, axis=-1, keepdims=True)
    return row_max + jnp.log(jnp.sum(jnp.exp(scores - row_max), axis=-1, keepdims=True))


def coarse_gathered(coarse_q, coarse_kv, cotangent, gain_table, timesteps, valid_cols):
    score_scale = 1.0 / math.sqrt(HD)
    frames_here, _, cols_here, fine_width = cotangent.shape
    total_frames = valid_cols.shape[0]
    steps_all = gain_table.shape[0]
    select = (timesteps[:, None] == jnp.arange(steps_all)[None, :]).astype(F32)
    frame_gain = jnp.dot(select, gain_table, precision=lax.Precision.HIGHEST)
    scaled_grad = frame_gain[:, None, None, :] * cotangent.astype(F32)
    half_pool = POOL // 2
    coarse_cols = cols_here // POOL
    coarse_width = coarse_q.shape[-1]
    coarse_count = frames_here * coarse_cols
    blocks = scaled_grad.reshape(frames_here, 2, half_pool, coarse_cols, 2, half_pool, fine_width)
    pooled = (
        jnp.sum(blocks, axis=(2, 5))
        .transpose(0, 2, 1, 3, 4)
        .reshape(coarse_count, coarse_width)
        .astype(BF16)
    )
    mine_query = coarse_q.reshape(coarse_count, coarse_width)
    mine_keys = coarse_kv[..., :coarse_width].reshape(coarse_count, coarse_width)
    mine_values = coarse_kv[..., coarse_width:].reshape(coarse_count, coarse_width)
    head_query, head_keys, head_values, head_grad = (
        lax.all_to_all(mine_query, "frames", split_axis=1, concat_axis=0, tiled=True),
        lax.all_to_all(mine_keys, "frames", split_axis=1, concat_axis=0, tiled=True),
        lax.all_to_all(mine_values, "frames", split_axis=1, concat_axis=0, tiled=True),
        lax.all_to_all(pooled, "frames", split_axis=1, concat_axis=0, tiled=True),
    )
    head_tokens, head_width = head_query.shape
    head_groups = head_width // HD
    query_heads = head_query.reshape(head_tokens, head_groups, HD)
    grad_heads = head_grad.reshape(head_tokens, head_groups, HD)
    every_keys, every_values = (
        lax.all_gather(head_keys, "rows", axis=0, tiled=True),
        lax.all_gather(head_values, "rows", axis=0, tiled=True),
    )
    every_count = every_keys.shape[0]
    key_heads = every_keys.reshape(every_count, head_groups, HD)
    value_heads = every_values.reshape(every_count, head_groups, HD)
    position = jnp.arange(every_count) % head_tokens
    key_frame = position // coarse_cols
    key_column = position % coarse_cols
    col_limit = jnp.sum(
        jnp.where(key_frame[:, None] == jnp.arange(total_frames)[None, :], valid_cols[None, :], 0),
        axis=1,
    )
    key_ok = key_column * POOL < col_limit
    coarse_scores = (
        jnp.einsum("qhd,khd->hqk", query_heads, key_heads, preferred_element_type=F32)
        * score_scale
    )
    coarse_scores = jnp.where(key_ok[None, None, :], coarse_scores, NEGATIVE)
    log_total = normalize(coarse_scores)
    coarse_weights = jnp.exp(coarse_scores - log_total)
    coarse_low = coarse_weights.astype(BF16)
    coarse_out = jnp.einsum("hqk,khd->qhd", coarse_low, value_heads, preferred_element_type=F32)
    coarse_dot = jnp.sum(grad_heads.astype(F32) * coarse_out, axis=-1)
    coarse_wgrad = jnp.einsum("qhd,khd->hqk", grad_heads, value_heads, preferred_element_type=F32)
    coarse_sgrad = (coarse_weights * (coarse_wgrad - coarse_dot.T[:, :, None])).astype(BF16)
    coarse_qgrad = (
        jnp.einsum("hqk,khd->qhd", coarse_sgrad, key_heads, preferred_element_type=F32)
        * score_scale
    )
    count = head_tokens * lax.axis_size("rows")
    key_part = (
        jnp.einsum("hqk,qhd->khd", coarse_sgrad, query_heads, preferred_element_type=F32)
        * score_scale
    )
    value_part = jnp.einsum("hqk,qhd->khd", coarse_low, grad_heads, preferred_element_type=F32)
    terms = lax.psum_scatter(
        jnp.concatenate(
            [key_part.reshape(count, head_width), value_part.reshape(count, head_width)], axis=1
        ),
        "rows",
        scatter_dimension=0,
        tiled=True,
    )
    total_keys = terms[:, :head_width]
    total_values = terms[:, head_width:]
    out_dims = (head_tokens // coarse_cols, 1, coarse_cols, head_width)
    return (
        coarse_qgrad.reshape(out_dims).astype(BF16),
        total_keys.reshape(out_dims).astype(BF16),
        total_values.reshape(out_dims).astype(BF16),
    ), frame_gain


def local(fine_q, fine_kv, coarse_q, coarse_kv, cotangent, gain_table, timesteps, valid_cols):
    frames, bands = lax.axis_size("frames"), lax.axis_size("rows")
    head_width = coarse_q.shape[-1] // frames
    tokens = coarse_q.shape[-2]
    direct = (
        head_width == cotangent.shape[-1]
        and 4 * tokens * head_width // LANES == 16
        and frames * bands * tokens <= 128
    )
    operands = (coarse_q, coarse_kv, cotangent, gain_table, timesteps, valid_cols)
    fine = (fine_q, fine_kv, cotangent)
    if direct:
        carried, gain, valid = coarse_direct(*operands)
        grad_q, grad_kv, *coarse_grads = fine_level(carried, gain, valid, *fine)
        shape = (frames, 1, tokens, head_width)
        return (grad_q, grad_kv, *(x.reshape(shape) for x in coarse_grads))
    coarse_grads, gain = coarse_gathered(*operands)
    return (*fine_level([], gain, valid_cols.reshape(1, -1), *fine), *coarse_grads)


def solution(mesh):
    placed = (
        P("frames", "rows", None, None),
        P("frames", "rows", None, None),
        P("frames", "rows", None, None),
        P("frames", "rows", None, None),
        P("frames", "rows", None, None),
        P(),
        P("frames"),
        P(),
    )
    return jax.shard_map(
        local,
        mesh=mesh,
        in_specs=placed,
        out_specs=(
            P("frames", "rows", None, None),
            P("frames", "rows", None, None),
            P(None, "rows", None, "frames"),
            P(None, "rows", None, "frames"),
            P(None, "rows", None, "frames"),
        ),
        check_vma=False,
    )
```

```python
import functools
import math

import jax
import jax.numpy as jnp
from jax import lax
from jax.experimental import pallas as pl
from jax.experimental.pallas import tpu as pltpu
from jax.sharding import PartitionSpec as P

HD = 64
KERNEL = 7
POOL = 8
LANES = 128

NEGATIVE = -1e30

F32 = jnp.float32
BF16 = jnp.bfloat16


def dot_nt(left, right):
    return lax.dot_general(left, right, (((1,), (1,)), ((), ())), preferred_element_type=F32)


def dot_nn(left, right):
    return jnp.dot(left, right, preferred_element_type=F32)


def iota(shape, dim):
    return lax.broadcasted_iota(jnp.int32, shape, dim)


def pairs_of(table):
    blocks = []
    for lo in range(0, table.shape[1], LANES):
        part = table[:, lo : lo + LANES]
        first = iota(part.shape, 1) < HD
        zero = jnp.zeros_like(part)
        blocks.append(
            jnp.concatenate([jnp.where(first, part, zero), jnp.where(first, zero, part)], axis=0)
        )
    return blocks


def softmax_grads(scores, weight_grad, axis):
    top = jnp.max(scores, axis=axis, keepdims=True)
    raised = jnp.exp(scores - top)
    share = 1.0 / jnp.sum(raised, axis=axis, keepdims=True)
    row_dot = jnp.sum(raised * weight_grad, axis=axis, keepdims=True) * share
    weights = raised * share
    return weights.astype(BF16), (weights * (weight_grad - row_dot)).astype(BF16)


def send_kernel(
    cols, bands, step_ref, valid_hbm, cot_hbm, gain_hbm, cq_hbm, ckv_hbm,
    send_ref, gain_ref, valid_ref, cot_ref, eight_ref, cq_ref, ckv_ref, sems,
):
    step = step_ref[0]
    eight = eight_ref.shape[0]
    first = pl.multiple_of(step // eight * eight, eight)
    gain_copy = pltpu.make_async_copy(gain_hbm.at[pl.ds(first, eight)], eight_ref, sems.at[0])
    copies = [
        pltpu.make_async_copy(source, target, sems.at[1 + at])
        for at, (source, target) in enumerate(
            tuple((cot_hbm.at[pl.ds(r, 64)], cot_ref.at[pl.ds(r, 64)]) for r in range(0, 128, 64)) + ((cq_hbm, cq_ref), (ckv_hbm, ckv_ref), (valid_hbm, valid_ref))
        )
    ]
    for copy in copies[:-1]:
        copy.start()
    gain_copy.start()
    copies[-1].start()
    pixels, width = cot_ref.shape
    tokens, cwidth = cq_ref.shape
    half = POOL // 2
    groups = cwidth // width
    part = iota((groups * tokens, pixels), 0)
    group, token = part // tokens, part % tokens
    pixel = iota((groups * tokens, pixels), 1)
    row, col = pixel // cols, pixel % cols
    inside = (row // half == group // 2) & (col // half == token * 2 + group % 2)
    for copy in copies[-3:]:
        copy.wait()
    query = cq_ref[...].astype(F32)
    both = ckv_ref[...].astype(F32)
    for copy in copies[:-3]:
        copy.wait()
    summed = dot_nn(inside.astype(BF16), cot_ref[...])
    gain_copy.wait()
    gain = eight_ref[pl.ds(step - first, 1), :]
    gain_ref[...] = gain
    pooled = summed * gain
    for g in range(groups):
        lo = g * width
        arrays = (
            query[:, lo : lo + width],
            both[:, lo : lo + width],
            both[:, cwidth + lo : cwidth + lo + width],
            pooled[g * tokens : (g + 1) * tokens, :],
        )
        tile = jnp.concatenate(
            [a[:, b : b + LANES] for a in arrays for b in range(0, width, LANES)], axis=0
        ).astype(BF16)
        height = tile.shape[0]
        for r in range(bands):
            start = (g * bands + r) * height
            send_ref[start : start + height, :] = tile


def valid_here(valid_ref):
    frame = lax.axis_index("frames")
    return sum(
        jnp.where(frame == f, valid_ref[:, f : f + 1], 0) for f in range(valid_ref.shape[1])
    )


def window_bias(shape, cols, valid, key_row, lane_rows, query_row, present=None):
    radius = KERNEL // 2
    place, lane = iota(shape, 0), iota(shape, 1)
    krow, kcol = key_row(place // cols), place % cols
    qrow, qcol = lane // cols % lane_rows + query_row, lane % cols
    seen = (jnp.abs(krow - qrow) <= radius) & (jnp.abs(kcol - qcol) <= radius) & (kcol < valid)
    if present is not None:
        seen = seen & present(krow)
    seen = seen | ((krow == qrow) & (kcol == qcol))
    return jnp.where(seen, 0.0, NEGATIVE)


def partial_sums(scores, weight_grad):
    top = jnp.max(scores, axis=0, keepdims=True)
    raised = jnp.exp(scores - top)
    total = jnp.sum(raised, axis=0, keepdims=True)
    return top, raised, total, jnp.sum(raised * weight_grad, axis=0, keepdims=True)


def completed(kept, scores, weight_grad):
    top_kept, total_kept, dot_kept = kept
    top = jnp.maximum(top_kept, jnp.max(scores, axis=0, keepdims=True))
    factor = jnp.exp(top_kept - top)
    raised = jnp.exp(scores - top)
    total = total_kept * factor + jnp.sum(raised, axis=0, keepdims=True)
    share = jnp.where(total > 0, 1.0 / total, 0.0)
    dot = dot_kept * factor + jnp.sum(raised * weight_grad, axis=0, keepdims=True)
    return factor * share, raised * share, dot * share


def in_parts(row):
    parts = []
    for _ in range(3):
        part = row.astype(BF16).astype(F32)
        parts.append(part)
        row = row - part
    return parts


def prep_kernel(cols, valid_ref, gain_ref, q_ref, kv_ref, cot_ref, near_ref, far_ref, grad_ref):
    radius = KERNEL // 2
    pixels, width = q_ref.shape
    rows = pixels // cols
    one, two = radius * cols, 2 * radius * cols
    scale = 1.0 / math.sqrt(HD)
    even = lax.axis_index("rows") % 2 == 0
    valid = valid_here(valid_ref)
    grad_ref[...] = (gain_ref[...] * cot_ref[...].astype(F32)).astype(BF16)
    pad = jnp.zeros((cols, width), BF16)

    sides = []
    for lo, key_lo, query_row in ((0, 0, 0), (pixels - one, pixels - two, radius)):
        bias = window_bias((two, LANES), cols, valid, lambda at: at, radius + 1, query_row)
        query = pairs_of(jnp.concatenate([q_ref[lo : lo + one, :] * scale, pad], axis=0))
        grad = pairs_of(jnp.concatenate([grad_ref[lo : lo + one, :], pad], axis=0))
        products = []
        for p in range(width // LANES):
            at = p * LANES
            keys = kv_ref[key_lo : key_lo + two, at : at + LANES]
            values = kv_ref[key_lo : key_lo + two, width + at : width + at + LANES]
            products.append((dot_nt(keys, query[p]) + bias, dot_nt(values, grad[p])))
        sides.append(products)

    def sums(products):
        tiles = []
        for scores, wgrad in products:
            top, _, total, dot = partial_sums(scores, wgrad)
            found = [part for row in (top, total, dot) for part in in_parts(row)]
            found.append(jnp.zeros((16 - len(found), LANES), F32))
            tiles.append(jnp.concatenate(found, axis=0))
        return jnp.concatenate(tiles, axis=1).astype(BF16)

    upper, lower = (sums(products) for products in sides)

    def pack(target, lo, found):
        parts = (kv_ref[lo : lo + one, :width], kv_ref[lo : lo + one, width:])
        parts += (q_ref[lo : lo + one, :], grad_ref[lo : lo + one, :])
        for at, part in enumerate(parts):
            target[at * one : (at + 1) * one, :] = part
        target[len(parts) * one :, :] = found

    @pl.when(even)
    def _():
        pack(near_ref, pixels - one, lower)
        pack(far_ref, 0, upper)

    @pl.when(jnp.logical_not(even))
    def _():
        pack(near_ref, 0, upper)
        pack(far_ref, pixels - one, lower)


def plan_kernel(
    cols, valid_ref, q_ref, kv_ref, grad_ref,
    beside_ref, above_ref, below_ref, queries_ref, grads_ref, keys_t_ref, raised_ref, wgrad_ref, sums_ref,
):
    radius = KERNEL // 2
    pixels, width = q_ref.shape
    rows = pixels // cols
    scale = 1.0 / math.sqrt(HD)
    band = lax.axis_index("rows")
    first, last = band == 0, band == lax.axis_size("rows") - 1
    valid = valid_here(valid_ref)

    def present(krow):
        return ((krow >= 0) | jnp.logical_not(first)) & ((krow < rows) | jnp.logical_not(last))

    beside_ref[...] = window_bias(
        beside_ref.shape, cols, valid,
        lambda at: jnp.where(at < radius, at - radius, at - radius + rows), rows, 0, present,
    )
    above_ref[...] = window_bias(
        above_ref.shape, cols, valid, lambda at: at, radius + 1, -radius
    )
    below_ref[...] = window_bias(
        below_ref.shape, cols, valid, lambda at: at + rows - radius, radius + 1, rows
    )
    bias = window_bias((pixels, pixels), cols, valid, lambda at: at, rows, 0)
    bias = jnp.concatenate([bias, bias], axis=1)
    keys_t_ref[...] = kv_ref[:, :width].T
    for p, (query, grad) in enumerate(zip(pairs_of(q_ref[...] * scale), pairs_of(grad_ref[...]))):
        at = p * LANES
        queries_ref[p], grads_ref[p] = query, grad
        wgrad = dot_nt(kv_ref[:, width + at : width + at + LANES], grad)
        top, raised, total, dot = partial_sums(
            dot_nt(kv_ref[:, at : at + LANES], query) + bias, wgrad
        )
        raised_ref[p], wgrad_ref[p] = raised, wgrad
        for row, value in enumerate((top, total, dot)):
            sums_ref[p, row : row + 1, :] = value


def fine_kernel(cols, carried, *refs):
    (kv_ref, near_ref, far_ref, beside_ref, above_ref, below_ref, queries_ref, grads_ref) = refs[:8]
    (keys_t_ref, raised_ref, wgrad_ref, sums_ref) = refs[8:12]
    outs = refs[12 + carried : 14 + 2 * carried]
    dq_ref, dkv_ref, sems = refs[14 + 2 * carried :]
    copies = [
        pltpu.make_async_copy(source, target, sems.at[2 + at])
        for at, (source, target) in enumerate(zip(refs[12 : 12 + carried], outs[2:]))
    ]
    for copy in copies:
        copy.start()
    radius = KERNEL // 2
    pixels, width = dq_ref.shape
    one = radius * cols
    scale = 1.0 / math.sqrt(HD)
    even = lax.axis_index("rows") % 2 == 0

    def received(at):
        rows_at = slice(at * one, (at + 1) * one) if at < 4 else slice(at * one, None)
        near, far = near_ref[rows_at, :], far_ref[rows_at, :]
        return jnp.where(even, far, near), jnp.where(even, near, far)

    def joined(table):
        return jnp.concatenate(table, axis=0)

    beside_keys, beside_values = joined(received(0)), joined(received(1))
    beside_t = beside_keys.T
    pad = jnp.zeros((cols, width), BF16)
    rest = jnp.zeros((pixels - one, LANES), BF16)
    side_lo = (0, pixels - one)
    side_query = [pairs_of(joined([t * scale, pad])) for t in received(2)]
    side_grad = [pairs_of(joined([t, pad])) for t in received(3)]
    side_sums = [t.astype(F32) for t in received(4)]
    beside_bias = jnp.concatenate([beside_ref[...], beside_ref[...]], axis=1)
    pairs = range(width // LANES)
    ats = [slice(p * LANES, (p + 1) * LANES) for p in pairs]
    value_ats = [slice(width + p * LANES, width + (p + 1) * LANES) for p in pairs]
    sides = [(side, p) for side in range(2) for p in pairs]
    beside_scores = [dot_nt(beside_keys[:, ats[p]], queries_ref[p]) + beside_bias for p in pairs]
    beside_wgrad = [dot_nt(beside_values[:, ats[p]], grads_ref[p]) for p in pairs]
    side_scores, side_wgrad = {}, {}
    for side, p in sides:
        keys_at = slice(side_lo[side], side_lo[side] + one)
        bias_ref = (above_ref, below_ref)[side]
        side_scores[side, p] = (
            dot_nt(kv_ref[keys_at, ats[p]], side_query[side][p]) + bias_ref[...]
        )
        side_wgrad[side, p] = dot_nt(kv_ref[keys_at, value_ats[p]], side_grad[side][p])
    lows, sgrads, beside_sgrads = {}, {}, {}
    for p in pairs:
        factor, beside_weights, row_dot = completed(
            tuple(sums_ref[p, row : row + 1, :] for row in range(3)),
            beside_scores[p],
            beside_wgrad[p],
        )
        beside_sgrads[p] = (beside_weights * (beside_wgrad[p] - row_dot)).astype(BF16)
        weights = raised_ref[p] * factor
        lows[p] = weights.astype(BF16)
        sgrads[p] = (weights * (wgrad_ref[p] - row_dot)).astype(BF16)
    for side, p in sides:
        found = side_sums[side][:, ats[p]]
        kept = tuple(
            found[row : row + 1] + found[row + 1 : row + 2] + found[row + 2 : row + 3]
            for row in (0, 3, 6)
        )
        _, weights, row_dot = completed(kept, side_scores[side, p], side_wgrad[side, p])
        order = slice(None, None, -1 if side else 1)
        lows[side, p] = joined([weights.astype(BF16), rest][order])
        sgrad = (weights * (side_wgrad[side, p] - row_dot)).astype(BF16)
        sgrads[side, p] = joined([sgrad, rest][order])
    for p in pairs:
        dq_t = dot_nn(keys_t_ref[ats[p], :], sgrads[p]) + dot_nn(beside_t[ats[p]], beside_sgrads[p])
        dq_t = joined([dq_t[:HD, :pixels], dq_t[HD:, pixels:]])
        dq_ref[:, ats[p]] = (dq_t * scale).astype(BF16).T
    for p in pairs:
        dkv_ref[:, ats[p]] = dot_nn(
            jnp.concatenate([sgrads[p], sgrads[0, p], sgrads[1, p]], axis=1),
            joined([queries_ref[p], side_query[0][p], side_query[1][p]]),
        ).astype(BF16)
        dkv_ref[:, value_ats[p]] = dot_nn(
            jnp.concatenate([lows[p], lows[0, p], lows[1, p]], axis=1),
            joined([grads_ref[p], side_grad[0][p], side_grad[1][p]]),
        ).astype(BF16)
    copies += [
        pltpu.make_async_copy(source, target, sems.at[at])
        for at, (source, target) in enumerate(((dq_ref, outs[0]), (dkv_ref, outs[1])))
    ]
    for copy in copies[carried:]:
        copy.start()
    for copy in copies:
        copy.wait()


def coarse_kernel(frames, tokens, valid_ref, x_ref, dq_ref, dk_ref, dv_ref, wide, low_ref, sg_ref):
    bands = lax.axis_size("rows")
    width = dq_ref.shape[-1]
    parts = width // LANES
    height = x_ref.shape[0] // (frames * bands)
    band = lax.axis_index("rows")
    scale = 1.0 / math.sqrt(HD)
    wide[...] = x_ref[...].astype(F32)
    devices, own = frames * bands, frames * tokens

    def every(array, b):
        first = (array * parts + b) * tokens
        return jnp.concatenate(
            [wide[pl.ds(first + t, devices, stride=height), :] for t in range(tokens)], axis=0
        ).astype(BF16)

    def mine(array, b):
        first = band * height + (array * parts + b) * tokens
        return jnp.concatenate(
            [wide[pl.ds(first + f * bands * height, tokens), :] for f in range(frames)], axis=0
        ).astype(BF16)

    count = devices * tokens

    def key_bias(shape, dim):
        place = iota(shape, dim)
        token, frame = place // devices, place // bands % frames
        limit = jnp.zeros(shape, jnp.int32)
        for f in range(frames):
            limit = jnp.where(frame == f, valid_ref[:, f : f + 1], limit)
        return jnp.where(token * POOL < limit, 0.0, NEGATIVE)

    bias, own_bias = key_bias((count, 2 * count), 0), key_bias((2 * own, count), 1)
    halves = range(parts)
    keys, values = ([every(a, b) for b in halves] for a in (1, 2))
    queries, grads = ([pairs_of(every(a, b))[0] for b in halves] for a in (0, 3))
    queries = [query * scale for query in queries]
    own_queries = [pairs_of(mine(0, b) * scale)[0] for b in halves]
    own_grads = [pairs_of(mine(3, b))[0] for b in halves]
    scores = [dot_nt(keys[b], queries[b]) + bias for b in halves]
    wgrads = [dot_nt(values[b], grads[b]) for b in halves]
    own_scores = [dot_nt(own_queries[b], keys[b]) + own_bias for b in halves]
    own_wgrads = [dot_nt(own_grads[b], values[b]) for b in halves]
    found = [softmax_grads(scores[b], wgrads[b], 0) for b in halves]
    own_sgrads = [softmax_grads(own_scores[b], own_wgrads[b], 1)[1] for b in halves]
    for b in halves:
        low_ref[b], sg_ref[b] = found[b][0].astype(F32), found[b][1].astype(F32)

    def mine_rows(ref, b):
        pieces = [
            ref[b, pl.ds(t * devices + f * bands + band, 1), :]
            for f in range(frames)
            for t in range(tokens)
        ]
        return jnp.concatenate(pieces, axis=0).astype(BF16)

    for b in halves:
        full = dot_nn(own_sgrads[b], keys[b])
        dq = jnp.where(iota((own, LANES), 1) < HD, full[:own], full[own:]) * scale
        dk = dot_nn(mine_rows(sg_ref, b), queries[b])
        dv = dot_nn(mine_rows(low_ref, b), grads[b])
        for ref, table in ((dq_ref, dq), (dk_ref, dk), (dv_ref, dv)):
            rounded = table.astype(BF16)
            for f in range(frames):
                ref[f, :, b * LANES : (b + 1) * LANES] = rounded[f * tokens : (f + 1) * tokens]


def vmem():
    return pl.BlockSpec(memory_space=pltpu.VMEM)


def smem():
    return pl.BlockSpec(memory_space=pltpu.SMEM)


def hbm():
    return pl.BlockSpec(memory_space=pltpu.HBM)


def in_hbm(array):
    return pltpu.with_memory_space_constraint(array, pltpu.HBM)


def params():
    return pltpu.CompilerParams(vmem_limit_bytes=16 * 2**20)


def out(shape, dtype=BF16):
    return jax.ShapeDtypeStruct(shape, dtype)


def fine_level(carried, gain, valid, fine_q, fine_kv, cotangent):
    bands = lax.axis_size("rows")
    _, rows, cols, width = fine_q.shape
    pixels = rows * cols
    radius = KERNEL // 2
    query = fine_q.reshape(pixels, width)
    key_value = fine_kv.reshape(pixels, 2 * width)
    cot = cotangent.reshape(pixels, width)
    one, sums = radius * cols, 16
    packed = (4 * one + sums, width)
    near, far, grad = pl.pallas_call(
        functools.partial(prep_kernel, cols),
        in_specs=[vmem()] * 5,
        out_specs=[vmem()] * 3,
        out_shape=[out(packed), out(packed), out((pixels, width))],
        compiler_params=params(),
    )(valid, gain, query, key_value, cot)
    pairs = [(i, i ^ 1) for i in range(bands) if i ^ 1 < bands]
    others = [(i, ((i + 1) ^ 1) - 1) for i in range(1, bands) if ((i + 1) ^ 1) - 1 < bands]
    near = lax.ppermute(near, "rows", pairs)
    far = lax.ppermute(far, "rows", others)
    count = width // LANES
    plan = pl.pallas_call(
        functools.partial(plan_kernel, cols),
        in_specs=[vmem()] * 4,
        out_specs=[vmem()] * 9,
        out_shape=[
            out((2 * one, pixels), F32),
            out((one, LANES), F32),
            out((one, LANES), F32),
            out((count, 2 * pixels, LANES)),
            out((count, 2 * pixels, LANES)),
            out((width, pixels)),
            out((count, pixels, 2 * pixels), F32),
            out((count, pixels, 2 * pixels), F32),
            out((count, 8, 2 * pixels), F32),
        ],
        compiler_params=params(),
    )(valid, query, key_value, grad)
    grads = pl.pallas_call(
        functools.partial(fine_kernel, cols, len(carried)),
        in_specs=[vmem()] * (12 + len(carried)),
        out_specs=[hbm()] * (2 + len(carried)),
        out_shape=[out((pixels, width)), out((pixels, 2 * width))]
        + [out(x.shape) for x in carried],
        scratch_shapes=[
            pltpu.VMEM((pixels, width), BF16),
            pltpu.VMEM((pixels, 2 * width), BF16),
            pltpu.SemaphoreType.DMA((2 + len(carried),)),
        ],
        compiler_params=params(),
        cost_estimate=pl.CostEstimate(flops=400_000_000, bytes_accessed=1_000_000, transcendentals=300_000),
    )(key_value, near, far, *plan, *carried)
    return (grads[0].reshape(fine_q.shape), grads[1].reshape(fine_kv.shape), *grads[2:])


def coarse_direct(coarse_q, coarse_kv, cotangent, gain_table, timesteps, valid_cols):
    frames, bands = lax.axis_size("frames"), lax.axis_size("rows")
    _, rows, cols, width = cotangent.shape
    tokens, cwidth = coarse_q.shape[-2:]
    head_width = cwidth // frames
    tile = 4 * tokens * head_width // LANES
    sent, gain, valid = pl.pallas_call(
        functools.partial(send_kernel, cols, bands),
        in_specs=[smem()] + [hbm()] * 5,
        out_specs=[vmem()] * 3,
        out_shape=[
            out((frames * bands * tile, LANES)),
            out((1, width), F32),
            out((1, frames), jnp.int32),
        ],
        scratch_shapes=[
            pltpu.VMEM((rows * cols, width), BF16),
            pltpu.VMEM((8, width), F32),
            pltpu.VMEM((tokens, cwidth), BF16),
            pltpu.VMEM((tokens, 2 * cwidth), BF16),
            pltpu.SemaphoreType.DMA((8,)),
        ],
        compiler_params=params(),
    )(
        timesteps,
        in_hbm(valid_cols.reshape(1, -1)),
        in_hbm(cotangent.reshape(rows * cols, width)),
        in_hbm(gain_table),
        in_hbm(coarse_q.reshape(tokens, cwidth)),
        in_hbm(coarse_kv.reshape(tokens, 2 * cwidth)),
    )
    held = lax.all_to_all(
        sent.reshape(frames * bands, tile, LANES),
        ("frames", "rows"),
        split_axis=0,
        concat_axis=0,
        tiled=True,
    ).reshape(frames * bands * tile, LANES)
    count = frames * bands * tokens
    outs = pl.pallas_call(
        functools.partial(coarse_kernel, frames, tokens),
        in_specs=[vmem()] * 2,
        out_specs=[vmem()] * 3,
        out_shape=[out((frames, tokens, head_width))] * 3,
        scratch_shapes=[
            pltpu.VMEM(held.shape, F32),
            pltpu.VMEM((head_width // LANES, count, 2 * count), F32),
            pltpu.VMEM((head_width // LANES, count, 2 * count), F32),
        ],
        compiler_params=params(),
        cost_estimate=pl.CostEstimate(flops=100_000_000_000, bytes_accessed=100_000_000, transcendentals=0),
    )(valid, held)
    return outs, gain, valid


def normalize(scores):
    row_max = jnp.max(scores, axis=-1, keepdims=True)
    return row_max + jnp.log(jnp.sum(jnp.exp(scores - row_max), axis=-1, keepdims=True))


def coarse_gathered(coarse_q, coarse_kv, cotangent, gain_table, timesteps, valid_cols):
    score_scale = 1.0 / math.sqrt(HD)
    frames_here, _, cols_here, fine_width = cotangent.shape
    total_frames = valid_cols.shape[0]
    steps_all = gain_table.shape[0]
    select = (timesteps[:, None] == jnp.arange(steps_all)[None, :]).astype(F32)
    frame_gain = jnp.dot(select, gain_table, precision=lax.Precision.HIGHEST)
    scaled_grad = frame_gain[:, None, None, :] * cotangent.astype(F32)
    half_pool = POOL // 2
    coarse_cols = cols_here // POOL
    coarse_width = coarse_q.shape[-1]
    coarse_count = frames_here * coarse_cols
    blocks = scaled_grad.reshape(frames_here, 2, half_pool, coarse_cols, 2, half_pool, fine_width)
    pooled = (
        jnp.sum(blocks, axis=(2, 5))
        .transpose(0, 2, 1, 3, 4)
        .reshape(coarse_count, coarse_width)
        .astype(BF16)
    )
    mine_query = coarse_q.reshape(coarse_count, coarse_width)
    mine_keys = coarse_kv[..., :coarse_width].reshape(coarse_count, coarse_width)
    mine_values = coarse_kv[..., coarse_width:].reshape(coarse_count, coarse_width)
    head_query, head_keys, head_values, head_grad = (
        lax.all_to_all(mine_query, "frames", split_axis=1, concat_axis=0, tiled=True),
        lax.all_to_all(mine_keys, "frames", split_axis=1, concat_axis=0, tiled=True),
        lax.all_to_all(mine_values, "frames", split_axis=1, concat_axis=0, tiled=True),
        lax.all_to_all(pooled, "frames", split_axis=1, concat_axis=0, tiled=True),
    )
    head_tokens, head_width = head_query.shape
    head_groups = head_width // HD
    query_heads = head_query.reshape(head_tokens, head_groups, HD)
    grad_heads = head_grad.reshape(head_tokens, head_groups, HD)
    every_keys, every_values = (
        lax.all_gather(head_keys, "rows", axis=0, tiled=True),
        lax.all_gather(head_values, "rows", axis=0, tiled=True),
    )
    every_count = every_keys.shape[0]
    key_heads = every_keys.reshape(every_count, head_groups, HD)
    value_heads = every_values.reshape(every_count, head_groups, HD)
    position = jnp.arange(every_count) % head_tokens
    key_frame = position // coarse_cols
    key_column = position % coarse_cols
    col_limit = jnp.sum(
        jnp.where(key_frame[:, None] == jnp.arange(total_frames)[None, :], valid_cols[None, :], 0),
        axis=1,
    )
    key_ok = key_column * POOL < col_limit
    coarse_scores = (
        jnp.einsum("qhd,khd->hqk", query_heads, key_heads, preferred_element_type=F32)
        * score_scale
    )
    coarse_scores = jnp.where(key_ok[None, None, :], coarse_scores, NEGATIVE)
    log_total = normalize(coarse_scores)
    coarse_weights = jnp.exp(coarse_scores - log_total)
    coarse_low = coarse_weights.astype(BF16)
    coarse_out = jnp.einsum("hqk,khd->qhd", coarse_low, value_heads, preferred_element_type=F32)
    coarse_dot = jnp.sum(grad_heads.astype(F32) * coarse_out, axis=-1)
    coarse_wgrad = jnp.einsum("qhd,khd->hqk", grad_heads, value_heads, preferred_element_type=F32)
    coarse_sgrad = (coarse_weights * (coarse_wgrad - coarse_dot.T[:, :, None])).astype(BF16)
    coarse_qgrad = (
        jnp.einsum("hqk,khd->qhd", coarse_sgrad, key_heads, preferred_element_type=F32)
        * score_scale
    )
    count = head_tokens * lax.axis_size("rows")
    key_part = (
        jnp.einsum("hqk,qhd->khd", coarse_sgrad, query_heads, preferred_element_type=F32)
        * score_scale
    )
    value_part = jnp.einsum("hqk,qhd->khd", coarse_low, grad_heads, preferred_element_type=F32)
    terms = lax.psum_scatter(
        jnp.concatenate(
            [key_part.reshape(count, head_width), value_part.reshape(count, head_width)], axis=1
        ),
        "rows",
        scatter_dimension=0,
        tiled=True,
    )
    total_keys = terms[:, :head_width]
    total_values = terms[:, head_width:]
    out_dims = (head_tokens // coarse_cols, 1, coarse_cols, head_width)
    return (
        coarse_qgrad.reshape(out_dims).astype(BF16),
        total_keys.reshape(out_dims).astype(BF16),
        total_values.reshape(out_dims).astype(BF16),
    ), frame_gain


def local(fine_q, fine_kv, coarse_q, coarse_kv, cotangent, gain_table, timesteps, valid_cols):
    frames, bands = lax.axis_size("frames"), lax.axis_size("rows")
    head_width = coarse_q.shape[-1] // frames
    tokens = coarse_q.shape[-2]
    direct = (
        head_width == cotangent.shape[-1]
        and 4 * tokens * head_width // LANES == 16
        and frames * bands * tokens <= 128
    )
    operands = (coarse_q, coarse_kv, cotangent, gain_table, timesteps, valid_cols)
    fine = (fine_q, fine_kv, cotangent)
    if direct:
        carried, gain, valid = coarse_direct(*operands)
        grad_q, grad_kv, *coarse_grads = fine_level(carried, gain, valid, *fine)
        shape = (frames, 1, tokens, head_width)
        return (grad_q, grad_kv, *(x.reshape(shape) for x in coarse_grads))
    coarse_grads, gain = coarse_gathered(*operands)
    return (*fine_level([], gain, valid_cols.reshape(1, -1), *fine), *coarse_grads)


def solution(mesh):
    placed = (
        P("frames", "rows", None, None),
        P("frames", "rows", None, None),
        P("frames", "rows", None, None),
        P("frames", "rows", None, None),
        P("frames", "rows", None, None),
        P(),
        P("frames"),
        P(),
    )
    return jax.shard_map(
        local,
        mesh=mesh,
        in_specs=placed,
        out_specs=(
            P("frames", "rows", None, None),
            P("frames", "rows", None, None),
            P(None, "rows", None, "frames"),
            P(None, "rows", None, "frames"),
            P(None, "rows", None, "frames"),
        ),
        check_vma=False,
    )
```
